32 devices in a mesh: ep: 2 (over x), row: 4 (over y, core), col: 4 (over z).
Axes of the slice: x: 2, y: 2, z: 4, core: 2. Of those that a mesh axis runs over, the one named last changes fastest.
Arguments:
- design: bfloat16 [512, 16384], P(('ep', 'col'), 'row'), may hold values from -0.125 to 0.125
- taps: float32 [64], replicated, may hold values from -1 to 1
- tap_count: int32 [512], P(('ep', 'col')), may hold values from 32 to 64
- order: int32 [16384], P('row'), may hold values from 0 to 16383, as said below
- regular: float32 [16384], replicated, may hold values from 0.5 to 2
Outputs:
- factored: float32 [16384, 16384], P('row', ('ep', 'col'))
The draws below stay inside these ranges and needn't reach their ends.
Inputs may be any that keep to these rules, and one draw needn't show every extreme that they name: `order`: a permutation of 0 to 16383 that maps every index into its own aligned group of 128.
All inputs are finite; a program needn't handle non-finite values.
Results may differ from the reference program's by a relative error of at most 0.0037.
Values may be sent and summed in bfloat16 or wider, within the bound.
No kernel may reach another device: no remote copies, remote signals or barrier semaphores. Data moves between devices by JAX's collectives and lax.ppermute only.
A program may use at most 128 MiB of HBM per device.

```python
import math
import jax
import jax.numpy as jnp
from jax import lax

P_SIZE = 16384
PANEL = 256
PB = 128
TAPS = 64
E = 512


def draw_order(key, part):
    group_keys = jax.random.split(key, P_SIZE // PB)
    group_perms = jax.vmap(lambda single: jax.random.permutation(single, PB))(group_keys)
    bases = jnp.arange(P_SIZE // PB, dtype=jnp.int32) * PB
    return (group_perms.astype(jnp.int32) + bases[:, None]).reshape(P_SIZE).astype(jnp.int32)


def plant(drawn, rng, low, largest):
    spot = [jax.random.randint(jax.random.fold_in(rng, axis), (), 0, length) for axis, length in enumerate(drawn.shape)]
    longest = drawn.shape.index(max(drawn.shape))
    neighbour = spot[:longest] + [(spot[longest] + 1) % drawn.shape[longest]] + spot[longest + 1:]
    return drawn.at[tuple(spot)].set(low).at[tuple(neighbour)].set(largest)


def level_of(stream_key, shape, cuts, low, largest):
    def one(position, parts):
        draws = jax.random.uniform(jax.random.fold_in(jax.random.fold_in(stream_key, 6), position), (parts,), jnp.float32, low / len(cuts), largest / len(cuts))
        return jnp.repeat(jnp.exp(draws), shape[position] // parts).reshape((-1,) + (1,) * (len(shape) - position - 1))

    factor_of = one(*cuts[0])
    for cut in cuts[1:]:
        factor_of = factor_of * one(*cut)
    return factor_of


def gaussian(key, dims, deviation, most, cuts=(), held_as=jnp.bfloat16):
    array = jax.random.normal(key, dims, jnp.float32) * deviation
    if len(cuts) > 0:
        array = level_of(key, dims, cuts, -0.22, 0.18) * array
    return jnp.clip(array, min=-most, max=most).astype(held_as)


def setup_inputs(seed: int = 0) -> dict:
    streams_of = jax.random.split(jax.random.key(seed), 6)
    design = gaussian(streams_of[0], (E, P_SIZE), (4 * E) ** -0.5, 0.125, ((0, 8), (1, 4)))
    taps = gaussian(streams_of[1], (TAPS,), 0.25, 1.0, (), jnp.float32)
    tap_count = plant(jax.random.randint(streams_of[2], (E,), TAPS // 2, TAPS + 1), jax.random.fold_in(streams_of[2], 1), TAPS // 2, TAPS).astype(jnp.int32)
    order = draw_order(jax.random.fold_in(streams_of[5], 71), 0)
    regular = jnp.clip(jnp.exp(jax.random.uniform(streams_of[4], (P_SIZE,), jnp.float32, math.log(0.5), math.log(2.0))), 0.5, 2.0)
    return dict(design=design, taps=taps, tap_count=tap_count, order=order, regular=regular)


def reference(design, taps, tap_count, order, regular):
    epoch_out = jnp.arange(E, dtype=jnp.int32)[:, None]
    epoch_in = jnp.arange(E, dtype=jnp.int32)[None, :]
    lag_steps = epoch_out - epoch_in
    valid = (lag_steps >= 0) & (lag_steps < tap_count.astype(jnp.int32)[:, None])
    toeplitz = jnp.where(valid, taps[jnp.clip(lag_steps, 0, TAPS - 1)], jnp.zeros((), taps.dtype)).astype(jnp.bfloat16)
    filtered = jnp.dot(toeplitz.astype(jnp.float32), design.astype(jnp.float32), preferred_element_type=jnp.float32).astype(jnp.bfloat16)
    permuted = jnp.take(filtered, order.astype(jnp.int32), axis=1)
    normal = jnp.dot(permuted.T.astype(jnp.float32), permuted.astype(jnp.float32), preferred_element_type=jnp.float32)
    all_rows = jnp.arange(P_SIZE, dtype=jnp.int32)
    normal = normal + jnp.diag(regular.astype(normal.dtype))
    for section in range(2):
        start_col = section * PANEL
        end_col = start_col + PANEL
        factor = jnp.linalg.cholesky(normal[start_col:end_col, start_col:end_col])
        solved = jax.scipy.linalg.solve_triangular(factor, normal[:, start_col:end_col].T, lower=True).T
        panel_factor = jnp.where((all_rows >= start_col)[:, None], solved, jnp.zeros((), solved.dtype))
        update = normal[:, end_col:] - jnp.dot(panel_factor, panel_factor[end_col:].T, precision=lax.Precision.HIGHEST)
        update = jnp.where((all_rows >= end_col)[:, None], update, jnp.zeros((), update.dtype))
        normal = jnp.concatenate([normal[:, :start_col], panel_factor, update], axis=1)
    return normal
```

```python
import functools

import jax
import jax.numpy as jnp
from jax import lax
from jax.experimental import pallas as pl
from jax.experimental.pallas import tpu as pltpu
from jax.sharding import PartitionSpec as P

PANEL = 256
SECTIONS = 2
HEAD = PANEL * SECTIONS
PB = 128
BLOCK = 128
SUB = 8
EXACT = lax.Precision.HIGHEST
F32 = jnp.float32
BF16 = jnp.bfloat16


def iota(shape, axis):
    return lax.broadcasted_iota(jnp.int32, shape, axis)


def dot(left, right, contract=((1,), (0,)), precision=None):
    return lax.dot_general(
        left, right, (contract, ((), ())), preferred_element_type=F32, precision=precision
    )


def apply_band(band, columns, store):
    for b in range(columns.shape[0] // BLOCK):
        here = slice(b * BLOCK, (b + 1) * BLOCK)
        if b == 0:
            got = dot(band[here, BLOCK:], columns[here, :])
        else:
            got = dot(band[here, :], columns[(b - 1) * BLOCK : (b + 1) * BLOCK, :])
        store(here, got.astype(BF16))


def permute_kernel(order_ref, counts_ref, design_ref, out_ref, head_ref):
    epochs, rows = design_ref.shape
    for g in range(rows // PB):
        cols = slice(g * PB, (g + 1) * PB)
        local = order_ref[:, cols] - (order_ref[:, cols] // PB) * PB
        one_hot = jnp.where(iota((PB, PB), 0) == local, 1.0, 0.0).astype(BF16)
        out_ref[:, cols] = dot(design_ref[:, cols], one_hot).astype(BF16)
    head_ref[:, :HEAD] = out_ref[:, :HEAD]
    head_ref[:, HEAD:] = jnp.broadcast_to(counts_ref[...], (epochs, PB)).astype(F32).astype(BF16)


def permute_local(design, order, tap_count):
    epochs, rows = design.shape
    return pl.pallas_call(
        permute_kernel,
        out_shape=(
            jax.ShapeDtypeStruct((epochs, rows), BF16),
            jax.ShapeDtypeStruct((epochs, HEAD + PB), BF16),
        ),
        name="permute_local",
    )(order.reshape(1, rows), tap_count.reshape(epochs, 1), design)


def spread(tile, lane):
    return jnp.broadcast_to(tile[:, lane : lane + 1], (SUB, tile.shape[1]))


def row_of(tile, k):
    return jnp.broadcast_to(tile[k : k + 1, :], (SUB, tile.shape[1]))


def factor_block(work):
    halves = work.shape[1] // BLOCK
    groups = BLOCK // SUB
    for g in range(groups):
        rows = slice(g * SUB, (g + 1) * SUB)
        own = [work[rows, h * BLOCK : (h + 1) * BLOCK] for h in range(halves)]
        cols = [spread(own[0], g * SUB + j) for j in range(SUB)]
        a = {(i, j): row_of(cols[j], i) for j in range(SUB) for i in range(j, SUB)}
        u = [[row_of(own[h], k) for k in range(SUB)] for h in range(halves)]
        inv = []
        low = {}
        for k in range(SUB):
            r = lax.rsqrt(a[k, k])
            inv.append(r)
            for i in range(k + 1, SUB):
                low[i, k] = a[i, k] * r
            for j in range(k + 1, SUB):
                for i in range(j, SUB):
                    a[i, j] = a[i, j] - low[i, k] * low[j, k]
            for h in range(halves):
                u[h][k] = u[h][k] * r
                for j in range(k + 1, SUB):
                    u[h][j] = u[h][j] - low[j, k] * u[h][k]
        for h in range(halves):
            merged = u[h][0]
            for k in range(1, SUB):
                merged = jnp.where(iota((SUB, BLOCK), 0) == k, u[h][k], merged)
            work[rows, h * BLOCK : (h + 1) * BLOCK] = merged
        for t in range(g + 1, groups):
            below = slice(t * SUB, (t + 1) * SUB)
            tile = [work[below, h * BLOCK : (h + 1) * BLOCK] for h in range(halves)]
            left = [spread(tile[0], g * SUB + j) for j in range(SUB)]
            for k in range(SUB):
                left[k] = left[k] * inv[k]
                for j in range(k + 1, SUB):
                    left[j] = left[j] - low[j, k] * left[k]
                for h in range(halves):
                    tile[h] = tile[h] - left[k] * u[h][k]
            for h in range(halves):
                work[below, h * BLOCK : (h + 1) * BLOCK] = tile[h]


def panel_kernel(
    taps_ref, head_ref, reg_ref, band_ref, factor_ref, w_ref, high_ref, low_ref, aug, a1, work
):
    epochs = head_ref.shape[0]
    lag = iota((BLOCK, 2 * BLOCK), 0) + BLOCK - iota((BLOCK, 2 * BLOCK), 1)
    base = lax.fori_loop(
        0,
        taps_ref.shape[0],
        lambda k, kept: jnp.where(lag == k, taps_ref[k], kept),
        jnp.zeros((BLOCK, 2 * BLOCK), F32),
    )
    lag = lag.astype(F32)
    for b in range(epochs // BLOCK):
        here = slice(b * BLOCK, (b + 1) * BLOCK)
        counts = head_ref[here, HEAD:].astype(F32)
        for side in (slice(0, BLOCK), slice(BLOCK, 2 * BLOCK)):
            kept = jnp.where(lag[:, side] < counts, base[:, side], 0.0)
            band_ref[here, side] = kept.astype(BF16)

    def store(here, got):
        a1[here, :] = got

    apply_band(band_ref, head_ref.at[:, :HEAD], store)
    columns = a1[...]
    square = (HEAD, HEAD)
    on_diagonal = iota(square, 0) == iota(square, 1)
    aug[:, :HEAD] = dot(columns, columns, ((0,), (0,))) + jnp.where(on_diagonal, reg_ref[...], 0.0)
    aug[:, HEAD:] = columns.astype(F32).T

    eye = jnp.where(iota((BLOCK, BLOCK), 0) == iota((BLOCK, BLOCK), 1), 1.0, 0.0)

    def eliminate(kb, carry):
        start = pl.multiple_of(kb * BLOCK, BLOCK)
        work[:, :BLOCK] = aug[pl.ds(start, BLOCK), pl.ds(start, BLOCK)]
        work[:, BLOCK:] = eye
        factor_block(work)
        u = dot(work[:, BLOCK:], aug[pl.ds(start, BLOCK), :], precision=EXACT)
        aug[pl.ds(start, BLOCK), :] = u

        def below(rb, inner):
            at = pl.multiple_of(rb * BLOCK, BLOCK)
            side = aug[pl.ds(start, BLOCK), pl.ds(at, BLOCK)]
            aug[pl.ds(at, BLOCK), :] -= dot(
                side, aug[pl.ds(start, BLOCK), :], ((0,), (0,)), precision=EXACT
            )
            return inner

        lax.fori_loop(kb + 1, HEAD // BLOCK, below, 0)
        return carry

    lax.fori_loop(0, HEAD // BLOCK, eliminate, 0)
    factor_ref[...] = jnp.where(iota(square, 0) >= iota(square, 1), aug[:, :HEAD].T, 0.0)
    wt = aug[:, HEAD:]
    w_ref[...] = wt.T.astype(BF16)
    for b in range(epochs // BLOCK):
        here = slice(b * BLOCK, (b + 1) * BLOCK)
        shape = (BLOCK, epochs)
        unit = jnp.where(iota(shape, 0) + b * BLOCK == iota(shape, 1), 1.0, 0.0)
        middle = unit - dot(wt[:, here], wt, ((0,), (0,)), precision=EXACT)
        high = middle.astype(BF16)
        high_ref[here, :] = high
        low_ref[here, :] = (middle - high.astype(F32)).astype(BF16)


def factor_panel(head, taps, regular):
    epochs = head.shape[0]
    vmem = pl.BlockSpec(memory_space=pltpu.VMEM)
    return pl.pallas_call(
        panel_kernel,
        out_shape=(
            jax.ShapeDtypeStruct((epochs, 2 * BLOCK), BF16),
            jax.ShapeDtypeStruct((HEAD, HEAD), F32),
            jax.ShapeDtypeStruct((epochs, HEAD), BF16),
            jax.ShapeDtypeStruct((epochs, epochs), BF16),
            jax.ShapeDtypeStruct((epochs, epochs), BF16),
        ),
        in_specs=[pl.BlockSpec(memory_space=pltpu.SMEM), vmem, vmem],
        scratch_shapes=[
            pltpu.VMEM((HEAD, HEAD + epochs), F32),
            pltpu.VMEM((epochs, HEAD), BF16),
            pltpu.VMEM((BLOCK, 2 * BLOCK), F32),
        ],
        compiler_params=pltpu.CompilerParams(vmem_limit_bytes=48 << 20),
        name="factor_panel",
    )(taps, head, regular[:HEAD].reshape(1, HEAD))


def columns_kernel(place_ref, right_ref, band_ref, w_ref, high_ref, low_ref, out_ref, filtered):
    def store(here, got):
        filtered[here, :] = got

    apply_band(band_ref, right_ref, store)
    out_ref[...] = (dot(high_ref[...], filtered[...]) + dot(low_ref[...], filtered[...])).astype(BF16)

    @pl.when((place_ref[1] == 0) & (pl.program_id(0) == 0))
    def _():
        out_ref[...] = w_ref[...]


def project_columns(place, right, band, w, high, low):
    epochs, cols = right.shape
    whole = lambda i, place: (0, 0)
    return pl.pallas_call(
        columns_kernel,
        out_shape=jax.ShapeDtypeStruct((epochs, cols), BF16),
        grid_spec=pltpu.PrefetchScalarGridSpec(
            num_scalar_prefetch=1,
            grid=(cols // HEAD,),
            in_specs=[
                pl.BlockSpec((epochs, HEAD), lambda i, place: (0, i)),
                pl.BlockSpec(band.shape, whole),
                pl.BlockSpec(w.shape, whole),
                pl.BlockSpec(high.shape, whole),
                pl.BlockSpec(low.shape, whole),
            ],
            out_specs=pl.BlockSpec((epochs, HEAD), lambda i, place: (0, i)),
            scratch_shapes=[pltpu.VMEM((epochs, HEAD), BF16)],
        ),
        compiler_params=pltpu.CompilerParams(vmem_limit_bytes=48 << 20),
        name="project_columns",
    )(place, right, band, w, high, low)


def tile_kernel(place_ref, left_ref, band_ref, right_ref, reg_ref, factor_ref, out_ref, filtered):
    def store(here, got):
        filtered[here, :] = got

    rows, cols = out_ref.shape
    dev_rows = pl.num_programs(0) * rows
    first_row = place_ref[0] * dev_rows + pl.program_id(0) * rows
    first_col = place_ref[1] * cols

    @pl.when(first_row >= HEAD)
    def _():
        apply_band(band_ref, left_ref, store)
        out_ref[...] = dot(filtered[...], right_ref[...], ((0,), (0,)))

        @pl.when((first_row >= first_col) & (first_row < first_col + cols))
        def _():
            at = pl.multiple_of(first_row - first_col, rows)
            on_diagonal = iota((rows, rows), 0) == iota((rows, rows), 1)
            out_ref[:, pl.ds(at, rows)] += jnp.where(on_diagonal, reg_ref[...], 0.0)

    @pl.when(first_row < HEAD)
    def _():
        out_ref[...] = jnp.zeros_like(out_ref)

        @pl.when(first_col == 0)
        def _():
            at = pl.multiple_of(first_row, rows)
            out_ref[:, :HEAD] = factor_ref[pl.ds(at, rows), :]


def multiply_tile(place, left, band, right, regular, factor, rows=256):
    epochs, dev_rows = left.shape
    cols = right.shape[1]
    steps = dev_rows // rows
    whole = lambda i, place: (0, 0)
    return pl.pallas_call(
        tile_kernel,
        out_shape=jax.ShapeDtypeStruct((dev_rows, cols), F32),
        grid_spec=pltpu.PrefetchScalarGridSpec(
            num_scalar_prefetch=1,
            grid=(steps,),
            in_specs=[
                pl.BlockSpec((epochs, rows), lambda i, place: (0, i)),
                pl.BlockSpec(band.shape, whole),
                pl.BlockSpec(right.shape, whole),
                pl.BlockSpec((1, rows), lambda i, place: (0, place[0] * steps + i)),
                pl.BlockSpec(factor.shape, whole),
            ],
            out_specs=pl.BlockSpec((rows, cols), lambda i, place: (i, 0)),
            scratch_shapes=[pltpu.VMEM((epochs, rows), BF16)],
        ),
        compiler_params=pltpu.CompilerParams(vmem_limit_bytes=48 << 20),
        name="multiply_tile",
    )(place, left, band, right, regular.reshape(1, -1), factor)


AXES = ("ep", "row", "col")


def spread_rows(block, owner_of):
    rows = lax.axis_size("row")
    groups = lax.axis_size(("ep", "col"))
    width = lax.axis_size("col")
    row = lax.axis_index("row")
    owner = jnp.asarray([owner_of(g) for g in range(groups)], jnp.int32)[lax.axis_index(("ep", "col"))]
    distance = rows // 2
    while distance >= 1:
        route = []
        for g in range(groups):
            for other in range(0, rows, 2 * distance):
                source = owner_of(g) ^ other
                place = lambda at: ((g // width) * rows + at) * width + g % width
                route.append((place(source), place(source ^ distance)))
        came = lax.ppermute(block, AXES, route)
        takes = ((row ^ owner) & (2 * distance - 1)) == distance
        block = jnp.where(takes, came, block)
        distance //= 2
    return block


def on_device(design, taps, tap_count, order, regular):
    epochs_dev, rows_dev = design.shape
    groups = lax.axis_size(("ep", "col"))
    cols_dev = regular.shape[0] // groups
    row = lax.axis_index("row")
    group = lax.axis_index(("ep", "col"))
    place = jnp.stack([row, group]).astype(jnp.int32)
    permuted, head = permute_local(design, order, tap_count)
    head = spread_rows(head, lambda g: 0)
    head = lax.all_gather(head, ("ep", "col"), axis=0, tiled=True)
    left = lax.all_gather(permuted, ("ep", "col"), axis=0, tiled=True)
    at = (group * cols_dev) % rows_dev
    right = lax.dynamic_slice_in_dim(left, at, cols_dev, 1)
    right = spread_rows(right, lambda g: g * cols_dev // rows_dev)
    band, factor, w, high, low = factor_panel(head, taps, regular)
    right = project_columns(place, right, band, w, high, low)
    return multiply_tile(place, left, band, right, regular, factor)


def solution(mesh):
    in_specs = (P(("ep", "col"), "row"), P(), P(("ep", "col")), P("row"), P())
    out_specs = P("row", ("ep", "col"))
    return jax.shard_map(
        on_device, mesh=mesh, in_specs=in_specs, out_specs=out_specs, check_vma=False
    )
```

```python
import functools

import jax
import jax.numpy as jnp
from jax import lax
from jax.experimental import pallas as pl
from jax.experimental.pallas import tpu as pltpu
from jax.sharding import PartitionSpec as P

PANEL = 256
SECTIONS = 2
HEAD = PANEL * SECTIONS
PB = 128
LANES = 128
BLOCK = 128
HALF = 256
SUB = 8
NOTE = 16
EXACT = lax.Precision.HIGHEST
F32 = jnp.float32
BF16 = jnp.bfloat16


def iota(shape, axis):
    return lax.broadcasted_iota(jnp.int32, shape, axis)


def dot(left, right, contract=((1,), (0,)), precision=None):
    return lax.dot_general(
        left, right, (contract, ((), ())), preferred_element_type=F32, precision=precision
    )


NT = ((1,), (1,))
TN = ((0,), (0,))
VMEM = pl.BlockSpec(memory_space=pltpu.VMEM)
SMEM = pl.BlockSpec(memory_space=pltpu.SMEM)
LIMIT = pltpu.CompilerParams(vmem_limit_bytes=48 << 20)


def permute_kernel(order_ref, counts_ref, design_ref, *out_refs):
    *chunk_refs, note_ref = out_refs
    epochs, rows = design_ref.shape
    halves = chunk_refs[0].shape[0]
    per_half = len(chunk_refs)
    local = order_ref[...] & (PB - 1)
    local = local.astype(F32).T
    lane = iota((PB, PB), 1).astype(F32)
    none = jnp.zeros((epochs, PB), BF16)
    for block in range(rows // (2 * HALF)):
        h, i = divmod(block, per_half)
        for part in range(HALF // PB):
            first = block * (2 * HALF // PB) + part
            second = first + HALF // PB
            pick = [jnp.where(local[:, g : g + 1] == lane, 1.0, 0.0) for g in (first, second)]
            pick = jnp.concatenate(pick, axis=1).astype(BF16)
            top = jnp.concatenate([design_ref[:, first * PB : (first + 1) * PB], none], axis=1)
            low = jnp.concatenate([none, design_ref[:, second * PB : (second + 1) * PB]], axis=1)
            packed = dot(pick, jnp.concatenate([top, low], axis=0), NT)
            chunk_refs[i][h, part * PB : (part + 1) * PB, :] = packed.astype(BF16)
    note_ref[:HALF, :] = chunk_refs[0][0]
    note_ref[HALF:, :] = jnp.broadcast_to(counts_ref[...].astype(F32), (NOTE, LANES)).astype(BF16)


def permute_local(design, order, tap_count, cols_dev):
    epochs, rows = design.shape
    halves, per_half = rows // cols_dev, cols_dev // (2 * HALF)
    chunk = jax.ShapeDtypeStruct((halves, HALF, LANES), BF16)
    note = jax.ShapeDtypeStruct((HALF + NOTE, LANES), BF16)
    counts = jnp.tile(tap_count, LANES // epochs).reshape(1, LANES)
    return pl.pallas_call(
        permute_kernel,
        out_shape=(chunk,) * per_half + (note,),
        in_specs=[VMEM] * 3,
        compiler_params=LIMIT,
        name="permute_local",
    )(order.reshape(rows // PB, PB), counts, design)


def filter_rows(blocks, band_ref, store):
    per = HALF // (LANES // 2)
    for b in range(band_ref.shape[0]):
        first = max(b * per - 1, 0)
        skip = 0 if b else LANES
        packed = jnp.concatenate([blocks(e) for e in range(first, (b + 1) * per)], axis=1)
        for half in range(2):
            got = dot(packed, band_ref[b, half, skip:, :]).astype(BF16)
            store(slice(half * HALF, (half + 1) * HALF), slice(b * HALF, (b + 1) * HALF), got)


def spread(tile, lane):
    return jnp.broadcast_to(tile[:, lane : lane + 1], (SUB, tile.shape[1]))


def row_of(tile, k):
    return jnp.broadcast_to(tile[k : k + 1, :], (SUB, tile.shape[1]))


def factor_block(work):
    halves = work.shape[1] // BLOCK
    groups = BLOCK // SUB
    for g in range(groups):
        rows = slice(g * SUB, (g + 1) * SUB)
        own = [work[rows, h * BLOCK : (h + 1) * BLOCK] for h in range(halves)]
        cols = [spread(own[0], g * SUB + j) for j in range(SUB)]
        a = {(i, j): row_of(cols[j], i) for j in range(SUB) for i in range(j, SUB)}
        u = [[row_of(own[h], k) for k in range(SUB)] for h in range(halves)]
        inv = []
        low = {}
        for k in range(SUB):
            r = lax.rsqrt(a[k, k])
            inv.append(r)
            for i in range(k + 1, SUB):
                low[i, k] = a[i, k] * r
            for j in range(k + 1, SUB):
                for i in range(j, SUB):
                    a[i, j] = a[i, j] - low[i, k] * low[j, k]
            for h in range(halves):
                u[h][k] = u[h][k] * r
                for j in range(k + 1, SUB):
                    u[h][j] = u[h][j] - low[j, k] * u[h][k]
        for h in range(halves):
            merged = u[h][0]
            for k in range(1, SUB):
                merged = jnp.where(iota((SUB, BLOCK), 0) == k, u[h][k], merged)
            work[rows, h * BLOCK : (h + 1) * BLOCK] = merged
        for t in range(g + 1, groups):
            below = slice(t * SUB, (t + 1) * SUB)
            tile = [work[below, h * BLOCK : (h + 1) * BLOCK] for h in range(halves)]
            left = [spread(tile[0], g * SUB + j) for j in range(SUB)]
            for k in range(SUB):
                left[k] = left[k] * inv[k]
                for j in range(k + 1, SUB):
                    left[j] = left[j] - low[j, k] * left[k]
                for h in range(halves):
                    tile[h] = tile[h] - left[k] * u[h][k]
            for h in range(halves):
                work[below, h * BLOCK : (h + 1) * BLOCK] = tile[h]


def start_kernel(
    sources, place_ref, taps_ref, own_ref, came_ref, reg_ref, band_ref, aug_ref, notes, a1, work
):
    chain, steps = sources
    epochs = aug_ref.shape[1] - HEAD
    half = LANES // 2

    @pl.when(place_ref[0] % 2 == 0)
    def _():
        for rel, at in enumerate(steps):
            notes[place_ref[chain + rel]] = own_ref[rel]

    @pl.when(place_ref[0] % 2 == 1)
    def _():
        for rel, at in enumerate(steps):
            notes[place_ref[chain + rel]] = came_ref[rel]

    shape = (half, LANES)
    lag = iota(shape, 1) - iota(shape, 0)
    base = lax.fori_loop(
        0,
        taps_ref.shape[0],
        lambda k, kept: jnp.where(lag == k, taps_ref[k], kept),
        jnp.zeros(shape, F32),
    )
    lane = iota(shape, 1)
    swapped = jnp.concatenate([base[:, half:], base[:, :half]], axis=1)
    early = jnp.where(lane < half, swapped, 0.0)
    late = jnp.where(lane >= half, swapped, 0.0)
    none = jnp.zeros(shape, F32)
    patterns = [(early, none), (base, none), (late, early), (none, base), (none, late)]
    row = iota((1, LANES), 1)
    band_ref[...] = jnp.zeros_like(band_ref)
    for b in range(epochs // HALF):
        for side in range(HALF // LANES):
            e = (b * HALF + side * LANES) // half
            counts = [notes[e + n, HALF : HALF + NOTE, :].astype(F32)[:1] for n in range(2)]
            counts = jnp.where(row < half, counts[0], counts[1])
            for j, pattern in enumerate(patterns):
                at = (lag + side * LANES + half - half * j).astype(F32)
                kept = jnp.where(at < counts, pattern[side], 0.0).astype(BF16)
                for h in range(2):
                    rows = slice(j * LANES + h * half, j * LANES + (h + 1) * half)
                    band_ref[b, h, rows, side * LANES : (side + 1) * LANES] = kept

    def store(rows, cols, got):
        a1[rows, cols] = got

    filter_rows(lambda e: notes[e, :HALF, :], band_ref, store)
    columns = a1[...]
    square = (HEAD, HEAD)
    on_diagonal = iota(square, 0) == iota(square, 1)
    aug_ref[:, :HEAD] = dot(columns, columns, NT) + jnp.where(on_diagonal, reg_ref[...], 0.0)
    aug_ref[:, HEAD:] = columns.astype(F32)
    eliminate(aug_ref, 0, work)


def eliminate(aug, kb, work):
    here = slice(kb * BLOCK, (kb + 1) * BLOCK)
    work[:, :BLOCK] = aug[here, here]
    work[:, BLOCK:] = jnp.where(iota((BLOCK, BLOCK), 0) == iota((BLOCK, BLOCK), 1), 1.0, 0.0)
    factor_block(work)
    rest = slice(kb * BLOCK, aug.shape[1])
    aug[here, rest] = dot(work[:, BLOCK:], aug[here, rest], precision=EXACT)
    for rb in range(kb + 1, HEAD // BLOCK):
        below = slice(rb * BLOCK, (rb + 1) * BLOCK)
        rest = slice(rb * BLOCK, aug.shape[1])
        aug[below, rest] -= dot(aug[here, below], aug[here, rest], TN, precision=EXACT)


def next_kernel(kb, aug_in, aug_ref, work):
    done = slice(0, kb * BLOCK)
    aug_ref[...] = aug_in[...]
    eliminate(aug_ref, kb, work)


def last_kernel(kb, aug_in, factor_ref, w_ref, high_ref, low_ref, aug, work):
    aug[...] = aug_in[...]
    eliminate(aug, kb, work)
    square = (HEAD, HEAD)
    epochs = aug.shape[1] - HEAD
    factor_ref[...] = jnp.where(iota(square, 0) >= iota(square, 1), aug[:, :HEAD].T, 0.0)
    wt = aug[:, HEAD:]
    w_ref[...] = wt.T.astype(BF16)
    for b in range(epochs // BLOCK):
        here = slice(b * BLOCK, (b + 1) * BLOCK)
        shape = (BLOCK, epochs)
        unit = jnp.where(iota(shape, 0) + b * BLOCK == iota(shape, 1), 1.0, 0.0)
        middle = unit - dot(wt[:, here], wt, TN, precision=EXACT)
        high = middle.astype(BF16)
        high_ref[here, :] = high
        low_ref[here, :] = (middle - high.astype(F32)).astype(BF16)


def start_panel(place, chain, taps, own, came, regular):
    sources, epochs = own.shape[0], own.shape[0] * (LANES // 2)
    per = HALF // (LANES // 2)
    return pl.pallas_call(
        functools.partial(start_kernel, (chain, range(sources))),
        out_shape=(
            jax.ShapeDtypeStruct((epochs // HALF, 2, (per + 1) * LANES, HALF), BF16),
            jax.ShapeDtypeStruct((HEAD, HEAD + epochs), F32),
        ),
        in_specs=[SMEM, SMEM, VMEM, VMEM, VMEM],
        out_specs=(VMEM, VMEM),
        scratch_shapes=[
            pltpu.VMEM(own.shape, BF16),
            pltpu.VMEM((HEAD, epochs), BF16),
            pltpu.VMEM((BLOCK, 2 * BLOCK), F32),
        ],
        compiler_params=LIMIT,
        cost_estimate=pl.CostEstimate(flops=1 << 30, bytes_accessed=24 << 20, transcendentals=0),
        name="start_panel",
    )(place, taps, own, came, regular[:HEAD].reshape(1, HEAD))


def next_panel(kb, aug):
    return pl.pallas_call(
        functools.partial(next_kernel, kb),
        out_shape=jax.ShapeDtypeStruct(aug.shape, F32),
        in_specs=[VMEM],
        out_specs=VMEM,
        scratch_shapes=[pltpu.VMEM((BLOCK, 2 * BLOCK), F32)],
        compiler_params=LIMIT,
        cost_estimate=pl.CostEstimate(flops=1 << 30, bytes_accessed=20 << 20, transcendentals=0),
        name="next_panel",
    )(aug)


def last_panel(kb, aug):
    epochs = aug.shape[1] - HEAD
    return pl.pallas_call(
        functools.partial(last_kernel, kb),
        out_shape=(
            jax.ShapeDtypeStruct((HEAD, HEAD), F32),
            jax.ShapeDtypeStruct((epochs, HEAD), BF16),
            jax.ShapeDtypeStruct((epochs, epochs), BF16),
            jax.ShapeDtypeStruct((epochs, epochs), BF16),
        ),
        in_specs=[VMEM],
        out_specs=(VMEM,) * 4,
        scratch_shapes=[pltpu.VMEM(aug.shape, F32), pltpu.VMEM((BLOCK, 2 * BLOCK), F32)],
        compiler_params=LIMIT,
        cost_estimate=pl.CostEstimate(flops=1 << 30, bytes_accessed=24 << 20, transcendentals=0),
        name="last_panel",
    )(aug)


def tile_kernel(chunks, halves, place_ref, *refs):
    own_refs, other_refs = refs[:chunks], refs[chunks : 2 * chunks]
    right_refs, came_refs = refs[2 * chunks : 3 * chunks], refs[3 * chunks : 4 * chunks]
    band_ref, w_ref, high_ref, low_ref, factor_ref, reg_ref, out_ref = refs[4 * chunks : -3]
    blocks, filtered, right = refs[-3:]
    rows, cols = out_ref.shape
    width = own_refs[0].shape[0]
    step = pl.program_id(0)
    row, group, side, takes = (place_ref[n] for n in range(4))
    first_row = (row * chunks * halves + (step % halves) * chunks + step // halves) * rows
    first_col = group * cols

    def store(at_rows, at_cols, got):
        filtered[at_rows, at_cols] = got

    @pl.when(step == 0)
    def _():
        for i in range(chunks):

            @pl.when(takes == 0)
            def _():
                blocks[...] = right_refs[i][...]

            @pl.when(takes != 0)
            def _():
                blocks[...] = came_refs[i][...]

            filter_rows(lambda e: blocks[e], band_ref, store)
            columns = filtered[...]
            projected = dot(high_ref[...], columns, NT) + dot(low_ref[...], columns, NT)
            right[:, i * rows : (i + 1) * rows] = projected.astype(BF16)

        @pl.when(group == 0)
        def _():
            right[:, :HEAD] = w_ref[...]

    @pl.when(first_row >= HEAD)
    def _():
        for i in range(chunks):
            for h in range(halves):

                @pl.when(step == i * halves + h)
                def _():
                    blocks[pl.ds(side * width, width)] = own_refs[i][:, h]
                    blocks[pl.ds((1 - side) * width, width)] = other_refs[i][:, h]

        filter_rows(lambda e: blocks[e], band_ref, store)
        out_ref[...] = dot(filtered[...], right[...])

        @pl.when((first_row >= first_col) & (first_row < first_col + cols))
        def _():
            at = pl.multiple_of(first_row - first_col, rows)
            on_diagonal = iota((rows, rows), 0) == iota((rows, rows), 1)
            out_ref[:, pl.ds(at, rows)] += jnp.where(on_diagonal, reg_ref[...], 0.0)

    @pl.when(first_row < HEAD)
    def _():
        out_ref[...] = jnp.zeros_like(out_ref)

        @pl.when(first_col == 0)
        def _():
            out_ref[:, :HEAD] = factor_ref[...]


def multiply_tile(place, own, other, right, came, band, w, high, low, factor, regular, cols):
    chunks, (width, halves) = len(own), own[0].shape[:2]
    rows = 2 * HALF
    steps = chunks * halves
    epochs = high.shape[0]
    block = lambda i: (i % halves) * chunks + i // halves
    fixed = lambda array: pl.BlockSpec(
        array.shape, lambda i, place: (0,) * array.ndim, pipeline_mode=pl.Buffered(1)
    )
    operands = (*own, *other, *right, *came, band, w, high, low, factor)
    return pl.pallas_call(
        functools.partial(tile_kernel, chunks, halves),
        out_shape=jax.ShapeDtypeStruct((steps * rows, cols), F32),
        grid_spec=pltpu.PrefetchScalarGridSpec(
            num_scalar_prefetch=1,
            grid=(steps,),
            in_specs=[fixed(array) for array in operands]
            + [pl.BlockSpec((1, rows), lambda i, place: (0, place[0] * steps + block(i)))],
            out_specs=pl.BlockSpec((rows, cols), lambda i, place: (block(i), 0)),
            scratch_shapes=[
                pltpu.VMEM((epochs // (LANES // 2), HALF, LANES), BF16),
                pltpu.VMEM((rows, epochs), BF16),
                pltpu.VMEM((epochs, cols), BF16),
            ],
        ),
        compiler_params=pltpu.CompilerParams(vmem_limit_bytes=56 << 20),
        name="multiply_tile",
    )(place, *operands, regular.reshape(1, -1))


AXES = ("ep", "row", "col")


def flat(ep, row, col):
    return (ep * lax.axis_size("row") + row) * lax.axis_size("col") + col


def spread_rows(block, owner_of, distances):
    row = lax.axis_index("row")
    eps, cols, rows = (lax.axis_size(axis) for axis in ("ep", "col", "row"))
    owners = jnp.asarray([owner_of(e, c) for e in range(eps) for c in range(cols)], jnp.int32)
    owner = owners[lax.axis_index(("ep", "col"))]
    for n, distance in enumerate(distances):
        route = []
        for e in range(eps):
            for c in range(cols):
                for other in range(0, rows, 2 * distance):
                    source = owner_of(e, c) ^ other
                    route.append((flat(e, source, c), flat(e, source ^ distance, c)))
        came = lax.ppermute(block, AXES, route)
        takes = ((row ^ owner) & (2 * distance - 1)) == distance
        if n == len(distances) - 1:
            return block, came, takes
        block = jnp.where(takes, came, block)


def doubling(count, least):
    distances = []
    distance = count // 2
    while distance >= least:
        distances.append(distance)
        distance //= 2
    return distances


def gather_panel(note):
    eps, cols, rows = (lax.axis_size(axis) for axis in ("ep", "col", "row"))
    distances = doubling(rows, 2)
    if distances:
        block, came, takes = spread_rows(note, lambda e, c: 0, distances)
        note = jnp.where(takes, came, block)
    notes = [note]
    steps = [(0, 0)]
    for de in range(eps):
        for dc in range(cols):
            if de or dc:
                route = [
                    (flat(e, r, c), flat((e + de) % eps, r, (c + dc) % cols))
                    for e in range(eps)
                    for r in range(0, rows, 2)
                    for c in range(cols)
                ]
                notes.append(lax.ppermute(note, AXES, route))
                steps.append((de, dc))
    notes = jnp.stack(notes)
    came = lax.ppermute(notes, "row", [(r, r + 1) for r in range(0, rows, 2)])
    ep, col = lax.axis_index("ep"), lax.axis_index("col")
    order = [((ep - de) % eps) * cols + (col - dc) % cols for de, dc in steps]
    return notes, came, order


def on_device(design, taps, tap_count, order, regular):
    epochs_dev, rows_dev = design.shape
    eps, cols, rows = (lax.axis_size(axis) for axis in ("ep", "col", "row"))
    groups = eps * cols
    cols_dev = regular.shape[0] // groups
    row, ep = lax.axis_index("row"), lax.axis_index("ep")
    group = lax.axis_index(("ep", "col"))
    *chunks, note = permute_local(design, order, tap_count, cols_dev)
    notes, came, sources = gather_panel(note)
    column = [lax.all_gather(chunk, "col", axis=0) for chunk in chunks]
    other = [lax.ppermute(chunk, "ep", [(0, 1), (1, 0)]) for chunk in column]
    owner = lambda e, c: (e * cols + c) * cols_dev // rows_dev
    half = (group * cols_dev % rows_dev) // cols_dev
    right, right_came = [], []
    for mine, theirs in zip(column, other):
        mine = lax.dynamic_index_in_dim(mine, half, 1, keepdims=False)
        theirs = lax.dynamic_index_in_dim(theirs, half, 1, keepdims=False)
        low = jnp.where(ep == 0, mine, theirs)
        high = jnp.where(ep == 0, theirs, mine)
        block, got, takes = spread_rows(jnp.concatenate([low, high]), owner, doubling(rows, 1))
        right.append(block)
        right_came.append(got)
    place = jnp.stack([row, group, ep, takes.astype(jnp.int32), *sources]).astype(jnp.int32)
    band, aug = start_panel(place, 4, taps, notes, came, regular)
    panels = HEAD // BLOCK
    for kb in range(1, panels - 1):
        aug = next_panel(kb, aug)
    factor, w, high, low = last_panel(panels - 1, aug)
    return multiply_tile(
        place, column, other, right, right_came, band, w, high, low, factor, regular, cols_dev
    )


def solution(mesh):
    in_specs = (P(("ep", "col"), "row"), P(), P(("ep", "col")), P("row"), P())
    out_specs = P("row", ("ep", "col"))
    return jax.shard_map(
        on_device, mesh=mesh, in_specs=in_specs, out_specs=out_specs, check_vma=False
    )
```

```python
import functools

import jax
import jax.numpy as jnp
from jax import lax
from jax.experimental import pallas as pl
from jax.experimental.pallas import tpu as pltpu
from jax.sharding import PartitionSpec as P

PANEL = 256
SECTIONS = 2
HEAD = PANEL * SECTIONS
PB = 128
LANES = 128
BLOCK = 128
HALF = 256
SUB = 8
NOTE = 16
EXACT = lax.Precision.HIGHEST
F32 = jnp.float32
BF16 = jnp.bfloat16


def iota(shape, axis):
    return lax.broadcasted_iota(jnp.int32, shape, axis)


def dot(left, right, contract=((1,), (0,)), precision=None):
    return lax.dot_general(
        left, right, (contract, ((), ())), preferred_element_type=F32, precision=precision
    )


NT = ((1,), (1,))
TN = ((0,), (0,))
VMEM = pl.BlockSpec(memory_space=pltpu.VMEM)
SMEM = pl.BlockSpec(memory_space=pltpu.SMEM)
ANY = pl.BlockSpec(memory_space=pl.ANY)
LIMIT = pltpu.CompilerParams(vmem_limit_bytes=48 << 20)


def permute_kernel(place_ref, order_ref, counts_ref, design_ref, *out_refs):
    *part_refs, note_ref = out_refs
    epochs = design_ref.shape[0]
    parts, per_part = len(part_refs), part_refs[0].shape[0]
    lane = iota((PB, PB), 1).astype(F32)
    none = jnp.zeros((epochs, PB), BF16)
    groups = 2 * HALF // PB

    def packed(local, columns, block, part):
        first = block * groups + part
        second = first + HALF // PB
        pick = [jnp.where(local[:, g : g + 1] == lane, 1.0, 0.0) for g in (first, second)]
        pick = jnp.concatenate(pick, axis=1).astype(BF16)
        top = jnp.concatenate([columns(first), none], axis=1)
        low = jnp.concatenate([none, columns(second)], axis=1)
        return dot(pick, jnp.concatenate([top, low], axis=0), NT).astype(BF16)

    def order_of(rows):
        return (order_ref[rows, :] & (PB - 1)).astype(F32).T

    local = order_of(slice(0, per_part * groups))
    for part in range(HALF // PB):
        columns = lambda g: design_ref[:, g * PB : (g + 1) * PB]
        note_ref[0, part * PB : (part + 1) * PB, :] = packed(local, columns, 0, part)
    counts = counts_ref[...].astype(F32)
    counts = jnp.concatenate([counts] * (LANES // epochs), axis=1)
    note_ref[0, HALF:, :] = jnp.broadcast_to(counts, (NOTE, LANES)).astype(BF16)
    for j in range(parts):
        piece = lax.rem(place_ref[PLACE_COL] + j, parts)
        at = pl.multiple_of(piece * per_part * groups, per_part * groups)
        local = order_of(pl.ds(at, per_part * groups))
        columns = lambda g: design_ref[:, pl.ds(pl.multiple_of((at + g) * PB, PB), PB)]
        for block in range(per_part):
            for part in range(HALF // PB):
                part_refs[j][block, part * PB : (part + 1) * PB, :] = packed(
                    local, columns, block, part
                )


def permute_local(place, design, order, tap_count, cols_dev):
    epochs, rows = design.shape
    parts, per_part = rows // cols_dev, cols_dev // (2 * HALF)
    piece = jax.ShapeDtypeStruct((per_part, HALF, LANES), BF16)
    note = jax.ShapeDtypeStruct((1, HALF + NOTE, LANES), BF16)
    return pl.pallas_call(
        permute_kernel,
        out_shape=(piece,) * parts + (note,),
        in_specs=[SMEM] + [VMEM] * 3,
        out_specs=(VMEM,) * (parts + 1),
        compiler_params=LIMIT,
        name="permute_local",
    )(place, order.reshape(rows // PB, PB), tap_count.reshape(1, epochs), design)


PLACE_ROW, PLACE_GROUP, PLACE_EP, PLACE_COL, PLACE_TAKES, PLACE_INSIDE, PLACE_OWNS, PLACE_BACK = range(8)


def assemble_kernel(flag, count, place_ref, *refs):
    first, second = refs[:count], refs[count : 2 * count]
    out_ref, sem = refs[-2:]

    def copy(sources):
        copies = [
            pltpu.make_async_copy(source, out_ref.at[n], sem.at[n]) for n, source in enumerate(sources)
        ]
        for c in copies:
            c.start()
        for c in copies:
            c.wait()

    if flag is None:
        copy(first)
        return

    @pl.when(place_ref[flag] != 0)
    def _():
        copy(first)

    @pl.when(place_ref[flag] == 0)
    def _():
        copy(second)


def assemble(place, first, second, flag, gated=(), after=()):
    count = len(first)
    shards = [*first, *(second if flag is not None else first)]

    def kernel(place_ref, *refs):
        inputs, rest = refs[: 2 * count], refs[2 * count + len(gated) + len(after) :]
        assemble_kernel(flag, count, place_ref, *inputs, rest[0], rest[-1])

    out = pl.pallas_call(
        kernel,
        out_shape=(
            jax.ShapeDtypeStruct((count,) + first[0].shape, BF16),
            *(jax.ShapeDtypeStruct(g.shape, g.dtype) for g in gated),
        ),
        in_specs=[SMEM] + [ANY] * (2 * count + len(gated) + len(after)),
        out_specs=(ANY,) * (1 + len(gated)),
        input_output_aliases={1 + 2 * count + n: 1 + n for n in range(len(gated))},
        scratch_shapes=[pltpu.SemaphoreType.DMA((count,))],
        compiler_params=LIMIT,
        name="assemble",
    )(place, *shards, *gated, *after)
    return out[0], list(out[1:])


def filter_rows(blocks, band_ref, store):
    per = HALF // (LANES // 2)
    for b in range(band_ref.shape[0]):
        first = max(b * per - 1, 0)
        skip = 0 if b else LANES
        packed = jnp.concatenate([blocks(e) for e in range(first, (b + 1) * per)], axis=1)
        for half in range(2):
            got = dot(packed, band_ref[b, half, skip:, :]).astype(BF16)
            store(slice(half * HALF, (half + 1) * HALF), slice(b * HALF, (b + 1) * HALF), got)


def spread(tile, lane):
    return jnp.broadcast_to(tile[:, lane : lane + 1], (SUB, tile.shape[1]))


def row_of(tile, k):
    return jnp.broadcast_to(tile[k : k + 1, :], (SUB, tile.shape[1]))


def factor_block(work):
    halves = work.shape[1] // BLOCK
    groups = BLOCK // SUB
    for g in range(groups):
        rows = slice(g * SUB, (g + 1) * SUB)
        own = [work[rows, h * BLOCK : (h + 1) * BLOCK] for h in range(halves)]
        cols = [spread(own[0], g * SUB + j) for j in range(SUB)]
        a = {(i, j): row_of(cols[j], i) for j in range(SUB) for i in range(j, SUB)}
        u = [[row_of(own[h], k) for k in range(SUB)] for h in range(halves)]
        inv = []
        low = {}
        for k in range(SUB):
            r = lax.rsqrt(a[k, k])
            inv.append(r)
            for i in range(k + 1, SUB):
                low[i, k] = a[i, k] * r
            for j in range(k + 1, SUB):
                for i in range(j, SUB):
                    a[i, j] = a[i, j] - low[i, k] * low[j, k]
            for h in range(halves):
                u[h][k] = u[h][k] * r
                for j in range(k + 1, SUB):
                    u[h][j] = u[h][j] - low[j, k] * u[h][k]
        for h in range(halves):
            merged = u[h][0]
            for k in range(1, SUB):
                merged = jnp.where(iota((SUB, BLOCK), 0) == k, u[h][k], merged)
            work[rows, h * BLOCK : (h + 1) * BLOCK] = merged
        for t in range(g + 1, groups):
            below = slice(t * SUB, (t + 1) * SUB)
            tile = [work[below, h * BLOCK : (h + 1) * BLOCK] for h in range(halves)]
            left = [spread(tile[0], g * SUB + j) for j in range(SUB)]
            for k in range(SUB):
                left[k] = left[k] * inv[k]
                for j in range(k + 1, SUB):
                    left[j] = left[j] - low[j, k] * left[k]
                for h in range(halves):
                    tile[h] = tile[h] - left[k] * u[h][k]
            for h in range(halves):
                work[below, h * BLOCK : (h + 1) * BLOCK] = tile[h]


def start_kernel(
    chain, place_ref, taps_ref, own_ref, came_ref, reg_ref, after, band_ref, aug_ref, notes, a1, work
):
    del after
    epochs = aug_ref.shape[1] - HEAD
    half = LANES // 2

    @pl.when(place_ref[0] % 2 == 0)
    def _():
        for rel in range(own_ref.shape[0]):
            notes[place_ref[chain + rel]] = own_ref[rel]

    @pl.when(place_ref[0] % 2 == 1)
    def _():
        for rel in range(own_ref.shape[0]):
            notes[place_ref[chain + rel]] = came_ref[rel]

    shape = (half, LANES)
    lag = iota(shape, 1) - iota(shape, 0)
    base = lax.fori_loop(
        0,
        taps_ref.shape[0],
        lambda k, kept: jnp.where(lag == k, taps_ref[k], kept),
        jnp.zeros(shape, F32),
    )
    lane = iota(shape, 1)
    swapped = jnp.concatenate([base[:, half:], base[:, :half]], axis=1)
    early = jnp.where(lane < half, swapped, 0.0)
    late = jnp.where(lane >= half, swapped, 0.0)
    none = jnp.zeros(shape, F32)
    patterns = [(early, none), (base, none), (late, early), (none, base), (none, late)]
    row = iota((1, LANES), 1)
    band_ref[...] = jnp.zeros_like(band_ref)
    for b in range(epochs // HALF):
        for side in range(HALF // LANES):
            e = (b * HALF + side * LANES) // half
            counts = [notes[e + n, HALF : HALF + NOTE, :].astype(F32)[:1] for n in range(2)]
            counts = jnp.where(row < half, counts[0], counts[1])
            for j, pattern in enumerate(patterns):
                at = (lag + side * LANES + half - half * j).astype(F32)
                kept = jnp.where(at < counts, pattern[side], 0.0).astype(BF16)
                for h in range(2):
                    rows = slice(j * LANES + h * half, j * LANES + (h + 1) * half)
                    band_ref[b, h, rows, side * LANES : (side + 1) * LANES] = kept

    def store(rows, cols, got):
        a1[rows, cols] = got

    filter_rows(lambda e: notes[e, :HALF, :], band_ref, store)
    columns = a1[...]
    square = (HEAD, HEAD)
    on_diagonal = iota(square, 0) == iota(square, 1)
    aug_ref[:, :HEAD] = dot(columns, columns, NT) + jnp.where(on_diagonal, reg_ref[...], 0.0)
    aug_ref[:, HEAD:] = columns.astype(F32)
    eliminate(aug_ref, 0, work)


def eliminate(aug, kb, work):
    here = slice(kb * BLOCK, (kb + 1) * BLOCK)
    work[:, :BLOCK] = aug[here, here]
    work[:, BLOCK:] = jnp.where(iota((BLOCK, BLOCK), 0) == iota((BLOCK, BLOCK), 1), 1.0, 0.0)
    factor_block(work)
    rest = slice(kb * BLOCK, aug.shape[1])
    aug[here, rest] = dot(work[:, BLOCK:], aug[here, rest], precision=EXACT)
    for rb in range(kb + 1, HEAD // BLOCK):
        below = slice(rb * BLOCK, (rb + 1) * BLOCK)
        rest = slice(rb * BLOCK, aug.shape[1])
        aug[below, rest] -= dot(aug[here, below], aug[here, rest], TN, precision=EXACT)


def next_kernel(kb, aug_in, after, aug_ref, work):
    del after
    aug_ref[...] = aug_in[...]
    eliminate(aug_ref, kb, work)


def last_kernel(kb, aug_in, after, factor_ref, w_ref, high_ref, low_ref, aug, work):
    del after
    aug[...] = aug_in[...]
    eliminate(aug, kb, work)
    square = (HEAD, HEAD)
    epochs = aug.shape[1] - HEAD
    factor_ref[...] = jnp.where(iota(square, 0) >= iota(square, 1), aug[:, :HEAD].T, 0.0)
    wt = aug[:, HEAD:]
    w_ref[...] = wt.T.astype(BF16)
    for b in range(epochs // BLOCK):
        here = slice(b * BLOCK, (b + 1) * BLOCK)
        shape = (BLOCK, epochs)
        unit = jnp.where(iota(shape, 0) + b * BLOCK == iota(shape, 1), 1.0, 0.0)
        middle = unit - dot(wt[:, here], wt, TN, precision=EXACT)
        high = middle.astype(BF16)
        high_ref[here, :] = high
        low_ref[here, :] = (middle - high.astype(F32)).astype(BF16)


def start_panel(place, chain, taps, own, came, regular, after):
    epochs = own.shape[0] * (LANES // 2)
    per = HALF // (LANES // 2)
    return pl.pallas_call(
        functools.partial(start_kernel, chain),
        out_shape=(
            jax.ShapeDtypeStruct((epochs // HALF, 2, (per + 1) * LANES, HALF), BF16),
            jax.ShapeDtypeStruct((HEAD, HEAD + epochs), F32),
        ),
        in_specs=[SMEM, SMEM, VMEM, VMEM, VMEM, ANY],
        out_specs=(VMEM, VMEM),
        scratch_shapes=[
            pltpu.VMEM(own.shape, BF16),
            pltpu.VMEM((HEAD, epochs), BF16),
            pltpu.VMEM((BLOCK, 2 * BLOCK), F32),
        ],
        compiler_params=LIMIT,
        cost_estimate=pl.CostEstimate(flops=7 << 30, bytes_accessed=24 << 20, transcendentals=0),
        name="start_panel",
    )(place, taps, own, came, regular[:HEAD].reshape(1, HEAD), after)


def next_panel(kb, aug, after):
    return pl.pallas_call(
        functools.partial(next_kernel, kb),
        out_shape=jax.ShapeDtypeStruct(aug.shape, F32),
        in_specs=[VMEM, ANY],
        out_specs=VMEM,
        scratch_shapes=[pltpu.VMEM((BLOCK, 2 * BLOCK), F32)],
        compiler_params=LIMIT,
        cost_estimate=pl.CostEstimate(flops=7 << 30, bytes_accessed=20 << 20, transcendentals=0),
        name="next_panel",
    )(aug, after)


def last_panel(kb, aug, after):
    epochs = aug.shape[1] - HEAD
    return pl.pallas_call(
        functools.partial(last_kernel, kb),
        out_shape=(
            jax.ShapeDtypeStruct((HEAD, HEAD), F32),
            jax.ShapeDtypeStruct((epochs, HEAD), BF16),
            jax.ShapeDtypeStruct((epochs, epochs), BF16),
            jax.ShapeDtypeStruct((epochs, epochs), BF16),
        ),
        in_specs=[VMEM, ANY],
        out_specs=(VMEM,) * 4,
        scratch_shapes=[pltpu.VMEM(aug.shape, F32), pltpu.VMEM((BLOCK, 2 * BLOCK), F32)],
        compiler_params=LIMIT,
        cost_estimate=pl.CostEstimate(flops=7 << 30, bytes_accessed=24 << 20, transcendentals=0),
        name="last_panel",
    )(aug, after)


def unpack(place_ref, own, other, blocks):
    width = own.shape[0]
    here = place_ref[PLACE_EP] * width
    there = width - here
    for n in range(width):
        back = place_ref[PLACE_BACK + n]
        blocks[here + back] = own[n, 0]
        blocks[there + back] = other[n, 0]


def choose(condition, yes, no):
    pl.when(condition)(yes)
    pl.when(jnp.logical_not(condition))(no)


def project_kernel(
    place_ref, own_ref, own_came, other_ref, other_came, band_ref, w_ref, high_ref, low_ref, after,
    out_ref, blocks, filtered,
):
    del after

    def store(rows, cols, got):
        filtered[rows, cols] = got

    choose(
        place_ref[PLACE_TAKES] != 0,
        lambda: unpack(place_ref, own_came, other_came, blocks),
        lambda: unpack(place_ref, own_ref, other_ref, blocks),
    )
    filter_rows(lambda e: blocks[e], band_ref, store)
    columns = filtered[...]
    projected = dot(high_ref[...], columns, NT) + dot(low_ref[...], columns, NT)
    out_ref[...] = projected.astype(BF16)

    @pl.when((place_ref[PLACE_GROUP] == 0) & (pl.program_id(0) == 0))
    def _():
        out_ref[...] = w_ref[...]


def fixed(array):
    return pl.BlockSpec(
        array.shape, lambda i, place: (0,) * array.ndim, pipeline_mode=pl.Buffered(1)
    )


def shards_spec(array):
    return pl.BlockSpec((array.shape[0], 1, HALF, LANES), lambda i, place: (0, i, 0, 0))


def project(place, shards, band, w, high, low, after):
    width, count = shards[0].shape[:2]
    epochs = high.shape[0]
    return pl.pallas_call(
        project_kernel,
        out_shape=jax.ShapeDtypeStruct((epochs, count * 2 * HALF), BF16),
        grid_spec=pltpu.PrefetchScalarGridSpec(
            num_scalar_prefetch=1,
            grid=(count,),
            in_specs=[shards_spec(array) for array in shards]
            + [fixed(array) for array in (band, w, high, low)]
            + [ANY],
            out_specs=pl.BlockSpec((epochs, 2 * HALF), lambda i, place: (0, i)),
            scratch_shapes=[
                pltpu.VMEM((epochs // (LANES // 2), HALF, LANES), BF16),
                pltpu.VMEM((2 * HALF, epochs), BF16),
            ],
        ),
        compiler_params=LIMIT,
        name="project",
    )(place, *shards, band, w, high, low, after)


def tile_kernel(
    part, parts, aliased, place_ref, own_ref, other_ref, theirs_ref, band_ref, right_ref, factor_ref,
    reg_ref, *refs,
):
    out_ref, blocks, filtered, made, sems = refs[aliased:]
    step, steps = pl.program_id(0), pl.num_programs(0)
    epochs, cols = right_ref.shape
    rows = 2 * HALF
    piece = lax.rem(place_ref[PLACE_COL] + part, parts)
    block = piece * steps + step
    first_row = (place_ref[PLACE_ROW] * parts * steps + block) * rows
    first_col = place_ref[PLACE_GROUP] * cols
    wide = rows
    count = cols // wide
    slot = lax.rem(step, 2)

    def copies(at_step, n):
        at_slot = lax.rem(at_step, 2)
        start = pl.multiple_of((piece * steps + at_step) * rows, rows)
        across = slice(n * wide, (n + 1) * wide)
        return pltpu.make_async_copy(
            made.at[at_slot, n], out_ref.at[pl.ds(start, rows), across], sems.at[at_slot, n]
        )

    def store(at_rows, at_cols, got):
        filtered[at_rows, at_cols] = got

    choose(
        (place_ref[PLACE_OWNS] != 0) & (part == 0),
        lambda: unpack(place_ref, own_ref, theirs_ref, blocks),
        lambda: unpack(place_ref, own_ref, other_ref, blocks),
    )
    filter_rows(lambda e: blocks[e], band_ref, store)
    for n in range(count):

        @pl.when(step >= 2)
        def _():
            copies(step - 2, n).wait()

        @pl.when(first_row >= HEAD)
        def _():
            made[slot, n] = dot(filtered[...], right_ref[:, n * wide : (n + 1) * wide])

            @pl.when(first_row == first_col + n * wide)
            def _():
                on_diagonal = iota((rows, rows), 0) == iota((rows, rows), 1)
                made[slot, n] += jnp.where(on_diagonal, reg_ref[...], 0.0)

        @pl.when(first_row < HEAD)
        def _():
            made[slot, n] = jnp.zeros((rows, wide), F32)
            if n == 0:

                @pl.when(first_col == 0)
                def _():
                    made[slot, n] = factor_ref[...]

        copies(step, n).start()

    @pl.when(step == steps - 1)
    def _():
        for n in range(count):

            @pl.when(steps > 1)
            def _():
                copies(step - 1, n).wait()

            copies(step, n).wait()


def multiply_part(part, parts, place, own, other, theirs, band, right, factor, regular, out):
    width, steps = own.shape[:2]
    rows = 2 * HALF
    epochs, cols = right.shape

    def reg_block(i, place):
        piece = lax.rem(place[PLACE_COL] + part, parts)
        return 0, (place[PLACE_ROW] * parts + piece) * steps + i

    aliased = 0 if out is None else 1
    return pl.pallas_call(
        functools.partial(tile_kernel, part, parts, aliased),
        out_shape=jax.ShapeDtypeStruct((parts * steps * rows, cols), F32),
        grid_spec=pltpu.PrefetchScalarGridSpec(
            num_scalar_prefetch=1,
            grid=(steps,),
            in_specs=[shards_spec(array) for array in (own, other, theirs)]
            + [fixed(array) for array in (band, right, factor)]
            + [pl.BlockSpec((1, rows), reg_block)]
            + [ANY] * aliased,
            out_specs=ANY,
            scratch_shapes=[
                pltpu.VMEM((epochs // (LANES // 2), HALF, LANES), BF16),
                pltpu.VMEM((rows, epochs), BF16),
                pltpu.VMEM((2, cols // rows, rows, rows), F32),
                pltpu.SemaphoreType.DMA((2, cols // rows)),
            ],
        ),
        input_output_aliases={8: 0} if aliased else {},
        compiler_params=pltpu.CompilerParams(vmem_limit_bytes=56 << 20),
        cost_estimate=pl.CostEstimate(
            flops=10 << 30, bytes_accessed=steps * rows * cols * 4, transcendentals=0
        ),
        name="multiply_part",
    )(
        place, own, other, theirs, band, right, factor, regular.reshape(1, -1),
        *([out] if aliased else []),
    )


AXES = ("ep", "row", "col")


def sizes():
    return tuple(lax.axis_size(axis) for axis in AXES)


def flat(ep, row, col):
    _, rows, cols = sizes()
    return (ep * rows + row) * cols + col


def doubling(count, least):
    distances = []
    distance = count // 2
    while distance >= least:
        distances.append(distance)
        distance //= 2
    return distances


def spread_step(block, owner_of, distance):
    eps, rows, cols = sizes()
    route = []
    for e in range(eps):
        for c in range(cols):
            for other in range(0, rows, 2 * distance):
                source = owner_of(e, c) ^ other
                route.append((flat(e, source, c), flat(e, source ^ distance, c)))
    return lax.ppermute(block, AXES, route)


def gather_panel(note):
    eps, rows, cols = sizes()
    row = lax.axis_index("row")
    for distance in doubling(rows, 2):
        came = spread_step(note, lambda e, c: 0, distance)
        note = jnp.where((row & (2 * distance - 1)) == distance, came, note)
    steps = [(0, 0)]
    hops = [(d, 0) for d in doubling(eps, 1)] + [(0, d) for d in reversed(doubling(cols, 1))]
    for de, dc in hops:
        route = [
            (flat(e, r, c), flat(e ^ de, r, c ^ dc))
            for e in range(eps)
            for r in range(0, rows, 2)
            for c in range(cols)
        ]
        note = jnp.concatenate([note, lax.ppermute(note, AXES, route)])
        steps += [(e ^ de, c ^ dc) for e, c in steps]
    came = lax.ppermute(note, "row", [(r, r + 1) for r in range(0, rows, 2)])
    ep, col = lax.axis_index("ep"), lax.axis_index("col")
    return note, came, [(ep ^ de) * cols + (col ^ dc) for de, dc in steps]


def on_device(design, taps, tap_count, order, regular):
    rows_dev = design.shape[1]
    eps, rows, cols = sizes()
    cols_dev = regular.shape[0] // (eps * cols)
    parts = rows_dev // cols_dev
    row, ep, col = (lax.axis_index(axis) for axis in ("row", "ep", "col"))
    group = lax.axis_index(("ep", "col"))
    everywhere = [(e, r, c) for e in range(eps) for r in range(rows) for c in range(cols)]
    owner = lambda e, c: (e * cols + c) * cols_dev // rows_dev
    home = lambda r: r * parts // cols
    inside = lambda r, c: c // parts == (r * parts % cols) // parts
    first_owner = group * cols_dev // rows_dev
    takes = ((row ^ first_owner) & 1) == 1
    is_inside = inside(row, col)
    owns = is_inside & (home(row) == ep)
    back = [(col - n) % cols for n in range(cols)]
    place = [row, group, ep, col, takes, is_inside, owns, *back]
    chain = len(place)
    steps = [(0, 0)]
    for de, dc in [(d, 0) for d in doubling(eps, 1)] + [(0, d) for d in reversed(doubling(cols, 1))]:
        steps += [(e ^ de, c ^ dc) for e, c in steps]
    place += [(ep ^ de) * cols + (col ^ dc) for de, dc in steps]
    place = jnp.stack([jnp.asarray(p, jnp.int32) for p in place])

    *local, note = permute_local(place, design, order, tap_count, cols_dev)
    notes, came, _ = gather_panel(note)

    def shift(block, n, wanted):
        route = [
            (flat(e, r, (c - n) % cols), flat(e, r, c)) for e, r, c in everywhere if wanted(r, c)
        ]
        return lax.ppermute(block, AXES, route)

    def across(block, wanted):
        route = [(flat(1 - e, r, c), flat(e, r, c)) for e, r, c in everywhere if wanted(e, r, c)]
        return lax.ppermute(block, AXES, route)

    def spread(block):
        distances = doubling(rows, 1)
        for distance in distances[:-1]:
            got = spread_step(block, owner, distance)
            hit = ((row ^ first_owner) & (2 * distance - 1)) == distance
            block = jnp.where(hit, got, block)
        return block, spread_step(block, owner, distances[-1])

    early = [shift(local[n % parts], n, inside) for n in range(1, cols)]
    mine_right, local = assemble(place, [local[0], *early], None, None, local)
    theirs_right = across(mine_right, lambda e, r, c: inside(r, c) and home(r) == e)
    own_block, own_came = spread(mine_right)
    other_block, other_came = spread(theirs_right)
    late = [shift(local[n % parts], n, lambda r, c: not inside(r, c)) for n in range(1, cols)]

    band, aug = start_panel(place, chain, taps, notes, came, regular, mine_right)
    first, local = assemble(
        place, [local[0], *early], [local[0], *late], PLACE_INSIDE, local, [aug]
    )
    mine = [first]
    others = [across(first, lambda e, r, c: not (inside(r, c) and home(r) == e))]
    late = [
        [shift(local[(n + j) % parts], n, lambda r, c: True) for n in range(1, cols)]
        for j in range(1, parts)
    ]
    panels = HEAD // BLOCK
    for kb in range(1, panels - 1):
        aug = next_panel(kb, aug, first if kb == 1 else other_block)
    factor, w, high, low = last_panel(panels - 1, aug, other_block)
    for j in range(1, parts):
        got, _ = assemble(place, [local[j], *late[j - 1]], None, None, (), [factor])
        mine.append(got)
        others.append(across(got, lambda e, r, c: True))
    shards = (own_block, own_came, other_block, other_came)
    right = project(place, shards, band, w, high, low, mine[-1])
    out = None
    for j in range(parts):
        out = multiply_part(
            j, parts, place, mine[j], others[j], theirs_right, band, right, factor, regular, out
        )
    return out


def solution(mesh):
    in_specs = (P(("ep", "col"), "row"), P(), P(("ep", "col")), P("row"), P())
    out_specs = P("row", ("ep", "col"))
    return jax.shard_map(
        on_device, mesh=mesh, in_specs=in_specs, out_specs=out_specs, check_vma=False
    )
```

```python
import functools

import jax
import jax.numpy as jnp
from jax import lax
from jax.experimental import pallas as pl
from jax.experimental.pallas import tpu as pltpu
from jax.sharding import PartitionSpec as P

PANEL = 256
SECTIONS = 2
HEAD = PANEL * SECTIONS
PB = 128
LANES = 128
BLOCK = 128
HALF = 256
SUB = 8
NOTE = 16
EXACT = lax.Precision.HIGHEST
F32 = jnp.float32
BF16 = jnp.bfloat16


def iota(shape, axis):
    return lax.broadcasted_iota(jnp.int32, shape, axis)


def dot(left, right, contract=((1,), (0,)), precision=None):
    return lax.dot_general(
        left, right, (contract, ((), ())), preferred_element_type=F32, precision=precision
    )


NT = ((1,), (1,))
TN = ((0,), (0,))
VMEM = pl.BlockSpec(memory_space=pltpu.VMEM)
SMEM = pl.BlockSpec(memory_space=pltpu.SMEM)
ANY = pl.BlockSpec(memory_space=pl.ANY)
FREE = pl.CostEstimate(flops=0, bytes_accessed=0, transcendentals=0)
LIMIT = pltpu.CompilerParams(vmem_limit_bytes=48 << 20)


def permute_kernel(place_ref, order_ref, counts_ref, design_ref, *out_refs):
    *part_refs, both_ref, note_ref = out_refs
    epochs = design_ref.shape[0]
    parts, per_part = len(part_refs), part_refs[0].shape[0]
    lane = iota((PB, PB), 1).astype(F32)
    none = jnp.zeros((epochs, PB), BF16)
    groups = 2 * HALF // PB

    def packed(local, columns, block, part):
        first = block * groups + part
        second = first + HALF // PB
        pick = [jnp.where(local[:, g : g + 1] == lane, 1.0, 0.0) for g in (first, second)]
        pick = jnp.concatenate(pick, axis=1).astype(BF16)
        top = jnp.concatenate([columns(first), none], axis=1)
        low = jnp.concatenate([none, columns(second)], axis=1)
        return dot(pick, jnp.concatenate([top, low], axis=0), NT).astype(BF16)

    def order_of(rows):
        return (order_ref[rows, :] & (PB - 1)).astype(F32).T

    local = order_of(slice(0, per_part * groups))
    for part in range(HALF // PB):
        columns = lambda g: design_ref[:, g * PB : (g + 1) * PB]
        note_ref[0, part * PB : (part + 1) * PB, :] = packed(local, columns, 0, part)
    counts = counts_ref[...].astype(F32)
    counts = jnp.concatenate([counts] * (LANES // epochs), axis=1)
    note_ref[0, HALF:, :] = jnp.broadcast_to(counts, (NOTE, LANES)).astype(BF16)
    for j in range(parts):
        piece = lax.rem(place_ref[PLACE_COL] + j, parts)
        at = pl.multiple_of(piece * per_part * groups, per_part * groups)
        local = order_of(pl.ds(at, per_part * groups))
        columns = lambda g: design_ref[:, pl.ds(pl.multiple_of((at + g) * PB, PB), PB)]
        for block in range(per_part):
            for part in range(HALF // PB):
                rows = slice(part * PB, (part + 1) * PB)
                part_refs[j][block, rows, :] = packed(local, columns, block, part)
        both_ref[j] = part_refs[j][...]


def permute_local(place, design, order, tap_count, cols_dev):
    epochs, rows = design.shape
    parts, per_part = rows // cols_dev, cols_dev // (2 * HALF)
    piece = jax.ShapeDtypeStruct((per_part, HALF, LANES), BF16)
    both = jax.ShapeDtypeStruct((parts,) + piece.shape, BF16)
    note = jax.ShapeDtypeStruct((1, HALF + NOTE, LANES), BF16)
    return pl.pallas_call(
        permute_kernel,
        out_shape=(piece,) * parts + (both, note),
        in_specs=[SMEM] + [VMEM] * 3,
        out_specs=(VMEM,) * (parts + 2),
        compiler_params=LIMIT,
        name="permute_local",
    )(place, order.reshape(rows // PB, PB), tap_count.reshape(1, epochs), design)


PLACE_ROW, PLACE_GROUP, PLACE_EP, PLACE_COL, PLACE_TAKES, PLACE_OWNS, PLACE_BACK = range(7)


def assemble_kernel(count, gated, after, whole, place_ref, *refs):
    shards, kept = refs[:count], refs[count : count + gated]
    out_refs, sem = refs[count + gated + after : -1], refs[-1]
    copies = [(shard, out_refs[0].at[n]) for n, shard in enumerate(shards)]
    if whole:
        copies += [(shard, out_refs[-1].at[n]) for n, shard in enumerate([kept[0], *shards])]
    copies = [pltpu.make_async_copy(a, b, sem.at[n]) for n, (a, b) in enumerate(copies)]
    for copy in copies:
        copy.start()
    for copy in copies:
        copy.wait()


def assemble(place, shards, gated, after, whole):
    count = len(shards)
    out_shape = [jax.ShapeDtypeStruct((count,) + shards[0].shape, BF16)]
    out_shape += [jax.ShapeDtypeStruct(g.shape, g.dtype) for g in gated]
    if whole:
        out_shape.append(jax.ShapeDtypeStruct((count + 1,) + shards[0].shape, BF16))
    return pl.pallas_call(
        functools.partial(assemble_kernel, count, len(gated), len(after), whole),
        out_shape=out_shape,
        in_specs=[SMEM] + [ANY] * (count + len(gated) + len(after)),
        out_specs=[ANY] * len(out_shape),
        input_output_aliases={1 + count + n: 1 + n for n in range(len(gated))},
        scratch_shapes=[pltpu.SemaphoreType.DMA((2 * count + 1,))],
        compiler_params=LIMIT,
        cost_estimate=FREE,
        name="assemble",
    )(place, *shards, *gated, *after)


def gate(arrays, after):
    count = len(arrays)
    return pl.pallas_call(
        lambda *refs: None,
        out_shape=tuple(jax.ShapeDtypeStruct(x.shape, x.dtype) for x in arrays),
        in_specs=[ANY] * (count + 1),
        out_specs=(ANY,) * count,
        input_output_aliases={n: n for n in range(count)},
        compiler_params=LIMIT,
        cost_estimate=FREE,
        name="gate",
    )(*arrays, after)


def filter_rows(blocks, band_ref, store):
    per = HALF // (LANES // 2)
    for b in range(band_ref.shape[0]):
        first = max(b * per - 1, 0)
        skip = 0 if b else LANES
        packed = jnp.concatenate([blocks(e) for e in range(first, (b + 1) * per)], axis=1)
        for half in range(2):
            got = dot(packed, band_ref[b, half, skip:, :]).astype(BF16)
            store(slice(half * HALF, (half + 1) * HALF), slice(b * HALF, (b + 1) * HALF), got)


def spread(tile, lane):
    return jnp.broadcast_to(tile[:, lane : lane + 1], (SUB, tile.shape[1]))


def row_of(tile, k):
    return jnp.broadcast_to(tile[k : k + 1, :], (SUB, tile.shape[1]))


def factor_block(work):
    groups = BLOCK // SUB
    sub, lane = iota((SUB, BLOCK), 0), iota((SUB, BLOCK), 1)
    tiles = [work[g * SUB : (g + 1) * SUB, :] for g in range(groups)]
    for g in range(groups):
        inside = (lane >= g * SUB) & (lane < (g + 1) * SUB)
        cols = [spread(tiles[g], g * SUB + j) for j in range(SUB)]
        a = {(i, j): row_of(cols[j], i) for j in range(SUB) for i in range(j, SUB)}
        own = jnp.where(inside, jnp.where(lane - g * SUB == sub, 1.0, 0.0), tiles[g])
        u = [row_of(own, k) for k in range(SUB)]
        inv = []
        low = {}
        for k in range(SUB):
            r = lax.rsqrt(a[k, k])
            inv.append(r)
            for i in range(k + 1, SUB):
                low[i, k] = a[i, k] * r
            for j in range(k + 1, SUB):
                for i in range(j, SUB):
                    a[i, j] = a[i, j] - low[i, k] * low[j, k]
            u[k] = u[k] * r
            for j in range(k + 1, SUB):
                u[j] = u[j] - low[j, k] * u[k]
        for t in range(g + 1, groups):
            left = [spread(tiles[t], g * SUB + j) for j in range(SUB)]
            tile = jnp.where(inside, 0.0, tiles[t])
            for k in range(SUB):
                left[k] = left[k] * inv[k]
                for j in range(k + 1, SUB):
                    left[j] = left[j] - low[j, k] * left[k]
                tile = tile - left[k] * u[k]
            tiles[t] = tile
        merged = u[0]
        for k in range(1, SUB):
            merged = jnp.where(sub == k, u[k], merged)
        work[g * SUB : (g + 1) * SUB, :] = jnp.where(lane < (g + 1) * SUB, merged, 0.0)


def start_kernel(
    chain, place_ref, taps_ref, own_ref, came_ref, reg_ref, after, band_ref, aug_ref, notes, a1, work
):
    del after
    epochs = aug_ref.shape[1] - HEAD
    half = LANES // 2

    @pl.when(place_ref[0] % 2 == 0)
    def _():
        for rel in range(own_ref.shape[0]):
            notes[place_ref[chain + rel]] = own_ref[rel]

    @pl.when(place_ref[0] % 2 == 1)
    def _():
        for rel in range(own_ref.shape[0]):
            notes[place_ref[chain + rel]] = came_ref[rel]

    shape = (half, LANES)
    lag = iota(shape, 1) - iota(shape, 0)
    base = lax.fori_loop(
        0,
        taps_ref.shape[0],
        lambda k, kept: jnp.where(lag == k, taps_ref[k], kept),
        jnp.zeros(shape, F32),
    )
    lane = iota(shape, 1)
    swapped = jnp.concatenate([base[:, half:], base[:, :half]], axis=1)
    early = jnp.where(lane < half, swapped, 0.0)
    late = jnp.where(lane >= half, swapped, 0.0)
    none = jnp.zeros(shape, F32)
    patterns = [(early, none), (base, none), (late, early), (none, base), (none, late)]
    row = iota((1, LANES), 1)
    band_ref[...] = jnp.zeros_like(band_ref)
    for b in range(epochs // HALF):
        for side in range(HALF // LANES):
            e = (b * HALF + side * LANES) // half
            counts = [notes[e + n, HALF : HALF + NOTE, :].astype(F32)[:1] for n in range(2)]
            counts = jnp.where(row < half, counts[0], counts[1])
            for j, pattern in enumerate(patterns):
                at = (lag + side * LANES + half - half * j).astype(F32)
                kept = jnp.where(at < counts, pattern[side], 0.0).astype(BF16)
                for h in range(2):
                    rows = slice(j * LANES + h * half, j * LANES + (h + 1) * half)
                    band_ref[b, h, rows, side * LANES : (side + 1) * LANES] = kept

    def store(rows, cols, got):
        a1[rows, cols] = got

    filter_rows(lambda e: notes[e, :HALF, :], band_ref, store)
    columns = a1[...]
    square = (HEAD, HEAD)
    on_diagonal = iota(square, 0) == iota(square, 1)
    aug_ref[:, :HEAD] = dot(columns, columns, NT) + jnp.where(on_diagonal, reg_ref[:, :HEAD], 0.0)
    aug_ref[:, HEAD:] = columns.astype(F32)
    eliminate(aug_ref, 0, work)


def eliminate(aug, kb, work):
    here = slice(kb * BLOCK, (kb + 1) * BLOCK)
    work[...] = aug[here, here]
    factor_block(work)
    rest = slice(kb * BLOCK, aug.shape[1])
    aug[here, rest] = dot(work[...], aug[here, rest], precision=EXACT)
    for rb in range(kb + 1, HEAD // BLOCK):
        below = slice(rb * BLOCK, (rb + 1) * BLOCK)
        rest = slice(rb * BLOCK, aug.shape[1])
        aug[below, rest] -= dot(aug[here, below], aug[here, rest], TN, precision=EXACT)


def next_kernel(kb, aug_in, after, aug_ref, work):
    del after
    aug_ref[...] = aug_in[...]
    eliminate(aug_ref, kb, work)


def last_kernel(kb, aug_in, after, factor_ref, w_ref, high_ref, low_ref, aug, work):
    del after
    aug[...] = aug_in[...]
    eliminate(aug, kb, work)
    square = (HEAD, HEAD)
    epochs = aug.shape[1] - HEAD
    factor_ref[...] = jnp.where(iota(square, 0) >= iota(square, 1), aug[:, :HEAD].T, 0.0)
    wt = aug[:, HEAD:]
    w_ref[...] = wt.T.astype(BF16)
    for b in range(epochs // BLOCK):
        here = slice(b * BLOCK, (b + 1) * BLOCK)
        shape = (BLOCK, epochs)
        unit = jnp.where(iota(shape, 0) + b * BLOCK == iota(shape, 1), 1.0, 0.0)
        middle = unit - dot(wt[:, here], wt, TN, precision=EXACT)
        high = middle.astype(BF16)
        high_ref[here, :] = high
        low_ref[here, :] = (middle - high.astype(F32)).astype(BF16)


def start_panel(place, chain, taps, own, came, regular, after):
    epochs = own.shape[0] * (LANES // 2)
    per = HALF // (LANES // 2)
    return pl.pallas_call(
        functools.partial(start_kernel, chain),
        out_shape=(
            jax.ShapeDtypeStruct((epochs // HALF, 2, (per + 1) * LANES, HALF), BF16),
            jax.ShapeDtypeStruct((HEAD, HEAD + epochs), F32),
        ),
        in_specs=[SMEM, SMEM, VMEM, VMEM, VMEM, ANY],
        out_specs=(VMEM, VMEM),
        scratch_shapes=[
            pltpu.VMEM(own.shape, BF16),
            pltpu.VMEM((HEAD, epochs), BF16),
            pltpu.VMEM((BLOCK, BLOCK), F32),
        ],
        compiler_params=LIMIT,
        cost_estimate=FREE,
        name="start_panel",
    )(place, taps, own, came, regular.reshape(1, -1), after)


def next_panel(kb, aug, after):
    return pl.pallas_call(
        functools.partial(next_kernel, kb),
        out_shape=jax.ShapeDtypeStruct(aug.shape, F32),
        in_specs=[VMEM, ANY],
        out_specs=VMEM,
        scratch_shapes=[pltpu.VMEM((BLOCK, BLOCK), F32)],
        compiler_params=LIMIT,
        cost_estimate=FREE,
        name="next_panel",
    )(aug, after)


def last_panel(kb, aug, after):
    epochs = aug.shape[1] - HEAD
    return pl.pallas_call(
        functools.partial(last_kernel, kb),
        out_shape=(
            jax.ShapeDtypeStruct((HEAD, HEAD), F32),
            jax.ShapeDtypeStruct((epochs, HEAD), BF16),
            jax.ShapeDtypeStruct((epochs, epochs), BF16),
            jax.ShapeDtypeStruct((epochs, epochs), BF16),
        ),
        in_specs=[VMEM, ANY],
        out_specs=(VMEM,) * 4,
        scratch_shapes=[pltpu.VMEM(aug.shape, F32), pltpu.VMEM((BLOCK, BLOCK), F32)],
        compiler_params=LIMIT,
        cost_estimate=FREE,
        name="last_panel",
    )(aug, after)


def whole_shards(ref):
    return [ref.at[n, 0] for n in range(ref.shape[0])]


def split_shards(first, rest):
    return [first, *whole_shards(rest)]


def unpack(place_ref, own, other, blocks):
    width = len(own)
    here = place_ref[PLACE_EP] * width
    there = width - here
    for n in range(width):
        back = place_ref[PLACE_BACK + n]
        blocks[here + back] = own[n][...]
        blocks[there + back] = other[n][...]


def choose(condition, yes, no):
    pl.when(condition)(yes)
    pl.when(jnp.logical_not(condition))(no)


def fixed(array):
    return pl.BlockSpec(
        array.shape, lambda n, i, place: (0,) * array.ndim, pipeline_mode=pl.Buffered(1)
    )


def tile_kernel(
    part, parts, place_ref, own_first, own_rest, other_first, other_rest, band_ref, factor_ref, reg_ref,
    *refs,
):
    if part == 0:
        theirs_ref, *right_refs, w_ref, high_ref, low_ref = refs[:8]
        out_ref, right_ref, blocks, filtered, columns = refs[8:]
    else:
        right_ref, _, out_ref, blocks, filtered = refs
    n, i = pl.program_id(0), pl.program_id(1)
    rows, wide = out_ref.shape
    steps = pl.num_programs(1)
    block = lax.rem(place_ref[PLACE_COL] + part, parts) * steps + i
    first_row = (place_ref[PLACE_ROW] * parts * steps + block) * rows
    first_col = (place_ref[PLACE_GROUP] * pl.num_programs(0) + n) * wide
    at = pl.multiple_of(i * rows, rows)

    if part == 0:

        @pl.when(i == 0)
        def _():
            def store(rows, cols, got):
                columns[rows, cols] = got

            own, own_came, other, other_came = right_refs
            choose(
                place_ref[PLACE_TAKES] != 0,
                lambda: unpack(place_ref, whole_shards(own_came), whole_shards(other_came), blocks),
                lambda: unpack(place_ref, whole_shards(own), whole_shards(other), blocks),
            )
            filter_rows(lambda e: blocks[e], band_ref, store)
            wanted = columns[...]
            projected = dot(high_ref[...], wanted, NT) + dot(low_ref[...], wanted, NT)
            right_ref[...] = projected.astype(BF16)

            @pl.when(first_col == 0)
            def _():
                right_ref[...] = w_ref[...]

    @pl.when(n == 0)
    def _():
        def store(rows, cols, got):
            filtered[pl.ds(at + rows.start, HALF), cols] = got

        own = split_shards(own_first.at[0], own_rest)
        other = split_shards(other_first.at[0, 0], other_rest)
        if part == 0:
            choose(
                place_ref[PLACE_OWNS] != 0,
                lambda: unpack(place_ref, own, whole_shards(theirs_ref), blocks),
                lambda: unpack(place_ref, own, other, blocks),
            )
        else:
            unpack(place_ref, own, other, blocks)
        filter_rows(lambda e: blocks[e], band_ref, store)

    @pl.when(first_row >= HEAD)
    def _():
        out_ref[...] = dot(filtered[pl.ds(at, rows), :], right_ref[...])

        @pl.when(first_row == first_col)
        def _():
            on_diagonal = iota((rows, wide), 0) == iota((rows, wide), 1)
            out_ref[...] += jnp.where(on_diagonal, reg_ref[...], 0.0)

    @pl.when(first_row < HEAD)
    def _():
        out_ref[...] = jnp.zeros_like(out_ref)

        @pl.when(first_col == 0)
        def _():
            out_ref[...] = factor_ref[...]


def multiply_part(part, parts, place, own, other, band, factor, regular, extra, out, right):
    steps = own[0].shape[0]
    rows = wide = 2 * HALF
    epochs = band.shape[0] * HALF
    cols = steps * wide

    def row_block(i, place):
        return lax.rem(place[PLACE_COL] + part, parts) * steps + i

    def reg_block(n, i, place):
        return 0, place[PLACE_ROW] * parts * steps + row_block(i, place)

    def left_block(n, i, place):
        return 0, jnp.where(n == 0, i, steps - 1), 0, 0

    def own_block(n, i, place):
        return left_block(n, i, place)[1:]

    def other_block(n, i, place):
        return part, *left_block(n, i, place)[1:]

    def right_block(took):
        return lambda n, i, place: (0, jnp.where(place[PLACE_TAKES] == took, n, 0), 0, 0)

    def shards_spec(array, index):
        return pl.BlockSpec((array.shape[0], 1, HALF, LANES), index)

    out_shape = [jax.ShapeDtypeStruct((parts * steps * rows, cols), F32)]
    out_specs = [pl.BlockSpec((rows, wide), lambda n, i, place: (row_block(i, place), n))]
    right_spec = pl.BlockSpec((epochs, wide), lambda n, i, place: (0, n))
    scratch = [
        pltpu.VMEM((epochs // (LANES // 2), HALF, LANES), BF16),
        pltpu.VMEM((steps * rows, epochs), BF16),
    ]
    operands = [*own, *other, band, factor, regular.reshape(1, -1)]
    in_specs = [pl.BlockSpec((1, HALF, LANES), own_block), shards_spec(own[1], left_block)]
    in_specs += [pl.BlockSpec((1, 1, HALF, LANES), other_block), shards_spec(other[1], left_block)]
    in_specs += [fixed(band), fixed(factor)]
    in_specs += [pl.BlockSpec((1, rows), reg_block)]
    if part == 0:
        operands += extra
        in_specs += [shards_spec(extra[0], left_block)]
        in_specs += [shards_spec(extra[0], right_block(took)) for took in (0, 1, 0, 1)]
        in_specs += [fixed(array) for array in extra[5:]]
        out_shape.append(jax.ShapeDtypeStruct((epochs, cols), BF16))
        out_specs.append(right_spec)
        scratch.append(pltpu.VMEM((wide, epochs), BF16))
    else:
        operands += [right, out]
        in_specs += [right_spec, ANY]
    return pl.pallas_call(
        functools.partial(tile_kernel, part, parts),
        out_shape=out_shape,
        grid_spec=pltpu.PrefetchScalarGridSpec(
            num_scalar_prefetch=1,
            grid=(cols // wide, steps),
            in_specs=in_specs,
            out_specs=out_specs,
            scratch_shapes=scratch,
        ),
        input_output_aliases={len(operands): 0} if part else {},
        compiler_params=pltpu.CompilerParams(vmem_limit_bytes=48 << 20),
        cost_estimate=FREE,
        name="multiply_part",
    )(place, *operands)


AXES = ("ep", "row", "col")


def sizes():
    return tuple(lax.axis_size(axis) for axis in AXES)


def flat(ep, row, col):
    _, rows, cols = sizes()
    return (ep * rows + row) * cols + col


def doubling(count, least):
    distances = []
    distance = count // 2
    while distance >= least:
        distances.append(distance)
        distance //= 2
    return distances


def spread_step(block, owner_of, distance):
    eps, rows, cols = sizes()
    route = []
    for e in range(eps):
        for c in range(cols):
            for other in range(0, rows, 2 * distance):
                source = owner_of(e, c) ^ other
                route.append((flat(e, source, c), flat(e, source ^ distance, c)))
    return lax.ppermute(block, AXES, route)


def panel_hops():
    eps, _, cols = sizes()
    return [(d, 0) for d in doubling(eps, 1)] + [(0, d) for d in reversed(doubling(cols, 1))]


def gather_panel(note):
    eps, rows, cols = sizes()
    row = lax.axis_index("row")
    for distance in doubling(rows, 2):
        came = spread_step(note, lambda e, c: 0, distance)
        note = jnp.where((row & (2 * distance - 1)) == distance, came, note)
    for de, dc in panel_hops():
        route = [
            (flat(e, r, c), flat(e ^ de, r, c ^ dc))
            for e in range(eps)
            for r in range(0, rows, 2)
            for c in range(cols)
        ]
        note = jnp.concatenate([note, lax.ppermute(note, AXES, route)])
    came = lax.ppermute(note, "row", [(r, r + 1) for r in range(0, rows, 2)])
    return note, came


def on_device(design, taps, tap_count, order, regular):
    rows_dev = design.shape[1]
    eps, rows, cols = sizes()
    cols_dev = regular.shape[0] // (eps * cols)
    parts = rows_dev // cols_dev
    row, ep, col = (lax.axis_index(axis) for axis in ("row", "ep", "col"))
    group = lax.axis_index(("ep", "col"))
    everywhere = [(e, r, c) for e in range(eps) for r in range(rows) for c in range(cols)]
    owner = lambda e, c: (e * cols + c) * cols_dev // rows_dev
    owns = lambda e, r, c: (c // parts == (r * parts % cols) // parts) & (r * parts // cols == e)
    first_owner = group * cols_dev // rows_dev
    takes = ((row ^ first_owner) & 1) == 1
    back = [(col - n) % cols for n in range(cols)]
    place = [row, group, ep, col, takes, owns(ep, row, col), *back]
    chain = len(place)
    steps = [(0, 0)]
    for de, dc in panel_hops():
        steps += [(e ^ de, c ^ dc) for e, c in steps]
    place += [(ep ^ de) * cols + (col ^ dc) for de, dc in steps]
    place = jnp.stack([jnp.asarray(p, jnp.int32) for p in place])

    *local, both, note = permute_local(place, design, order, tap_count, cols_dev)

    def shift(block, n):
        route = [(flat(e, r, (c - n) % cols), flat(e, r, c)) for e, r, c in everywhere]
        return lax.ppermute(block, AXES, route)

    def across(block, wanted):
        route = [(flat(1 - e, r, c), flat(e, r, c)) for e, r, c in everywhere if wanted(e, r, c)]
        return lax.ppermute(block, AXES, route)

    distances = doubling(rows, 1)

    def spread_rest(block, got):
        for n, distance in enumerate(distances[1:]):
            hit = ((row ^ first_owner) & (4 * distance - 1)) == 2 * distance
            block = jnp.where(hit, got, block)
            got = spread_step(block, owner, distance)
        return block, got

    anyone = lambda e, r, c: True
    early = [shift(local[n % parts], n) for n in range(1, cols)]
    swapped = across(both, anyone)
    notes, came = lax.cond(
        tap_count[0] > 0,
        gather_panel,
        lambda note: (jnp.zeros((eps * cols,) + note.shape[1:], BF16),) * 2,
        note,
    )
    rest, *local, first = assemble(place, early, local, [notes, swapped], True)
    theirs = across(first, owns)
    own_got = spread_step(first, owner, distances[0])
    others = [across(rest, lambda e, r, c: not owns(e, r, c))]
    mine = [rest]
    late = [
        [shift(local[(n + j) % parts], n) for n in range(1, cols)] for j in range(1, parts)
    ]
    band, aug = start_panel(place, chain, taps, notes, came, regular, first)
    theirs, own_got, *begun = gate([theirs, own_got, *(shards[0] for shards in late)], aug)
    other_got = spread_step(theirs, owner, distances[0])
    own_block, own_came = spread_rest(first, own_got)
    aug = next_panel(1, aug, theirs)
    aug = next_panel(2, aug, theirs)
    flat_late = [shard for shards in late for shard in shards[1:]]
    other_got, others[0], *flat_late = gate([other_got, others[0], *flat_late], aug)
    for j in range(1, parts):
        shards = [begun[j - 1], *flat_late[(j - 1) * (cols - 2) : j * (cols - 2)]]
        (got,) = assemble(place, shards, [], [aug], False)
        mine.append(got)
        others.append(across(got, anyone))
    factor, w, high, low = last_panel(3, aug, mine[-1])
    other_block, other_came = spread_rest(theirs, other_got)
    extra = [theirs, own_block, own_came, other_block, other_came, w, high, low]
    mine = [(local[j], mine[j]) for j in range(parts)]
    others = [(swapped, others[j]) for j in range(parts)]
    out, right = multiply_part(
        0, parts, place, mine[0], others[0], band, factor, regular, extra, None, None
    )
    for j in range(1, parts):
        (out,) = multiply_part(
            j, parts, place, mine[j], others[j], band, factor, regular, None, out, right
        )
    return out


def solution(mesh):
    in_specs = (P(("ep", "col"), "row"), P(), P(("ep", "col")), P("row"), P())
    out_specs = P("row", ("ep", "col"))
    return jax.shard_map(
        on_device, mesh=mesh, in_specs=in_specs, out_specs=out_specs, check_vma=False
    )
```

```python
import functools

import jax
import jax.numpy as jnp
from jax import lax
from jax.experimental import pallas as pl
from jax.experimental.pallas import tpu as pltpu
from jax.sharding import PartitionSpec as P

PANEL = 256
SECTIONS = 2
HEAD = PANEL * SECTIONS
PB = 128
LANES = 128
BLOCK = 128
HALF = 256
SUB = 8
NOTE = 16
EXACT = lax.Precision.HIGHEST
F32 = jnp.float32
BF16 = jnp.bfloat16


def iota(shape, axis):
    return lax.broadcasted_iota(jnp.int32, shape, axis)


def dot(left, right, contract=((1,), (0,)), precision=None):
    return lax.dot_general(
        left, right, (contract, ((), ())), preferred_element_type=F32, precision=precision
    )


NT = ((1,), (1,))
TN = ((0,), (0,))
VMEM = pl.BlockSpec(memory_space=pltpu.VMEM)
SMEM = pl.BlockSpec(memory_space=pltpu.SMEM)
ANY = pl.BlockSpec(memory_space=pl.ANY)
FREE = pl.CostEstimate(flops=0, bytes_accessed=0, transcendentals=0)
LIMIT = pltpu.CompilerParams(vmem_limit_bytes=48 << 20)


def permute_kernel(place_ref, *refs):
    sources, refs = refs[:3], refs[3:]
    all_ref, note_ref = refs[:-4]
    order_ref, counts_ref, design_ref = targets = refs[-4:-1]
    copies = [
        pltpu.make_async_copy(source, target, refs[-1].at[n])
        for n, (source, target) in enumerate(zip(sources, targets))
    ]
    for copy in copies:
        copy.start()
    for copy in copies:
        copy.wait()
    epochs = design_ref.shape[0]
    parts, per_part = all_ref.shape[:2]
    lane = iota((PB, PB), 1).astype(F32)
    none = jnp.zeros((epochs, PB), BF16)
    groups = 2 * HALF // PB

    def packed(local, columns, block, part):
        first = block * groups + part
        second = first + HALF // PB
        pick = [jnp.where(local[:, g : g + 1] == lane, 1.0, 0.0) for g in (first, second)]
        pick = jnp.concatenate(pick, axis=1).astype(BF16)
        top = jnp.concatenate([columns(first), none], axis=1)
        low = jnp.concatenate([none, columns(second)], axis=1)
        return dot(pick, jnp.concatenate([top, low], axis=0), NT).astype(BF16)

    def order_of(rows):
        return (order_ref[rows, :] & (PB - 1)).astype(F32).T

    local = order_of(slice(0, per_part * groups))
    for part in range(HALF // PB):
        columns = lambda g: design_ref[:, g * PB : (g + 1) * PB]
        note_ref[0, part * PB : (part + 1) * PB, :] = packed(local, columns, 0, part)
    counts = counts_ref[...].astype(F32)
    counts = jnp.concatenate([counts] * (LANES // epochs), axis=1)
    note_ref[0, HALF:, :] = jnp.broadcast_to(counts, (NOTE, LANES)).astype(BF16)
    for j in range(parts):
        at = j * per_part * groups
        local = order_of(slice(at, at + per_part * groups))
        columns = lambda g: design_ref[:, (at + g) * PB : (at + g + 1) * PB]
        for block in range(per_part):
            for part in range(HALF // PB):
                rows = slice(part * PB, (part + 1) * PB)
                all_ref[j, block, rows, :] = packed(local, columns, block, part)


def permute_local(place, design, order, tap_count, cols_dev):
    epochs, rows = design.shape
    parts, per_part = rows // cols_dev, cols_dev // (2 * HALF)
    piece = jax.ShapeDtypeStruct((parts, per_part, HALF, LANES), BF16)
    note = jax.ShapeDtypeStruct((1, HALF + NOTE, LANES), BF16)
    return pl.pallas_call(
        permute_kernel,
        out_shape=(piece, note),
        in_specs=[SMEM] + [ANY] * 3,
        out_specs=(VMEM,) * 2,
        scratch_shapes=[
            pltpu.VMEM((rows // PB, PB), jnp.int32),
            pltpu.VMEM((1, epochs), jnp.int32),
            pltpu.VMEM((epochs, rows), BF16),
            pltpu.SemaphoreType.DMA((3,)),
        ],
        compiler_params=LIMIT,
        name="permute_local",
    )(place, order.reshape(rows // PB, PB), tap_count.reshape(1, epochs), design)


PLACE_ROW, PLACE_GROUP, PLACE_EP, PLACE_COL, PLACE_TAKES = range(5)


def separate_kernel(place_ref, all_ref, after, *refs):
    del after
    *part_refs, wanted_ref, sem = refs
    parts = len(part_refs)
    copies = [
        pltpu.make_async_copy(all_ref.at[n, j], part_refs[j].at[n], sem.at[n, j])
        for j in range(parts)
        for n in range(all_ref.shape[0])
    ]
    for copy in copies:
        copy.start()
    for j in range(parts):

        @pl.when(lax.rem(place_ref[PLACE_COL], parts) == j)
        def _():
            again = [
                pltpu.make_async_copy(all_ref.at[n, j], wanted_ref.at[n], sem.at[n, parts])
                for n in range(all_ref.shape[0])
            ]
            for copy in again:
                copy.start()
            for copy in again:
                copy.wait()

    for copy in copies:
        copy.wait()


def separate(place, gathered, after):
    width, parts = gathered.shape[:2]
    part = jax.ShapeDtypeStruct((width,) + gathered.shape[2:], BF16)
    *column, wanted = pl.pallas_call(
        separate_kernel,
        out_shape=(part,) * (parts + 1),
        in_specs=[SMEM, ANY, ANY],
        out_specs=(ANY,) * (parts + 1),
        scratch_shapes=[pltpu.SemaphoreType.DMA((width, parts + 1))],
        compiler_params=LIMIT,
        cost_estimate=FREE,
        name="separate",
    )(place, gathered, after)
    return column, wanted


def gate(arrays, after):
    count = len(arrays)
    return pl.pallas_call(
        lambda *refs: None,
        out_shape=tuple(jax.ShapeDtypeStruct(x.shape, x.dtype) for x in arrays),
        in_specs=[ANY] * (count + 1),
        out_specs=(ANY,) * count,
        input_output_aliases={n: n for n in range(count)},
        compiler_params=LIMIT,
        cost_estimate=FREE,
        name="gate",
    )(*arrays, after)


def filter_rows(blocks, band_ref, store):
    for b in range(band_ref.shape[0]):
        first = max(2 * b - 1, 0)
        skip = 0 if b else LANES
        packed = jnp.concatenate([blocks(e) for e in range(first, 2 * b + 2)], axis=1)
        got = dot(packed, band_ref[b, skip:, :]).astype(BF16)
        for half in range(2):
            across = slice(half * LANES, (half + 1) * LANES)
            store(slice(half * HALF, (half + 1) * HALF), slice(b * LANES, (b + 1) * LANES), got[:, across])


def spread(tile, lane):
    return jnp.broadcast_to(tile[:, lane : lane + 1], (SUB, tile.shape[1]))


def row_of(tile, k):
    return jnp.broadcast_to(tile[k : k + 1, :], (SUB, tile.shape[1]))


def factor_block(work):
    groups = BLOCK // SUB
    sub, lane = iota((SUB, BLOCK), 0), iota((SUB, BLOCK), 1)
    tiles = [work[g * SUB : (g + 1) * SUB, :] for g in range(groups)]
    for g in range(groups):
        inside = (lane >= g * SUB) & (lane < (g + 1) * SUB)
        cols = [spread(tiles[g], g * SUB + j) for j in range(SUB)]
        a = {(i, j): row_of(cols[j], i) for j in range(SUB) for i in range(j, SUB)}
        own = jnp.where(inside, jnp.where(lane - g * SUB == sub, 1.0, 0.0), tiles[g])
        u = [row_of(own, k) for k in range(SUB)]
        inv = []
        low = {}
        for k in range(SUB):
            r = lax.rsqrt(a[k, k])
            inv.append(r)
            for i in range(k + 1, SUB):
                low[i, k] = a[i, k] * r
            for j in range(k + 1, SUB):
                for i in range(j, SUB):
                    a[i, j] = a[i, j] - low[i, k] * low[j, k]
            u[k] = u[k] * r
            for j in range(k + 1, SUB):
                u[j] = u[j] - low[j, k] * u[k]
        for t in range(g + 1, groups):
            left = [spread(tiles[t], g * SUB + j) for j in range(SUB)]
            tile = jnp.where(inside, 0.0, tiles[t])
            for k in range(SUB):
                left[k] = left[k] * inv[k]
                for j in range(k + 1, SUB):
                    left[j] = left[j] - low[j, k] * left[k]
                tile = tile - left[k] * u[k]
            tiles[t] = tile
        merged = u[0]
        for k in range(1, SUB):
            merged = jnp.where(sub == k, u[k], merged)
        work[g * SUB : (g + 1) * SUB, :] = jnp.where(lane < (g + 1) * SUB, merged, 0.0)


def start_kernel(
    chain, place_ref, taps_ref, own_ref, came_ref, reg_ref, band_ref, taper_ref, aug_ref, notes, a1,
    work,
):
    epochs = aug_ref.shape[1] - HEAD
    half = LANES // 2

    @pl.when(place_ref[0] % 2 == 0)
    def _():
        for rel in range(own_ref.shape[0]):
            notes[place_ref[chain + rel]] = own_ref[rel]

    @pl.when(place_ref[0] % 2 == 1)
    def _():
        for rel in range(own_ref.shape[0]):
            notes[place_ref[chain + rel]] = came_ref[rel]

    shape = (half, LANES)
    lag = iota(shape, 1) - iota(shape, 0)
    base = lax.fori_loop(
        0,
        taps_ref.shape[0],
        lambda k, kept: jnp.where(lag == k, taps_ref[k], kept),
        jnp.zeros(shape, F32),
    )
    lane = iota(shape, 1)
    swapped = jnp.concatenate([base[:, half:], base[:, :half]], axis=1)
    patterns = (jnp.where(lane < half, swapped, 0.0), base, jnp.where(lane >= half, swapped, 0.0))
    row = iota((1, LANES), 1)
    sources = epochs // half
    counts = [notes[e, HALF : HALF + NOTE, :].astype(F32)[:1] for e in range(sources)]
    counts.append(jnp.zeros_like(counts[0]))
    band_ref[...] = jnp.zeros_like(band_ref)
    for e in range(sources):
        limit = jnp.where(row < half, counts[e], counts[e + 1])
        taper_ref[e] = jnp.where(lag.astype(F32) < limit, base, 0.0).astype(BF16)
    for b in range(epochs // LANES):
        limit = jnp.where(row < half, counts[2 * b], counts[2 * b + 1])
        for j, pattern in enumerate(patterns):
            at = (lag + half - half * j).astype(F32)
            kept = jnp.where(at < limit, pattern, 0.0).astype(BF16)
            for h in range(2):
                rows = slice(j * LANES + h * half, j * LANES + (h + 1) * half)
                band_ref[b, rows, h * LANES : (h + 1) * LANES] = kept

    def store(rows, cols, got):
        a1[rows, cols] = got

    filter_rows(lambda e: notes[e, :HALF, :], band_ref, store)
    columns = a1[...]
    square = (HEAD, HEAD)
    on_diagonal = iota(square, 0) == iota(square, 1)
    aug_ref[:, :HEAD] = dot(columns, columns, NT) + jnp.where(on_diagonal, reg_ref[:, :HEAD], 0.0)
    aug_ref[:, HEAD:] = columns.astype(F32)
    eliminate(aug_ref, 0, work)


def eliminate(aug, kb, work):
    here = slice(kb * BLOCK, (kb + 1) * BLOCK)
    work[...] = aug[here, here]
    factor_block(work)
    rest = slice(kb * BLOCK, aug.shape[1])
    aug[here, rest] = dot(work[...], aug[here, rest], precision=EXACT)
    for rb in range(kb + 1, HEAD // BLOCK):
        below = slice(rb * BLOCK, (rb + 1) * BLOCK)
        rest = slice(rb * BLOCK, aug.shape[1])
        aug[below, rest] -= dot(aug[here, below], aug[here, rest], TN, precision=EXACT)


def next_kernel(kb, aug_in, after, aug_ref, work):
    del after
    aug_ref[...] = aug_in[...]
    eliminate(aug_ref, kb, work)


def last_kernel(kb, aug_in, after, taper_ref, factor_ref, w_ref, high_ref, low_ref, aug, work, high, low):
    del after
    aug[...] = aug_in[...]
    eliminate(aug, kb, work)
    square = (HEAD, HEAD)
    epochs = aug.shape[1] - HEAD
    factor_ref[...] = jnp.where(iota(square, 0) >= iota(square, 1), aug[:, :HEAD].T, 0.0)
    wt = aug[:, HEAD:]

    def keep(rows, cols, values):
        top = values.astype(BF16)
        high[rows, cols] = top
        low[rows, cols] = (values - top.astype(F32)).astype(BF16)

    keep(slice(None), slice(epochs, None), wt.T)
    for b in range(epochs // BLOCK):
        here = slice(b * BLOCK, (b + 1) * BLOCK)
        shape = (BLOCK, epochs)
        unit = jnp.where(iota(shape, 0) + b * BLOCK == iota(shape, 1), 1.0, 0.0)
        keep(here, slice(0, epochs), unit - dot(wt[:, here], wt, TN, precision=EXACT))
    count, half = taper_ref.shape[:2]
    for e in range(count):
        reach = min(LANES, epochs - e * half)
        rows = slice(e * half, e * half + reach)
        taper = taper_ref[e, :, :reach]
        got = dot(taper, high[rows, :]) + dot(taper, low[rows, :])
        here = slice(e * half, (e + 1) * half)
        w_ref[here, :] = got[:, epochs:].astype(BF16)
        top = got[:, :epochs].astype(BF16)
        high_ref[here, :] = top
        low_ref[here, :] = (got[:, :epochs] - top.astype(F32)).astype(BF16)


def start_panel(place, chain, taps, own, came, regular):
    epochs = own.shape[0] * (LANES // 2)
    half = LANES // 2
    return pl.pallas_call(
        functools.partial(start_kernel, chain),
        out_shape=(
            jax.ShapeDtypeStruct((epochs // LANES, 3 * LANES, 2 * LANES), BF16),
            jax.ShapeDtypeStruct((epochs // half, half, LANES), BF16),
            jax.ShapeDtypeStruct((HEAD, HEAD + epochs), F32),
        ),
        in_specs=[SMEM, SMEM, VMEM, VMEM, VMEM],
        out_specs=(VMEM,) * 3,
        scratch_shapes=[
            pltpu.VMEM(own.shape, BF16),
            pltpu.VMEM((HEAD, epochs), BF16),
            pltpu.VMEM((BLOCK, BLOCK), F32),
        ],
        compiler_params=LIMIT,
        cost_estimate=FREE,
        name="start_panel",
    )(place, taps, own, came, regular.reshape(1, -1))


def next_panel(kb, aug, after):
    return pl.pallas_call(
        functools.partial(next_kernel, kb),
        out_shape=jax.ShapeDtypeStruct(aug.shape, F32),
        in_specs=[VMEM, ANY],
        out_specs=VMEM,
        scratch_shapes=[pltpu.VMEM((BLOCK, BLOCK), F32)],
        compiler_params=LIMIT,
        cost_estimate=FREE,
        name="next_panel",
    )(aug, after)


def last_panel(kb, aug, after, taper):
    epochs = aug.shape[1] - HEAD
    return pl.pallas_call(
        functools.partial(last_kernel, kb),
        out_shape=(
            jax.ShapeDtypeStruct((HEAD, HEAD), F32),
            jax.ShapeDtypeStruct((epochs, HEAD), BF16),
            jax.ShapeDtypeStruct((epochs, epochs), BF16),
            jax.ShapeDtypeStruct((epochs, epochs), BF16),
        ),
        in_specs=[VMEM, ANY, VMEM],
        out_specs=(VMEM,) * 4,
        scratch_shapes=[
            pltpu.VMEM(aug.shape, F32),
            pltpu.VMEM((BLOCK, BLOCK), F32),
            pltpu.VMEM((epochs, epochs + HEAD), BF16),
            pltpu.VMEM((epochs, epochs + HEAD), BF16),
        ],
        compiler_params=LIMIT,
        cost_estimate=FREE,
        name="last_panel",
    )(aug, after, taper)


def shards_of(ref, block):
    return [ref.at[n, block] for n in range(ref.shape[0])]


def unpack(place_ref, own, other, blocks):
    width = len(own)
    here = place_ref[PLACE_EP] * width
    there = width - here
    for n in range(width):
        blocks[here + n] = own[n][...]
        blocks[there + n] = other[n][...]


def choose(condition, yes, no):
    pl.when(condition)(yes)
    pl.when(jnp.logical_not(condition))(no)


def fixed(array):
    return pl.BlockSpec(
        array.shape, lambda i, place: (0,) * array.ndim, pipeline_mode=pl.Buffered(1)
    )


def tile_kernel(part, parts, place_ref, left_ref, *refs):
    if part == 0:
        own, own_came, other, other_came, w_ref, high_ref, low_ref, band_ref = refs[:8]
        factor_ref, reg_ref, out_ref, right_ref, lhs, columns, blocks = refs[8:]
    else:
        right_ref, _, factor_ref, reg_ref, out_ref, lhs = refs
    i, steps = pl.program_id(0), pl.num_programs(0)
    rows, cols = out_ref.shape
    half = LANES // 2
    block = part * steps + i
    first_row = (place_ref[PLACE_ROW] * parts * steps + block) * rows
    first_col = place_ref[PLACE_GROUP] * cols

    if part == 0:

        @pl.when(i == 0)
        def _():
            def store(rows, cols, got):
                columns[rows, cols] = got

            for n in range(cols // rows):
                choose(
                    place_ref[PLACE_TAKES] != 0,
                    lambda: unpack(place_ref, shards_of(own_came, n), shards_of(other_came, n), blocks),
                    lambda: unpack(place_ref, shards_of(own, n), shards_of(other, n), blocks),
                )
                filter_rows(lambda e: blocks[e], band_ref, store)
                wanted = columns[...]
                projected = dot(high_ref[...], wanted, NT) + dot(low_ref[...], wanted, NT)
                right_ref[:, n * rows : (n + 1) * rows] = projected.astype(BF16)

            @pl.when(first_col == 0)
            def _():
                right_ref[:, :HEAD] = w_ref[...]

    @pl.when(first_row >= HEAD)
    def _():
        eps, width = left_ref.shape[:2]
        sources = [left_ref.at[e, n, 0] for e in range(eps) for n in range(width)]
        for pair in range(lhs.shape[1] // LANES):
            even, odd = sources[2 * pair][...], sources[2 * pair + 1][...]
            across = slice(pair * LANES, (pair + 1) * LANES)
            lhs[:HALF, across] = jnp.concatenate([even[:, :half], odd[:, :half]], axis=1)
            lhs[HALF:, across] = jnp.concatenate([even[:, half:], odd[:, half:]], axis=1)
        out_ref[...] = dot(lhs[...], right_ref[...])

        @pl.when((first_row >= first_col) & (first_row < first_col + cols))
        def _():
            at = pl.multiple_of(first_row - first_col, rows)
            on_diagonal = iota((rows, rows), 0) == iota((rows, rows), 1)
            out_ref[:, pl.ds(at, rows)] += jnp.where(on_diagonal, reg_ref[...], 0.0)

    @pl.when(first_row < HEAD)
    def _():
        out_ref[...] = jnp.zeros_like(out_ref)

        @pl.when(first_col == 0)
        def _():
            out_ref[:, :HEAD] = factor_ref[...]


def multiply_part(part, parts, place, left, factor, regular, extra, out, right):
    eps, width, steps = left.shape[:3]
    rows = 2 * HALF
    cols = steps * rows
    epochs = eps * width * (LANES // 2)

    def reg_block(i, place):
        return 0, (place[PLACE_ROW] * parts + part) * steps + i

    def out_block(i, place):
        return part * steps + i, 0

    out_shape = [jax.ShapeDtypeStruct((parts * steps * rows, cols), F32)]
    out_specs = [pl.BlockSpec((rows, cols), out_block)]
    scratch = [pltpu.VMEM((rows, epochs), BF16)]
    operands = [left]
    in_specs = [
        pl.BlockSpec((eps, width, 1, HALF, LANES), lambda i, place: (0, 0, i, 0, 0)),
    ]
    if part == 0:
        operands += extra
        in_specs += [fixed(array) for array in extra]
        out_shape.append(jax.ShapeDtypeStruct((epochs, cols), BF16))
        out_specs.append(pl.BlockSpec((epochs, cols), lambda i, place: (0, 0)))
        scratch.append(pltpu.VMEM((rows, epochs), BF16))
        scratch.append(pltpu.VMEM((eps * width, HALF, LANES), BF16))
    else:
        operands += [right, out]
        in_specs += [fixed(right), ANY]
    alias = {len(operands): 0} if part else {}
    operands += [factor, regular.reshape(1, -1)]
    in_specs += [fixed(factor), pl.BlockSpec((1, rows), reg_block)]
    return pl.pallas_call(
        functools.partial(tile_kernel, part, parts),
        out_shape=out_shape,
        grid_spec=pltpu.PrefetchScalarGridSpec(
            num_scalar_prefetch=1,
            grid=(steps,),
            in_specs=in_specs,
            out_specs=out_specs,
            scratch_shapes=scratch,
        ),
        input_output_aliases=alias,
        compiler_params=pltpu.CompilerParams(vmem_limit_bytes=48 << 20),
        cost_estimate=FREE,
        name="multiply_part",
    )(place, *operands)


AXES = ("ep", "row", "col")


def sizes():
    return tuple(lax.axis_size(axis) for axis in AXES)


def flat(ep, row, col):
    _, rows, cols = sizes()
    return (ep * rows + row) * cols + col


def doubling(count, least):
    distances = []
    distance = count // 2
    while distance >= least:
        distances.append(distance)
        distance //= 2
    return distances


def spread_step(block, owner_of, distance):
    eps, rows, cols = sizes()
    route = []
    for e in range(eps):
        for c in range(cols):
            for other in range(0, rows, 2 * distance):
                source = owner_of(e, c) ^ other
                route.append((flat(e, source, c), flat(e, source ^ distance, c)))
    return lax.ppermute(block, AXES, route)


def panel_steps():
    eps, _, cols = sizes()
    return [(de, dc) for de in range(eps) for dc in range(cols)]


def gather_panel(note):
    eps, rows, cols = sizes()
    row = lax.axis_index("row")
    for distance in doubling(rows, 2):
        came = spread_step(note, lambda e, c: 0, distance)
        note = jnp.where((row & (2 * distance - 1)) == distance, came, note)
    notes = [note]
    for de, dc in panel_steps()[1:]:
        route = [
            (flat(e, r, c), flat((e + de) % eps, r, (c + dc) % cols))
            for e in range(eps)
            for r in range(0, rows, 2)
            for c in range(cols)
        ]
        notes.append(lax.ppermute(note, AXES, route))
    notes = jnp.concatenate(notes)
    came = lax.ppermute(notes, "row", [(r, r + 1) for r in range(0, rows, 2)])
    return notes, came


def on_device(design, taps, tap_count, order, regular):
    rows_dev = design.shape[1]
    eps, rows, cols = sizes()
    cols_dev = regular.shape[0] // (eps * cols)
    parts = rows_dev // cols_dev
    row, ep, col = (lax.axis_index(axis) for axis in ("row", "ep", "col"))
    group = lax.axis_index(("ep", "col"))
    everywhere = [(e, r, c) for e in range(eps) for r in range(rows) for c in range(cols)]
    owner = lambda e, c: (e * cols + c) * cols_dev // rows_dev
    inside = lambda r, c: c // parts == (r * parts % cols) // parts
    owns = lambda e, r, c: inside(r, c) and r * parts // cols == e
    first_owner = group * cols_dev // rows_dev
    takes = ((row ^ first_owner) & 1) == 1
    place = [row, group, ep, col, takes]
    chain = len(place)
    place += [((ep - de) % eps) * cols + (col - dc) % cols for de, dc in panel_steps()]
    place = jnp.stack([jnp.asarray(p, jnp.int32) for p in place])

    local, note = permute_local(place, design, order, tap_count, cols_dev)

    def across(block, wanted):
        route = [(flat(1 - e, r, c), flat(e, r, c)) for e, r, c in everywhere if wanted(e, r, c)]
        return lax.ppermute(block, AXES, route)

    distances = doubling(rows, 1)

    def spread_rest(block, got):
        for n, distance in enumerate(distances[1:]):
            hit = ((row ^ first_owner) & (4 * distance - 1)) == 2 * distance
            block = jnp.where(hit, got, block)
            got = spread_step(block, owner, distance)
        return block, got

    gathered = lax.all_gather(local, "col", axis=0)
    notes, came = gather_panel(note)
    band, taper, aug = start_panel(place, chain, taps, notes, came, regular)
    column, mine = separate(place, gathered, aug)
    theirs = across(mine, owns)
    own_got = spread_step(mine, owner, distances[0])
    rows_of = [lax.all_gather(part, "ep", axis=0) for part in column]
    aug = next_panel(1, aug, mine)
    aug = next_panel(2, aug, mine)
    theirs, own_got = gate([theirs, own_got], aug)
    other_got = spread_step(theirs, owner, distances[0])
    own_block, own_came = spread_rest(mine, own_got)
    factor, w, high, low = last_panel(3, aug, theirs, taper)
    (other_got,) = gate([other_got], factor)
    other_block, other_came = spread_rest(theirs, other_got)
    extra = [own_block, own_came, other_block, other_came, w, high, low, band]
    out, right = multiply_part(
        0, parts, place, rows_of[0], factor, regular, extra, None, None
    )
    for j in range(1, parts):
        (out,) = multiply_part(
            j, parts, place, rows_of[j], factor, regular, None, out, right
        )
    return out


def solution(mesh):
    in_specs = (P(("ep", "col"), "row"), P(), P(("ep", "col")), P("row"), P())
    out_specs = P("row", ("ep", "col"))
    return jax.shard_map(
        on_device, mesh=mesh, in_specs=in_specs, out_specs=out_specs, check_vma=False
    )
```

```python
import functools

import jax
import jax.numpy as jnp
from jax import lax
from jax.experimental import pallas as pl
from jax.experimental.pallas import tpu as pltpu
from jax.sharding import PartitionSpec as P

PANEL = 256
SECTIONS = 2
HEAD = PANEL * SECTIONS
PB = 128
LANES = 128
BLOCK = 128
HALF = 256
SUB = 8
NOTE = 16
EXACT = lax.Precision.HIGHEST
F32 = jnp.float32
BF16 = jnp.bfloat16


def iota(shape, axis):
    return lax.broadcasted_iota(jnp.int32, shape, axis)


def dot(left, right, contract=((1,), (0,)), precision=None):
    return lax.dot_general(
        left, right, (contract, ((), ())), preferred_element_type=F32, precision=precision
    )


NT = ((1,), (1,))
TN = ((0,), (0,))
VMEM = pl.BlockSpec(memory_space=pltpu.VMEM)
SMEM = pl.BlockSpec(memory_space=pltpu.SMEM)
ANY = pl.BlockSpec(memory_space=pl.ANY)
FREE = pl.CostEstimate(flops=0, bytes_accessed=0, transcendentals=0)
LIMIT = pltpu.CompilerParams(vmem_limit_bytes=24 << 20)
WIDE = pltpu.CompilerParams(vmem_limit_bytes=58 << 20)


def permute_kernel(place_ref, *refs):
    sources, refs = refs[:3], refs[3:]
    *part_refs, both_ref, note_ref = refs[:-4]
    order_ref, counts_ref, design_ref = targets = refs[-4:-1]
    copies = [
        pltpu.make_async_copy(source, target, refs[-1].at[n])
        for n, (source, target) in enumerate(zip(sources, targets))
    ]
    for copy in copies:
        copy.start()
    for copy in copies:
        copy.wait()
    epochs = design_ref.shape[0]
    parts, per_part = len(part_refs), part_refs[0].shape[0]
    lane = iota((PB, PB), 1).astype(F32)
    none = jnp.zeros((epochs, PB), BF16)
    groups = 2 * HALF // PB

    def packed(local, columns, block, part):
        first = block * groups + part
        second = first + HALF // PB
        pick = [jnp.where(local[:, g : g + 1] == lane, 1.0, 0.0) for g in (first, second)]
        pick = jnp.concatenate(pick, axis=1).astype(BF16)
        top = jnp.concatenate([columns(first), none], axis=1)
        low = jnp.concatenate([none, columns(second)], axis=1)
        return dot(pick, jnp.concatenate([top, low], axis=0), NT).astype(BF16)

    def order_of(rows):
        return (order_ref[rows, :] & (PB - 1)).astype(F32).T

    local = order_of(slice(0, per_part * groups))
    for part in range(HALF // PB):
        columns = lambda g: design_ref[:, g * PB : (g + 1) * PB]
        note_ref[0, part * PB : (part + 1) * PB, :] = packed(local, columns, 0, part)
    counts = counts_ref[...].astype(F32)
    counts = jnp.concatenate([counts] * (LANES // epochs), axis=1)
    note_ref[0, HALF:, :] = jnp.broadcast_to(counts, (NOTE, LANES)).astype(BF16)
    for j in range(parts):
        piece = lax.rem(place_ref[PLACE_COL] + j, parts)
        at = pl.multiple_of(piece * per_part * groups, per_part * groups)
        local = order_of(pl.ds(at, per_part * groups))
        columns = lambda g: design_ref[:, pl.ds(pl.multiple_of((at + g) * PB, PB), PB)]
        for block in range(per_part):
            for part in range(HALF // PB):
                rows = slice(part * PB, (part + 1) * PB)
                part_refs[j][block, rows, :] = packed(local, columns, block, part)
        both_ref[j] = part_refs[j][...]


def permute_local(place, design, order, tap_count, cols_dev):
    epochs, rows = design.shape
    parts, per_part = rows // cols_dev, cols_dev // (2 * HALF)
    piece = jax.ShapeDtypeStruct((per_part, HALF, LANES), BF16)
    both = jax.ShapeDtypeStruct((parts,) + piece.shape, BF16)
    note = jax.ShapeDtypeStruct((1, HALF + NOTE, LANES), BF16)
    return pl.pallas_call(
        permute_kernel,
        out_shape=(piece,) * parts + (both, note),
        in_specs=[SMEM] + [ANY] * 3,
        out_specs=(VMEM,) * (parts + 2),
        scratch_shapes=[
            pltpu.VMEM((rows // PB, PB), jnp.int32),
            pltpu.VMEM((1, epochs), jnp.int32),
            pltpu.VMEM((epochs, rows), BF16),
            pltpu.SemaphoreType.DMA((3,)),
        ],
        compiler_params=WIDE,
        name="permute_local",
    )(place, order.reshape(rows // PB, PB), tap_count.reshape(1, epochs), design)


PLACE_ROW, PLACE_GROUP, PLACE_EP, PLACE_COL, PLACE_TAKES, PLACE_OWNS, PLACE_FAR, PLACE_BACK = range(8)


def assemble_kernel(count, gated, after, whole, place_ref, *refs):
    shards, kept = refs[:count], refs[count : count + gated]
    out_refs, sem = refs[count + gated + after : -1], refs[-1]
    copies = [(shard, out_refs[0].at[n]) for n, shard in enumerate(shards)]
    if whole:
        copies += [(shard, out_refs[-1].at[n]) for n, shard in enumerate([kept[0], *shards])]
    copies = [pltpu.make_async_copy(a, b, sem.at[n]) for n, (a, b) in enumerate(copies)]
    for copy in copies:
        copy.start()
    for copy in copies:
        copy.wait()


def assemble(place, shards, gated, after, whole):
    count = len(shards)
    out_shape = [jax.ShapeDtypeStruct((count,) + shards[0].shape, BF16)]
    out_shape += [jax.ShapeDtypeStruct(g.shape, g.dtype) for g in gated]
    if whole:
        out_shape.append(jax.ShapeDtypeStruct((count + 1,) + shards[0].shape, BF16))
    return pl.pallas_call(
        functools.partial(assemble_kernel, count, len(gated), len(after), whole),
        out_shape=out_shape,
        in_specs=[SMEM] + [ANY] * (count + len(gated) + len(after)),
        out_specs=[ANY] * len(out_shape),
        input_output_aliases={1 + count + n: 1 + n for n in range(len(gated))},
        scratch_shapes=[pltpu.SemaphoreType.DMA((2 * count + 1,))],
        compiler_params=LIMIT,
        cost_estimate=FREE,
        name="assemble",
    )(place, *shards, *gated, *after)


def collect_kernel(place_ref, *refs):
    near, far, (out_ref, sem) = refs[:2], refs[2:4], refs[5:]

    def copy(sources):
        copies = [
            pltpu.make_async_copy(source, out_ref.at[n], sem.at[n]) for n, source in enumerate(sources)
        ]
        for c in copies:
            c.start()
        for c in copies:
            c.wait()

    choose(place_ref[PLACE_FAR] != 0, lambda: copy(far), lambda: copy(near))


def collect(place, near, far, after):
    return pl.pallas_call(
        collect_kernel,
        out_shape=jax.ShapeDtypeStruct((2,) + near[0].shape, BF16),
        in_specs=[SMEM] + [ANY] * 5,
        out_specs=ANY,
        scratch_shapes=[pltpu.SemaphoreType.DMA((2,))],
        compiler_params=LIMIT,
        cost_estimate=FREE,
        name="collect",
    )(place, *near, *far, after)


def gate(arrays, after):
    count = len(arrays)
    return pl.pallas_call(
        lambda *refs: None,
        out_shape=tuple(jax.ShapeDtypeStruct(x.shape, x.dtype) for x in arrays),
        in_specs=[ANY] * (count + 1),
        out_specs=(ANY,) * count,
        input_output_aliases={n: n for n in range(count)},
        compiler_params=LIMIT,
        cost_estimate=FREE,
        name="gate",
    )(*arrays, after)


def filter_rows(blocks, band_ref, store):
    for b in range(band_ref.shape[0]):
        first = max(2 * b - 1, 0)
        skip = 0 if b else LANES
        packed = jnp.concatenate([blocks(e) for e in range(first, 2 * b + 2)], axis=1)
        got = dot(packed, band_ref[b, skip:, :]).astype(BF16)
        for half in range(2):
            across = slice(half * LANES, (half + 1) * LANES)
            store(slice(half * HALF, (half + 1) * HALF), slice(b * LANES, (b + 1) * LANES), got[:, across])


def spread(tile, lane):
    return jnp.broadcast_to(tile[:, lane : lane + 1], (SUB, tile.shape[1]))


def row_of(tile, k):
    return jnp.broadcast_to(tile[k : k + 1, :], (SUB, tile.shape[1]))


def factor_block(work):
    groups = BLOCK // SUB
    sub, lane = iota((SUB, BLOCK), 0), iota((SUB, BLOCK), 1)
    tiles = [work[g * SUB : (g + 1) * SUB, :] for g in range(groups)]
    for g in range(groups):
        inside = (lane >= g * SUB) & (lane < (g + 1) * SUB)
        cols = [spread(tiles[g], g * SUB + j) for j in range(SUB)]
        a = {(i, j): row_of(cols[j], i) for j in range(SUB) for i in range(j, SUB)}
        own = jnp.where(inside, jnp.where(lane - g * SUB == sub, 1.0, 0.0), tiles[g])
        u = [row_of(own, k) for k in range(SUB)]
        inv = []
        low = {}
        for k in range(SUB):
            r = lax.rsqrt(a[k, k])
            inv.append(r)
            for i in range(k + 1, SUB):
                low[i, k] = a[i, k] * r
            for j in range(k + 1, SUB):
                for i in range(j, SUB):
                    a[i, j] = a[i, j] - low[i, k] * low[j, k]
            u[k] = u[k] * r
            for j in range(k + 1, SUB):
                u[j] = u[j] - low[j, k] * u[k]
        for t in range(g + 1, groups):
            left = [spread(tiles[t], g * SUB + j) for j in range(SUB)]
            tile = jnp.where(inside, 0.0, tiles[t])
            for k in range(SUB):
                left[k] = left[k] * inv[k]
                for j in range(k + 1, SUB):
                    left[j] = left[j] - low[j, k] * left[k]
                tile = tile - left[k] * u[k]
            tiles[t] = tile
        merged = u[0]
        for k in range(1, SUB):
            merged = jnp.where(sub == k, u[k], merged)
        work[g * SUB : (g + 1) * SUB, :] = jnp.where(lane < (g + 1) * SUB, merged, 0.0)


def start_kernel(
    chain, place_ref, taps_ref, own_ref, came_ref, reg_ref, after, band_ref, taper_ref, aug_ref, notes, a1,
    work,
):
    del after
    epochs = aug_ref.shape[1] - HEAD
    half = LANES // 2

    @pl.when(place_ref[0] % 2 == 0)
    def _():
        for rel in range(own_ref.shape[0]):
            notes[place_ref[chain + rel]] = own_ref[rel]

    @pl.when(place_ref[0] % 2 == 1)
    def _():
        for rel in range(own_ref.shape[0]):
            notes[place_ref[chain + rel]] = came_ref[rel]

    shape = (half, LANES)
    lag = iota(shape, 1) - iota(shape, 0)
    base = lax.fori_loop(
        0,
        taps_ref.shape[0],
        lambda k, kept: jnp.where(lag == k, taps_ref[k], kept),
        jnp.zeros(shape, F32),
    )
    lane = iota(shape, 1)
    swapped = jnp.concatenate([base[:, half:], base[:, :half]], axis=1)
    patterns = (jnp.where(lane < half, swapped, 0.0), base, jnp.where(lane >= half, swapped, 0.0))
    row = iota((1, LANES), 1)
    sources = epochs // half
    counts = [notes[e, HALF : HALF + NOTE, :].astype(F32)[:1] for e in range(sources)]
    counts.append(jnp.zeros_like(counts[0]))
    band_ref[...] = jnp.zeros_like(band_ref)
    for e in range(sources):
        limit = jnp.where(row < half, counts[e], counts[e + 1])
        taper_ref[e] = jnp.where(lag.astype(F32) < limit, base, 0.0).astype(BF16)
    for b in range(epochs // LANES):
        limit = jnp.where(row < half, counts[2 * b], counts[2 * b + 1])
        for j, pattern in enumerate(patterns):
            at = (lag + half - half * j).astype(F32)
            kept = jnp.where(at < limit, pattern, 0.0).astype(BF16)
            for h in range(2):
                rows = slice(j * LANES + h * half, j * LANES + (h + 1) * half)
                band_ref[b, rows, h * LANES : (h + 1) * LANES] = kept

    def store(rows, cols, got):
        a1[rows, cols] = got

    filter_rows(lambda e: notes[e, :HALF, :], band_ref, store)
    columns = a1[...]
    square = (HEAD, HEAD)
    on_diagonal = iota(square, 0) == iota(square, 1)
    aug_ref[:, :HEAD] = dot(columns, columns, NT) + jnp.where(on_diagonal, reg_ref[:, :HEAD], 0.0)
    aug_ref[:, HEAD:] = columns.astype(F32)
    eliminate(aug_ref, 0, work)


def eliminate(aug, kb, work):
    here = slice(kb * BLOCK, (kb + 1) * BLOCK)
    work[...] = aug[here, here]
    factor_block(work)
    rest = slice(kb * BLOCK, aug.shape[1])
    aug[here, rest] = dot(work[...], aug[here, rest], precision=EXACT)
    for rb in range(kb + 1, HEAD // BLOCK):
        below = slice(rb * BLOCK, (rb + 1) * BLOCK)
        rest = slice(rb * BLOCK, aug.shape[1])
        aug[below, rest] -= dot(aug[here, below], aug[here, rest], TN, precision=EXACT)


def next_kernel(kb, aug_in, after, aug_ref, work):
    del after
    aug_ref[...] = aug_in[...]
    eliminate(aug_ref, kb, work)


def last_kernel(kb, aug_in, after, taper_ref, factor_ref, w_ref, high_ref, low_ref, aug, work, high, low):
    del after
    aug[...] = aug_in[...]
    eliminate(aug, kb, work)
    square = (HEAD, HEAD)
    epochs = aug.shape[1] - HEAD
    factor_ref[...] = jnp.where(iota(square, 0) >= iota(square, 1), aug[:, :HEAD].T, 0.0)
    wt = aug[:, HEAD:]

    def keep(rows, cols, values):
        top = values.astype(BF16)
        high[rows, cols] = top
        low[rows, cols] = (values - top.astype(F32)).astype(BF16)

    keep(slice(None), slice(epochs, None), wt.T)
    for b in range(epochs // BLOCK):
        here = slice(b * BLOCK, (b + 1) * BLOCK)
        shape = (BLOCK, epochs)
        unit = jnp.where(iota(shape, 0) + b * BLOCK == iota(shape, 1), 1.0, 0.0)
        keep(here, slice(0, epochs), unit - dot(wt[:, here], wt, TN, precision=EXACT))
    count, half = taper_ref.shape[:2]
    for e in range(count):
        reach = min(LANES, epochs - e * half)
        rows = slice(e * half, e * half + reach)
        taper = taper_ref[e, :, :reach]
        got = dot(taper, high[rows, :]) + dot(taper, low[rows, :])
        here = slice(e * half, (e + 1) * half)
        w_ref[here, :] = got[:, epochs:].astype(BF16)
        top = got[:, :epochs].astype(BF16)
        high_ref[here, :] = top
        low_ref[here, :] = (got[:, :epochs] - top.astype(F32)).astype(BF16)


def start_panel(place, chain, taps, own, came, regular, after):
    epochs = own.shape[0] * (LANES // 2)
    half = LANES // 2
    return pl.pallas_call(
        functools.partial(start_kernel, chain),
        out_shape=(
            jax.ShapeDtypeStruct((epochs // LANES, 3 * LANES, 2 * LANES), BF16),
            jax.ShapeDtypeStruct((epochs // half, half, LANES), BF16),
            jax.ShapeDtypeStruct((HEAD, HEAD + epochs), F32),
        ),
        in_specs=[SMEM, SMEM, VMEM, VMEM, VMEM, ANY],
        out_specs=(VMEM,) * 3,
        scratch_shapes=[
            pltpu.VMEM(own.shape, BF16),
            pltpu.VMEM((HEAD, epochs), BF16),
            pltpu.VMEM((BLOCK, BLOCK), F32),
        ],
        compiler_params=LIMIT,
        cost_estimate=FREE,
        name="start_panel",
    )(place, taps, own, came, regular.reshape(1, -1), after)


def next_panel(kb, aug, after):
    return pl.pallas_call(
        functools.partial(next_kernel, kb),
        out_shape=jax.ShapeDtypeStruct(aug.shape, F32),
        in_specs=[VMEM, ANY],
        out_specs=VMEM,
        scratch_shapes=[pltpu.VMEM((BLOCK, BLOCK), F32)],
        compiler_params=LIMIT,
        cost_estimate=FREE,
        name="next_panel",
    )(aug, after)


def last_panel(kb, aug, after, taper):
    epochs = aug.shape[1] - HEAD
    return pl.pallas_call(
        functools.partial(last_kernel, kb),
        out_shape=(
            jax.ShapeDtypeStruct((HEAD, HEAD), F32),
            jax.ShapeDtypeStruct((epochs, HEAD), BF16),
            jax.ShapeDtypeStruct((epochs, epochs), BF16),
            jax.ShapeDtypeStruct((epochs, epochs), BF16),
        ),
        in_specs=[VMEM, ANY, VMEM],
        out_specs=(VMEM,) * 4,
        scratch_shapes=[
            pltpu.VMEM(aug.shape, F32),
            pltpu.VMEM((BLOCK, BLOCK), F32),
            pltpu.VMEM((epochs, epochs + HEAD), BF16),
            pltpu.VMEM((epochs, epochs + HEAD), BF16),
        ],
        compiler_params=LIMIT,
        cost_estimate=FREE,
        name="last_panel",
    )(aug, after, taper)


def shards_of(ref, block):
    return [ref.at[n, block] for n in range(ref.shape[0])]


def unpack(place_ref, own, other, blocks):
    width = len(own)
    here = place_ref[PLACE_EP] * width
    there = width - here
    for n in range(width):
        back = place_ref[PLACE_BACK + n]
        blocks[here + back] = own[n][...]
        blocks[there + back] = other[n][...]


def unpack_both(place_ref, both, block, blocks):
    unpack(place_ref, shards_of(both.at[0], block), shards_of(both.at[1], block), blocks)


def choose(condition, yes, no):
    pl.when(condition)(yes)
    pl.when(jnp.logical_not(condition))(no)


def fixed(array):
    return pl.BlockSpec(
        array.shape, lambda i, place: (0,) * array.ndim, pipeline_mode=pl.Buffered(1)
    )


def tile_kernel(part, parts, place_ref, own_first, own_rest, other_first, other_rest, *refs):
    if part == 0:
        theirs_ref, near_ref, came_ref, w_ref, high_ref, low_ref, band_ref = refs[:7]
        factor_ref, reg_ref, out_ref, right_ref, blocks, lhs, columns = refs[7:]
    else:
        right_ref, _, factor_ref, reg_ref, out_ref, blocks, lhs = refs
    i, steps = pl.program_id(0), pl.num_programs(0)
    rows, cols = out_ref.shape
    half = LANES // 2
    block = lax.rem(place_ref[PLACE_COL] + part, parts) * steps + i
    first_row = (place_ref[PLACE_ROW] * parts * steps + block) * rows
    first_col = place_ref[PLACE_GROUP] * cols

    if part == 0:

        @pl.when(i == 0)
        def _():
            def store(rows, cols, got):
                columns[rows, cols] = got

            for n in range(cols // rows):
                choose(
                    place_ref[PLACE_TAKES] != 0,
                    lambda: unpack_both(place_ref, came_ref, n, blocks),
                    lambda: unpack_both(place_ref, near_ref, n, blocks),
                )
                filter_rows(lambda e: blocks[e], band_ref, store)
                wanted = columns[...]
                projected = dot(high_ref[...], wanted, NT) + dot(low_ref[...], wanted, NT)
                right_ref[:, n * rows : (n + 1) * rows] = projected.astype(BF16)

            @pl.when(first_col == 0)
            def _():
                right_ref[:, :HEAD] = w_ref[...]

    @pl.when(first_row >= HEAD)
    def _():
        mine = [own_first.at[0], *shards_of(own_rest, 0)]
        others = [other_first.at[0, 0], *shards_of(other_rest, 0)]
        if part == 0:
            choose(
                place_ref[PLACE_OWNS] != 0,
                lambda: unpack(place_ref, mine, shards_of(theirs_ref, 0), blocks),
                lambda: unpack(place_ref, mine, others, blocks),
            )
        else:
            unpack(place_ref, mine, others, blocks)
        for pair in range(lhs.shape[1] // LANES):
            even, odd = blocks[2 * pair], blocks[2 * pair + 1]
            across = slice(pair * LANES, (pair + 1) * LANES)
            lhs[:HALF, across] = jnp.concatenate([even[:, :half], odd[:, :half]], axis=1)
            lhs[HALF:, across] = jnp.concatenate([even[:, half:], odd[:, half:]], axis=1)
        out_ref[...] = dot(lhs[...], right_ref[...])

        @pl.when((first_row >= first_col) & (first_row < first_col + cols))
        def _():
            at = pl.multiple_of(first_row - first_col, rows)
            on_diagonal = iota((rows, rows), 0) == iota((rows, rows), 1)
            out_ref[:, pl.ds(at, rows)] += jnp.where(on_diagonal, reg_ref[...], 0.0)

    @pl.when(first_row < HEAD)
    def _():
        out_ref[...] = jnp.zeros_like(out_ref)

        @pl.when(first_col == 0)
        def _():
            out_ref[:, :HEAD] = factor_ref[...]


def multiply_part(part, parts, place, own, other, factor, regular, extra, out, right):
    steps = own[0].shape[0]
    rows = 2 * HALF
    cols = steps * rows
    epochs = (own[1].shape[0] + 1) * 2 * (LANES // 2)

    def reg_block(i, place):
        block = lax.rem(place[PLACE_COL] + part, parts) * steps + i
        return 0, place[PLACE_ROW] * parts * steps + block

    def out_block(i, place):
        return lax.rem(place[PLACE_COL] + part, parts) * steps + i, 0

    def shards_spec(array):
        return pl.BlockSpec((array.shape[0], 1, HALF, LANES), lambda i, place: (0, i, 0, 0))

    out_shape = [jax.ShapeDtypeStruct((parts * steps * rows, cols), F32)]
    out_specs = [pl.BlockSpec((rows, cols), out_block)]
    scratch = [
        pltpu.VMEM((epochs // (LANES // 2), HALF, LANES), BF16),
        pltpu.VMEM((rows, epochs), BF16),
    ]
    operands = [*own, *other]
    in_specs = [pl.BlockSpec((1, HALF, LANES), lambda i, place: (i, 0, 0)), shards_spec(own[1])]
    in_specs += [pl.BlockSpec((1, 1, HALF, LANES), lambda i, place: (part, i, 0, 0))]
    in_specs += [shards_spec(other[1])]
    if part == 0:
        operands += extra
        in_specs += [shards_spec(extra[0])]
        in_specs += [fixed(array) for array in extra[1:]]
        out_shape.append(jax.ShapeDtypeStruct((epochs, cols), BF16))
        out_specs.append(pl.BlockSpec((epochs, cols), lambda i, place: (0, 0)))
        scratch.append(pltpu.VMEM((rows, epochs), BF16))
    else:
        operands += [right, out]
        in_specs += [fixed(right), ANY]
    alias = {len(operands): 0} if part else {}
    operands += [factor, regular.reshape(1, -1)]
    in_specs += [fixed(factor), pl.BlockSpec((1, rows), reg_block)]
    return pl.pallas_call(
        functools.partial(tile_kernel, part, parts),
        out_shape=out_shape,
        grid_spec=pltpu.PrefetchScalarGridSpec(
            num_scalar_prefetch=1,
            grid=(steps,),
            in_specs=in_specs,
            out_specs=out_specs,
            scratch_shapes=scratch,
        ),
        input_output_aliases=alias,
        compiler_params=WIDE,
        cost_estimate=FREE,
        name="multiply_part",
    )(place, *operands)


AXES = ("ep", "row", "col")


def sizes():
    return tuple(lax.axis_size(axis) for axis in AXES)


def flat(ep, row, col):
    _, rows, cols = sizes()
    return (ep * rows + row) * cols + col


def doubling(count, least):
    distances = []
    distance = count // 2
    while distance >= least:
        distances.append(distance)
        distance //= 2
    return distances


def spread_step(block, owner_of, distance):
    eps, rows, cols = sizes()
    route = []
    for e in range(eps):
        for c in range(cols):
            for other in range(0, rows, 2 * distance):
                source = owner_of(e, c) ^ other
                route.append((flat(e, source, c), flat(e, source ^ distance, c)))
    return lax.ppermute(block, AXES, route)


def panel_steps():
    eps, _, cols = sizes()
    return [(de, dc) for de in range(eps) for dc in range(cols)]


def gather_panel(note):
    eps, rows, cols = sizes()
    row = lax.axis_index("row")
    for distance in doubling(rows, 2):
        came = spread_step(note, lambda e, c: 0, distance)
        note = jnp.where((row & (2 * distance - 1)) == distance, came, note)
    notes = [note]
    for de, dc in panel_steps()[1:]:
        route = [
            (flat(e, r, c), flat((e + de) % eps, r, (c + dc) % cols))
            for e in range(eps)
            for r in range(0, rows, 2)
            for c in range(cols)
        ]
        notes.append(lax.ppermute(note, AXES, route))
    notes = jnp.concatenate(notes)
    came = lax.ppermute(notes, "row", [(r, r + 1) for r in range(0, rows, 2)])
    return notes, came


def on_device(design, taps, tap_count, order, regular):
    rows_dev = design.shape[1]
    eps, rows, cols = sizes()
    cols_dev = regular.shape[0] // (eps * cols)
    parts = rows_dev // cols_dev
    row, ep, col = (lax.axis_index(axis) for axis in ("row", "ep", "col"))
    group = lax.axis_index(("ep", "col"))
    everywhere = [(e, r, c) for e in range(eps) for r in range(rows) for c in range(cols)]
    owner = lambda e, c: (e * cols + c) * cols_dev // rows_dev
    owns = lambda e, r, c: (c // parts == (r * parts % cols) // parts) & (r * parts // cols == e)
    first_owner = group * cols_dev // rows_dev
    takes = ((row ^ first_owner) & 1) == 1
    far = (row ^ first_owner) >= rows // 2
    back = [(col - n) % cols for n in range(cols)]
    place = [row, group, ep, col, takes, owns(ep, row, col), far, *back]
    chain = len(place)
    place += [((ep - de) % eps) * cols + (col - dc) % cols for de, dc in panel_steps()]
    place = jnp.stack([jnp.asarray(p, jnp.int32) for p in place])

    *local, both, note = permute_local(place, design, order, tap_count, cols_dev)

    def shift(block, n):
        route = [(flat(e, r, (c - n) % cols), flat(e, r, c)) for e, r, c in everywhere]
        return lax.ppermute(block, AXES, route)

    def across(block, wanted):
        route = [(flat(1 - e, r, c), flat(e, r, c)) for e, r, c in everywhere if wanted(e, r, c)]
        return lax.ppermute(block, AXES, route)

    distances = doubling(rows, 1)

    def diagonal(block):
        route = [
            (flat(1 - e, owner(e, c), c), flat(e, owner(e, c) ^ distances[0], c))
            for e in range(eps)
            for c in range(cols)
        ]
        return lax.ppermute(block, AXES, route)

    anyone = lambda e, r, c: True
    notes, came = gather_panel(note)
    *local, both = gate([*local, both], notes)
    early = [shift(local[n % parts], n) for n in range(1, cols)]
    swapped = across(both, anyone)
    band, taper, aug = start_panel(place, chain, taps, notes, came, regular, notes)
    aug = next_panel(1, aug, aug)
    rest, *local, first = assemble(place, early, local, [aug, swapped], True)
    theirs = across(first, owns)
    far_own = spread_step(first, owner, distances[0])
    far_other = diagonal(first)
    others = [across(rest, lambda e, r, c: not owns(e, r, c))]
    mine = [rest]
    order = [(j, n) for j in range(1, parts) for n in range(1, cols)]
    late = [shift(local[(n + j) % parts], n) for j, n in order[:1]]
    aug = next_panel(2, aug, first)
    theirs, far_own, far_other, *passed = gate([theirs, far_own, far_other, *late, *local], aug)
    late, local = passed[: len(late)], passed[len(late) :]
    late += [shift(local[(n + j) % parts], n) for j, n in order[1:]]
    factor, w, high, low = last_panel(3, aug, theirs, taper)
    others[0], *late[1:] = gate([others[0], *late[1:]], factor)
    wanted = collect(place, [first, theirs], [far_own, far_other], others[0])
    for distance in distances[1:]:
        got = spread_step(wanted, owner, distance)
        if distance > 1:
            wanted = jnp.where(((row ^ first_owner) & (2 * distance - 1)) == distance, got, wanted)
    for j in range(1, parts):
        shards = late[(j - 1) * (cols - 1) : j * (cols - 1)]
        (whole,) = assemble(place, shards, [], [factor], False)
        mine.append(whole)
        others.append(across(whole, anyone))
    extra = [theirs, wanted, got, w, high, low, band]
    mine = [(local[j], mine[j]) for j in range(parts)]
    others = [(swapped, others[j]) for j in range(parts)]
    out, right = multiply_part(
        0, parts, place, mine[0], others[0], factor, regular, extra, None, None
    )
    for j in range(1, parts):
        (out,) = multiply_part(
            j, parts, place, mine[j], others[j], factor, regular, None, out, right
        )
    return out


def solution(mesh):
    in_specs = (P(("ep", "col"), "row"), P(), P(("ep", "col")), P("row"), P())
    out_specs = P("row", ("ep", "col"))
    return jax.shard_map(
        on_device, mesh=mesh, in_specs=in_specs, out_specs=out_specs, check_vma=False
    )
```

```python
import functools

import jax
import jax.numpy as jnp
from jax import lax
from jax.experimental import pallas as pl
from jax.experimental.pallas import tpu as pltpu
from jax.sharding import PartitionSpec as P

PANEL = 256
SECTIONS = 2
HEAD = PANEL * SECTIONS
PB = 128
LANES = 128
BLOCK = 128
HALF = 256
SUB = 8
NOTE = 16
EXACT = lax.Precision.HIGHEST
F32 = jnp.float32
BF16 = jnp.bfloat16


def iota(shape, axis):
    return lax.broadcasted_iota(jnp.int32, shape, axis)


def dot(left, right, contract=((1,), (0,)), precision=None):
    return lax.dot_general(
        left, right, (contract, ((), ())), preferred_element_type=F32, precision=precision
    )


NT = ((1,), (1,))
TN = ((0,), (0,))
VMEM = pl.BlockSpec(memory_space=pltpu.VMEM)
SMEM = pl.BlockSpec(memory_space=pltpu.SMEM)
ANY = pl.BlockSpec(memory_space=pl.ANY)
FREE = pl.CostEstimate(flops=0, bytes_accessed=0, transcendentals=0)
LIMIT = pltpu.CompilerParams(vmem_limit_bytes=24 << 20)
MIDDLE = pltpu.CompilerParams(vmem_limit_bytes=32 << 20)
WIDE = pltpu.CompilerParams(vmem_limit_bytes=58 << 20)


def permute_kernel(place_ref, *refs):
    sources, refs = refs[:3], refs[3:]
    *part_refs, both_ref, note_ref = refs[:-4]
    order_ref, counts_ref, design_ref = targets = refs[-4:-1]
    copies = [
        pltpu.make_async_copy(source, target, refs[-1].at[n])
        for n, (source, target) in enumerate(zip(sources, targets))
    ]
    for copy in copies:
        copy.start()
    for copy in copies:
        copy.wait()
    epochs = design_ref.shape[0]
    parts, per_part = len(part_refs), part_refs[0].shape[0]
    lane = iota((PB, PB), 1).astype(F32)
    none = jnp.zeros((epochs, PB), BF16)
    groups = 2 * HALF // PB

    def packed(local, columns, block, part):
        first = block * groups + part
        second = first + HALF // PB
        pick = [jnp.where(local[:, g : g + 1] == lane, 1.0, 0.0) for g in (first, second)]
        pick = jnp.concatenate(pick, axis=1).astype(BF16)
        top = jnp.concatenate([columns(first), none], axis=1)
        low = jnp.concatenate([none, columns(second)], axis=1)
        return dot(pick, jnp.concatenate([top, low], axis=0), NT).astype(BF16)

    def order_of(rows):
        return (order_ref[rows, :] & (PB - 1)).astype(F32).T

    local = order_of(slice(0, per_part * groups))
    for part in range(HALF // PB):
        columns = lambda g: design_ref[:, g * PB : (g + 1) * PB]
        note_ref[0, part * PB : (part + 1) * PB, :] = packed(local, columns, 0, part)
    counts = counts_ref[...].astype(F32)
    counts = jnp.concatenate([counts] * (LANES // epochs), axis=1)
    note_ref[0, HALF:, :] = jnp.broadcast_to(counts, (NOTE, LANES)).astype(BF16)
    for j in range(parts):
        piece = lax.rem(place_ref[PLACE_COL] + j, parts)
        at = pl.multiple_of(piece * per_part * groups, per_part * groups)
        local = order_of(pl.ds(at, per_part * groups))
        columns = lambda g: design_ref[:, pl.ds(pl.multiple_of((at + g) * PB, PB), PB)]
        for block in range(per_part):
            for part in range(HALF // PB):
                rows = slice(part * PB, (part + 1) * PB)
                part_refs[j][block, rows, :] = packed(local, columns, block, part)
        both_ref[j] = part_refs[j][...]


def permute_local(place, design, order, tap_count, cols_dev):
    epochs, rows = design.shape
    parts, per_part = rows // cols_dev, cols_dev // (2 * HALF)
    piece = jax.ShapeDtypeStruct((per_part, HALF, LANES), BF16)
    both = jax.ShapeDtypeStruct((parts,) + piece.shape, BF16)
    note = jax.ShapeDtypeStruct((1, HALF + NOTE, LANES), BF16)
    return pl.pallas_call(
        permute_kernel,
        out_shape=(piece,) * parts + (both, note),
        in_specs=[SMEM] + [ANY] * 3,
        out_specs=(VMEM,) * (parts + 2),
        scratch_shapes=[
            pltpu.VMEM((rows // PB, PB), jnp.int32),
            pltpu.VMEM((1, epochs), jnp.int32),
            pltpu.VMEM((epochs, rows), BF16),
            pltpu.SemaphoreType.DMA((3,)),
        ],
        compiler_params=WIDE,
        name="permute_local",
    )(place, order.reshape(rows // PB, PB), tap_count.reshape(1, epochs), design)


PLACE_ROW, PLACE_GROUP, PLACE_EP, PLACE_COL, PLACE_TAKES, PLACE_OWNS, PLACE_HOME, PLACE_BACK = range(8)


def assemble_kernel(count, gated, after, whole, place_ref, *refs):
    shards, kept = refs[:count], refs[count : count + gated]
    out_refs, sem = refs[count + gated + after : -1], refs[-1]
    copies = [(shard, out_refs[0].at[n]) for n, shard in enumerate(shards)]
    if whole:
        copies += [(shard, out_refs[-1].at[n]) for n, shard in enumerate([kept[0], *shards])]
    copies = [pltpu.make_async_copy(a, b, sem.at[n]) for n, (a, b) in enumerate(copies)]
    for copy in copies:
        copy.start()
    for copy in copies:
        copy.wait()


def assemble(place, shards, gated, after, whole):
    count = len(shards)
    out_shape = [jax.ShapeDtypeStruct((count,) + shards[0].shape, BF16)]
    out_shape += [jax.ShapeDtypeStruct(g.shape, g.dtype) for g in gated]
    if whole:
        out_shape.append(jax.ShapeDtypeStruct((count + 1,) + shards[0].shape, BF16))
    return pl.pallas_call(
        functools.partial(assemble_kernel, count, len(gated), len(after), whole),
        out_shape=out_shape,
        in_specs=[SMEM] + [ANY] * (count + len(gated) + len(after)),
        out_specs=[ANY] * len(out_shape),
        input_output_aliases={1 + count + n: 1 + n for n in range(len(gated))},
        scratch_shapes=[pltpu.SemaphoreType.DMA((2 * count + 1,))],
        compiler_params=LIMIT,
        cost_estimate=FREE,
        name="assemble",
    )(place, *shards, *gated, *after)


def sort_kernel(place_ref, native_ref, foreign_ref, keep_ref, send_ref, sem):
    def copy(kept, sent):
        copies = [
            pltpu.make_async_copy(kept, keep_ref, sem.at[0]),
            pltpu.make_async_copy(sent, send_ref, sem.at[1]),
        ]
        for c in copies:
            c.start()
        for c in copies:
            c.wait()

    choose(
        place_ref[PLACE_HOME] != 0,
        lambda: copy(native_ref, foreign_ref),
        lambda: copy(foreign_ref, native_ref),
    )


def sort(place, native, foreign):
    shape = jax.ShapeDtypeStruct(native.shape, BF16)
    return pl.pallas_call(
        sort_kernel,
        out_shape=(shape, shape),
        in_specs=[SMEM, ANY, ANY],
        out_specs=(ANY, ANY),
        scratch_shapes=[pltpu.SemaphoreType.DMA((2,))],
        compiler_params=LIMIT,
        cost_estimate=FREE,
        name="sort",
    )(place, native, foreign)


def gate(arrays, after):
    count = len(arrays)
    return pl.pallas_call(
        lambda *refs: None,
        out_shape=tuple(jax.ShapeDtypeStruct(x.shape, x.dtype) for x in arrays),
        in_specs=[ANY] * (count + 1),
        out_specs=(ANY,) * count,
        input_output_aliases={n: n for n in range(count)},
        compiler_params=LIMIT,
        cost_estimate=FREE,
        name="gate",
    )(*arrays, after)


def filter_rows(blocks, band_ref, store):
    for b in range(band_ref.shape[0]):
        first = max(2 * b - 1, 0)
        skip = 0 if b else LANES
        packed = jnp.concatenate([blocks(e) for e in range(first, 2 * b + 2)], axis=1)
        got = dot(packed, band_ref[b, skip:, :]).astype(BF16)
        for half in range(2):
            across = slice(half * LANES, (half + 1) * LANES)
            store(slice(half * HALF, (half + 1) * HALF), slice(b * LANES, (b + 1) * LANES), got[:, across])


def spread(tile, lane):
    return jnp.broadcast_to(tile[:, lane : lane + 1], (SUB, tile.shape[1]))


def row_of(tile, k):
    return jnp.broadcast_to(tile[k : k + 1, :], (SUB, tile.shape[1]))


def factor_block(work):
    groups = BLOCK // SUB
    sub, lane = iota((SUB, BLOCK), 0), iota((SUB, BLOCK), 1)
    tiles = [work[g * SUB : (g + 1) * SUB, :] for g in range(groups)]
    for g in range(groups):
        inside = (lane >= g * SUB) & (lane < (g + 1) * SUB)
        cols = [spread(tiles[g], g * SUB + j) for j in range(SUB)]
        a = {(i, j): row_of(cols[j], i) for j in range(SUB) for i in range(j, SUB)}
        own = jnp.where(inside, jnp.where(lane - g * SUB == sub, 1.0, 0.0), tiles[g])
        u = [row_of(own, k) for k in range(SUB)]
        inv = []
        low = {}
        for k in range(SUB):
            r = lax.rsqrt(a[k, k])
            inv.append(r)
            for i in range(k + 1, SUB):
                low[i, k] = a[i, k] * r
            for j in range(k + 1, SUB):
                for i in range(j, SUB):
                    a[i, j] = a[i, j] - low[i, k] * low[j, k]
            u[k] = u[k] * r
            for j in range(k + 1, SUB):
                u[j] = u[j] - low[j, k] * u[k]
        for t in range(g + 1, groups):
            left = [spread(tiles[t], g * SUB + j) for j in range(SUB)]
            tile = jnp.where(inside, 0.0, tiles[t])
            for k in range(SUB):
                left[k] = left[k] * inv[k]
                for j in range(k + 1, SUB):
                    left[j] = left[j] - low[j, k] * left[k]
                tile = tile - left[k] * u[k]
            tiles[t] = tile
        merged = u[0]
        for k in range(1, SUB):
            merged = jnp.where(sub == k, u[k], merged)
        work[g * SUB : (g + 1) * SUB, :] = jnp.where(lane < (g + 1) * SUB, merged, 0.0)


def start_kernel(
    chain, place_ref, taps_ref, own_ref, came_ref, reg_ref, after, band_ref, taper_ref, aug_ref, notes, a1,
    work,
):
    del after
    epochs = aug_ref.shape[1] - HEAD
    half = LANES // 2

    @pl.when(place_ref[0] % 2 == 0)
    def _():
        for rel in range(own_ref.shape[0]):
            notes[place_ref[chain + rel]] = own_ref[rel]

    @pl.when(place_ref[0] % 2 == 1)
    def _():
        for rel in range(own_ref.shape[0]):
            notes[place_ref[chain + rel]] = came_ref[rel]

    shape = (half, LANES)
    lag = iota(shape, 1) - iota(shape, 0)
    base = lax.fori_loop(
        0,
        taps_ref.shape[0],
        lambda k, kept: jnp.where(lag == k, taps_ref[k], kept),
        jnp.zeros(shape, F32),
    )
    lane = iota(shape, 1)
    swapped = jnp.concatenate([base[:, half:], base[:, :half]], axis=1)
    patterns = (jnp.where(lane < half, swapped, 0.0), base, jnp.where(lane >= half, swapped, 0.0))
    row = iota((1, LANES), 1)
    sources = epochs // half
    counts = [notes[e, HALF : HALF + NOTE, :].astype(F32)[:1] for e in range(sources)]
    counts.append(jnp.zeros_like(counts[0]))
    band_ref[...] = jnp.zeros_like(band_ref)
    for e in range(sources):
        limit = jnp.where(row < half, counts[e], counts[e + 1])
        taper_ref[e] = jnp.where(lag.astype(F32) < limit, base, 0.0).astype(BF16)
    for b in range(epochs // LANES):
        limit = jnp.where(row < half, counts[2 * b], counts[2 * b + 1])
        for j, pattern in enumerate(patterns):
            at = (lag + half - half * j).astype(F32)
            kept = jnp.where(at < limit, pattern, 0.0).astype(BF16)
            for h in range(2):
                rows = slice(j * LANES + h * half, j * LANES + (h + 1) * half)
                band_ref[b, rows, h * LANES : (h + 1) * LANES] = kept

    def store(rows, cols, got):
        a1[rows, cols] = got

    filter_rows(lambda e: notes[e, :HALF, :], band_ref, store)
    columns = a1[...]
    square = (HEAD, HEAD)
    on_diagonal = iota(square, 0) == iota(square, 1)
    aug_ref[:, :HEAD] = dot(columns, columns, NT) + jnp.where(on_diagonal, reg_ref[:, :HEAD], 0.0)
    aug_ref[:, HEAD:] = columns.astype(F32)
    eliminate(aug_ref, 0, work)


def eliminate(aug, kb, work):
    here = slice(kb * BLOCK, (kb + 1) * BLOCK)
    work[...] = aug[here, here]
    factor_block(work)
    rest = slice(kb * BLOCK, aug.shape[1])
    aug[here, rest] = dot(work[...], aug[here, rest], precision=EXACT)
    for rb in range(kb + 1, HEAD // BLOCK):
        below = slice(rb * BLOCK, (rb + 1) * BLOCK)
        rest = slice(rb * BLOCK, aug.shape[1])
        aug[below, rest] -= dot(aug[here, below], aug[here, rest], TN, precision=EXACT)


def next_kernel(kb, aug_in, after, aug_ref, work):
    del after
    aug_ref[...] = aug_in[...]
    eliminate(aug_ref, kb, work)


def last_kernel(kb, aug_in, after, taper_ref, factor_ref, w_ref, high_ref, low_ref, aug, work, high, low):
    del after
    aug[...] = aug_in[...]
    eliminate(aug, kb, work)
    square = (HEAD, HEAD)
    epochs = aug.shape[1] - HEAD
    factor_ref[...] = jnp.where(iota(square, 0) >= iota(square, 1), aug[:, :HEAD].T, 0.0)
    wt = aug[:, HEAD:]

    def keep(rows, cols, values):
        top = values.astype(BF16)
        high[rows, cols] = top
        low[rows, cols] = (values - top.astype(F32)).astype(BF16)

    keep(slice(None), slice(epochs, None), wt.T)
    for b in range(epochs // BLOCK):
        here = slice(b * BLOCK, (b + 1) * BLOCK)
        shape = (BLOCK, epochs)
        unit = jnp.where(iota(shape, 0) + b * BLOCK == iota(shape, 1), 1.0, 0.0)
        keep(here, slice(0, epochs), unit - dot(wt[:, here], wt, TN, precision=lax.Precision.HIGH))
    count, half = taper_ref.shape[:2]
    for e in range(count):
        reach = min(LANES, epochs - e * half)
        rows = slice(e * half, e * half + reach)
        taper = taper_ref[e, :, :reach]
        got = dot(taper, high[rows, :]) + dot(taper, low[rows, :])
        here = slice(e * half, (e + 1) * half)
        w_ref[here, :] = got[:, epochs:].astype(BF16)
        top = got[:, :epochs].astype(BF16)
        high_ref[here, :] = top
        low_ref[here, :] = (got[:, :epochs] - top.astype(F32)).astype(BF16)


def start_panel(place, chain, taps, own, came, regular, after):
    epochs = own.shape[0] * (LANES // 2)
    half = LANES // 2
    return pl.pallas_call(
        functools.partial(start_kernel, chain),
        out_shape=(
            jax.ShapeDtypeStruct((epochs // LANES, 3 * LANES, 2 * LANES), BF16),
            jax.ShapeDtypeStruct((epochs // half, half, LANES), BF16),
            jax.ShapeDtypeStruct((HEAD, HEAD + epochs), F32),
        ),
        in_specs=[SMEM, SMEM, VMEM, VMEM, VMEM, ANY],
        out_specs=(VMEM,) * 3,
        scratch_shapes=[
            pltpu.VMEM(own.shape, BF16),
            pltpu.VMEM((HEAD, epochs), BF16),
            pltpu.VMEM((BLOCK, BLOCK), F32),
        ],
        compiler_params=LIMIT,
        cost_estimate=FREE,
        name="start_panel",
    )(place, taps, own, came, regular.reshape(1, -1), after)


def next_panel(kb, aug, after):
    return pl.pallas_call(
        functools.partial(next_kernel, kb),
        out_shape=jax.ShapeDtypeStruct(aug.shape, F32),
        in_specs=[VMEM, ANY],
        out_specs=VMEM,
        scratch_shapes=[pltpu.VMEM((BLOCK, BLOCK), F32)],
        compiler_params=LIMIT,
        cost_estimate=FREE,
        name="next_panel",
    )(aug, after)


def last_panel(kb, aug, after, taper):
    epochs = aug.shape[1] - HEAD
    return pl.pallas_call(
        functools.partial(last_kernel, kb),
        out_shape=(
            jax.ShapeDtypeStruct((HEAD, HEAD), F32),
            jax.ShapeDtypeStruct((epochs, HEAD), BF16),
            jax.ShapeDtypeStruct((epochs, epochs), BF16),
            jax.ShapeDtypeStruct((epochs, epochs), BF16),
        ),
        in_specs=[VMEM, ANY, VMEM],
        out_specs=(VMEM,) * 4,
        scratch_shapes=[
            pltpu.VMEM(aug.shape, F32),
            pltpu.VMEM((BLOCK, BLOCK), F32),
            pltpu.VMEM((epochs, epochs + HEAD), BF16),
            pltpu.VMEM((epochs, epochs + HEAD), BF16),
        ],
        compiler_params=LIMIT,
        cost_estimate=FREE,
        name="last_panel",
    )(aug, after, taper)


def shards_of(ref, block):
    return [ref.at[n, block] for n in range(ref.shape[0])]


def unpack(place_ref, own, other, blocks):
    width = len(own)
    here = place_ref[PLACE_EP] * width
    there = width - here
    for n in range(width):
        back = place_ref[PLACE_BACK + n]
        blocks[here + back] = own[n][...]
        blocks[there + back] = other[n][...]


def choose(condition, yes, no):
    pl.when(condition)(yes)
    pl.when(jnp.logical_not(condition))(no)


def fixed(array):
    return pl.BlockSpec(
        array.shape, lambda i, place: (0,) * array.ndim, pipeline_mode=pl.Buffered(1)
    )


def project_kernel(
    place_ref, own, own_came, other, other_came, w_ref, high_ref, low_ref, band_ref, right_ref,
    both, blocks, columns, sem,
):
    def bring(sources):
        copies = [
            pltpu.make_async_copy(source, both.at[n], sem.at[n]) for n, source in enumerate(sources)
        ]
        for copy in copies:
            copy.start()
        for copy in copies:
            copy.wait()

    choose(
        place_ref[PLACE_TAKES] != 0,
        lambda: bring((own_came, other_came)),
        lambda: bring((own, other)),
    )

    def store(rows, cols, got):
        columns[rows, cols] = got

    rows = 2 * HALF
    for n in range(right_ref.shape[1] // rows):
        unpack(place_ref, shards_of(both.at[0], n), shards_of(both.at[1], n), blocks)
        filter_rows(lambda e: blocks[e], band_ref, store)
        wanted = columns[...]
        projected = dot(high_ref[...], wanted, NT) + dot(low_ref[...], wanted, NT)
        right_ref[:, n * rows : (n + 1) * rows] = projected.astype(BF16)

    @pl.when(place_ref[PLACE_GROUP] == 0)
    def _():
        right_ref[:, :HEAD] = w_ref[...]


def project(place, own, own_came, other, other_came, w, high, low, band):
    width, count = own.shape[:2]
    epochs = high.shape[0]
    return pl.pallas_call(
        project_kernel,
        out_shape=jax.ShapeDtypeStruct((epochs, count * 2 * HALF), BF16),
        in_specs=[SMEM] + [ANY] * 4 + [VMEM] * 4,
        out_specs=VMEM,
        scratch_shapes=[
            pltpu.VMEM((2,) + own.shape, BF16),
            pltpu.VMEM((2 * width, HALF, LANES), BF16),
            pltpu.VMEM((2 * HALF, epochs), BF16),
            pltpu.SemaphoreType.DMA((2,)),
        ],
        compiler_params=LIMIT,
        cost_estimate=FREE,
        name="project",
    )(place, own, own_came, other, other_came, w, high, low, band)


def tile_kernel(part, parts, place_ref, own_first, own_rest, other_first, other_rest, *refs):
    theirs_ref = refs[0]
    right_ref, factor_ref, reg_ref = refs[:3] if part else refs[1:4]
    out_ref, blocks, lhs = refs[-3:]
    i, steps = pl.program_id(0), pl.num_programs(0)
    rows, cols = out_ref.shape
    half = LANES // 2
    block = lax.rem(place_ref[PLACE_COL] + part, parts) * steps + i
    first_row = (place_ref[PLACE_ROW] * parts * steps + block) * rows
    first_col = place_ref[PLACE_GROUP] * cols

    @pl.when(first_row >= HEAD)
    def _():
        mine = [own_first.at[0], *shards_of(own_rest, 0)]
        others = [other_first.at[0, 0], *shards_of(other_rest, 0)]
        if part == 0:
            choose(
                place_ref[PLACE_OWNS] != 0,
                lambda: unpack(place_ref, mine, shards_of(theirs_ref, 0), blocks),
                lambda: unpack(place_ref, mine, others, blocks),
            )
        else:
            unpack(place_ref, mine, others, blocks)
        for pair in range(lhs.shape[1] // LANES):
            even, odd = blocks[2 * pair], blocks[2 * pair + 1]
            across = slice(pair * LANES, (pair + 1) * LANES)
            lhs[:HALF, across] = jnp.concatenate([even[:, :half], odd[:, :half]], axis=1)
            lhs[HALF:, across] = jnp.concatenate([even[:, half:], odd[:, half:]], axis=1)
        out_ref[...] = dot(lhs[...], right_ref[...])

        @pl.when((first_row >= first_col) & (first_row < first_col + cols))
        def _():
            at = pl.multiple_of(first_row - first_col, rows)
            on_diagonal = iota((rows, rows), 0) == iota((rows, rows), 1)
            out_ref[:, pl.ds(at, rows)] += jnp.where(on_diagonal, reg_ref[...], 0.0)

    @pl.when(first_row < HEAD)
    def _():
        out_ref[...] = jnp.zeros_like(out_ref)

        @pl.when(first_col == 0)
        def _():
            out_ref[:, :HEAD] = factor_ref[...]


def multiply_part(part, parts, place, own, other, theirs, right, factor, regular, out):
    steps = own[0].shape[0]
    rows = 2 * HALF
    epochs, cols = right.shape

    def reg_block(i, place):
        block = lax.rem(place[PLACE_COL] + part, parts) * steps + i
        return 0, place[PLACE_ROW] * parts * steps + block

    def out_block(i, place):
        return lax.rem(place[PLACE_COL] + part, parts) * steps + i, 0

    def shards_spec(array):
        return pl.BlockSpec((array.shape[0], 1, HALF, LANES), lambda i, place: (0, i, 0, 0))

    operands = [*own, *other]
    in_specs = [pl.BlockSpec((1, HALF, LANES), lambda i, place: (i, 0, 0)), shards_spec(own[1])]
    in_specs += [pl.BlockSpec((1, 1, HALF, LANES), lambda i, place: (part, i, 0, 0))]
    in_specs += [shards_spec(other[1])]
    if part == 0:
        operands.append(theirs)
        in_specs.append(shards_spec(theirs))
    operands += [right, factor, regular.reshape(1, -1)]
    in_specs += [fixed(right), fixed(factor), pl.BlockSpec((1, rows), reg_block)]
    if part:
        operands.append(out)
        in_specs.append(ANY)
    return pl.pallas_call(
        functools.partial(tile_kernel, part, parts),
        out_shape=jax.ShapeDtypeStruct((parts * steps * rows, cols), F32),
        grid_spec=pltpu.PrefetchScalarGridSpec(
            num_scalar_prefetch=1,
            grid=(steps,),
            in_specs=in_specs,
            out_specs=pl.BlockSpec((rows, cols), out_block),
            scratch_shapes=[
                pltpu.VMEM((epochs // (LANES // 2), HALF, LANES), BF16),
                pltpu.VMEM((rows, epochs), BF16),
            ],
        ),
        input_output_aliases={len(operands): 0} if part else {},
        compiler_params=MIDDLE,
        cost_estimate=FREE,
        name="multiply_part",
    )(place, *operands)


AXES = ("ep", "row", "col")


def sizes():
    return tuple(lax.axis_size(axis) for axis in AXES)


def flat(ep, row, col):
    _, rows, cols = sizes()
    return (ep * rows + row) * cols + col


def doubling(count, least):
    distances = []
    distance = count // 2
    while distance >= least:
        distances.append(distance)
        distance //= 2
    return distances


def spread_step(block, owner_of, distance):
    eps, rows, cols = sizes()
    route = []
    for e in range(eps):
        for c in range(cols):
            for other in range(0, rows, 2 * distance):
                source = owner_of(e, c) ^ other
                route.append((flat(e, source, c), flat(e, source ^ distance, c)))
    return lax.ppermute(block, AXES, route)


def panel_hops():
    eps, _, cols = sizes()
    return [(d, 0) for d in doubling(eps, 1)] + [(0, d) for d in reversed(doubling(cols, 1))]


def gather_panel(note):
    eps, rows, cols = sizes()
    row = lax.axis_index("row")
    for distance in doubling(rows, 2):
        came = spread_step(note, lambda e, c: 0, distance)
        note = jnp.where((row & (2 * distance - 1)) == distance, came, note)
    for de, dc in panel_hops():
        route = [
            (flat(e, r, c), flat(e ^ de, r, c ^ dc))
            for e in range(eps)
            for r in range(0, rows, 2)
            for c in range(cols)
        ]
        note = jnp.concatenate([note, lax.ppermute(note, AXES, route)])
    came = lax.ppermute(note, "row", [(r, r + 1) for r in range(0, rows, 2)])
    return note, came


def on_device(design, taps, tap_count, order, regular):
    rows_dev = design.shape[1]
    eps, rows, cols = sizes()
    cols_dev = regular.shape[0] // (eps * cols)
    parts = rows_dev // cols_dev
    row, ep, col = (lax.axis_index(axis) for axis in ("row", "ep", "col"))
    group = lax.axis_index(("ep", "col"))
    everywhere = [(e, r, c) for e in range(eps) for r in range(rows) for c in range(cols)]
    owner = lambda e, c: (e * cols + c) * cols_dev // rows_dev
    inside = lambda r, c: c // parts == (r * parts % cols) // parts
    owns = lambda e, r, c: inside(r, c) & (r * parts // cols == e)
    first_owner = group * cols_dev // rows_dev
    takes = ((row ^ first_owner) & 1) == 1
    home = row * parts // cols == ep
    back = [(col - n) % cols for n in range(cols)]
    place = [row, group, ep, col, takes, owns(ep, row, col), home, *back]
    chain = len(place)
    steps = [(0, 0)]
    for de, dc in panel_hops():
        steps += [(e ^ de, c ^ dc) for e, c in steps]
    place += [(ep ^ de) * cols + (col ^ dc) for de, dc in steps]
    place = jnp.stack([jnp.asarray(p, jnp.int32) for p in place])

    *local, both, note = permute_local(place, design, order, tap_count, cols_dev)

    def shift(block, n):
        route = [(flat(e, r, (c - n) % cols), flat(e, r, c)) for e, r, c in everywhere]
        return lax.ppermute(block, AXES, route)

    def across(block, wanted):
        route = [(flat(1 - e, r, c), flat(e, r, c)) for e, r, c in everywhere if wanted(e, r, c)]
        return lax.ppermute(block, AXES, route)

    distances = doubling(rows, 1)

    def trade(block):
        route = [
            (flat(e, r, c), flat(e, r ^ distances[0], c)) for e, r, c in everywhere if inside(r, c)
        ]
        return lax.ppermute(block, AXES, route)

    def spread_rest(block):
        for distance in distances[1:-1]:
            got = spread_step(block, owner, distance)
            hit = ((row ^ first_owner) & (2 * distance - 1)) == distance
            block = jnp.where(hit, got, block)
        return block, spread_step(block, owner, distances[-1])

    notes, came = gather_panel(note)
    early = [shift(local[n % parts], n) for n in range(1, cols)]
    swapped = across(both, lambda e, r, c: True)
    band, taper, aug = start_panel(place, chain, taps, notes, came, regular, notes)
    aug = next_panel(1, aug, aug)
    rest, *local, first = assemble(place, early, local, [aug, swapped], True)
    foreign = trade(first)
    others = [across(rest, lambda e, r, c: not owns(e, r, c))]
    mine = [rest]
    order = [(j, n) for j in range(1, parts) for n in range(1, cols)]
    late = [shift(local[(n + j) % parts], n) for j, n in order]
    aug = next_panel(2, aug, first)
    foreign, *late[:1] = gate([foreign, *late[:1]], aug)
    own, sent = sort(place, first, foreign)
    theirs = across(sent, lambda e, r, c: inside(r, c))
    factor, w, high, low = last_panel(3, aug, own, taper)
    theirs, others[0], *late[1:] = gate([theirs, others[0], *late[1:]], factor)
    own, own_came = spread_rest(own)
    other, other_came = spread_rest(theirs)
    for j in range(1, parts):
        shards = late[(j - 1) * (cols - 1) : j * (cols - 1)]
        (whole,) = assemble(place, shards, [], [factor], False)
        mine.append(whole)
        others.append(across(whole, lambda e, r, c: True))
    right = project(place, own, own_came, other, other_came, w, high, low, band)
    out = None
    for j in range(parts):
        out = multiply_part(
            j, parts, place, (local[j], mine[j]), (swapped, others[j]), theirs, right, factor,
            regular, out,
        )
    return out


def solution(mesh):
    in_specs = (P(("ep", "col"), "row"), P(), P(("ep", "col")), P("row"), P())
    out_specs = P("row", ("ep", "col"))
    return jax.shard_map(
        on_device, mesh=mesh, in_specs=in_specs, out_specs=out_specs, check_vma=False
    )
```

```python
import functools

import jax
import jax.numpy as jnp
from jax import lax
from jax.experimental import pallas as pl
from jax.experimental.pallas import tpu as pltpu
from jax.sharding import PartitionSpec as P

PANEL = 256
SECTIONS = 2
HEAD = PANEL * SECTIONS
PB = 128
LANES = 128
BLOCK = 128
HALF = 256
SUB = 8
NOTE = 16
EXACT = lax.Precision.HIGHEST
F32 = jnp.float32
BF16 = jnp.bfloat16


def iota(shape, axis):
    return lax.broadcasted_iota(jnp.int32, shape, axis)


def dot(left, right, contract=((1,), (0,)), precision=None):
    return lax.dot_general(
        left, right, (contract, ((), ())), preferred_element_type=F32, precision=precision
    )


NT = ((1,), (1,))
TN = ((0,), (0,))
VMEM = pl.BlockSpec(memory_space=pltpu.VMEM)
SMEM = pl.BlockSpec(memory_space=pltpu.SMEM)
ANY = pl.BlockSpec(memory_space=pl.ANY)
FREE = pl.CostEstimate(flops=0, bytes_accessed=0, transcendentals=0)
LIMIT = pltpu.CompilerParams(vmem_limit_bytes=24 << 20)
MIDDLE = pltpu.CompilerParams(vmem_limit_bytes=32 << 20)
WIDE = pltpu.CompilerParams(vmem_limit_bytes=58 << 20)


def permute_kernel(place_ref, *refs):
    sources, refs = refs[:3], refs[3:]
    *part_refs, both_ref, note_ref = refs[:-4]
    order_ref, counts_ref, design_ref = targets = refs[-4:-1]
    copies = [
        pltpu.make_async_copy(source, target, refs[-1].at[n])
        for n, (source, target) in enumerate(zip(sources, targets))
    ]
    for copy in copies:
        copy.start()
    for copy in copies:
        copy.wait()
    epochs = design_ref.shape[0]
    parts, per_part = len(part_refs), part_refs[0].shape[0]
    lane = iota((PB, PB), 1).astype(F32)
    none = jnp.zeros((epochs, PB), BF16)
    groups = 2 * HALF // PB

    def packed(local, columns, block, part):
        first = block * groups + part
        second = first + HALF // PB
        pick = [jnp.where(local[:, g : g + 1] == lane, 1.0, 0.0) for g in (first, second)]
        pick = jnp.concatenate(pick, axis=1).astype(BF16)
        top = jnp.concatenate([columns(first), none], axis=1)
        low = jnp.concatenate([none, columns(second)], axis=1)
        return dot(pick, jnp.concatenate([top, low], axis=0), NT).astype(BF16)

    def order_of(rows):
        return (order_ref[rows, :] & (PB - 1)).astype(F32).T

    local = order_of(slice(0, per_part * groups))
    for part in range(HALF // PB):
        columns = lambda g: design_ref[:, g * PB : (g + 1) * PB]
        note_ref[0, part * PB : (part + 1) * PB, :] = packed(local, columns, 0, part)
    counts = counts_ref[...].astype(F32)
    counts = jnp.concatenate([counts] * (LANES // epochs), axis=1)
    note_ref[0, HALF:, :] = jnp.broadcast_to(counts, (NOTE, LANES)).astype(BF16)
    for j in range(parts):
        piece = lax.rem(place_ref[PLACE_COL] + j, parts)
        at = pl.multiple_of(piece * per_part * groups, per_part * groups)
        local = order_of(pl.ds(at, per_part * groups))
        columns = lambda g: design_ref[:, pl.ds(pl.multiple_of((at + g) * PB, PB), PB)]
        for block in range(per_part):
            for part in range(HALF // PB):
                rows = slice(part * PB, (part + 1) * PB)
                part_refs[j][block, rows, :] = packed(local, columns, block, part)
        both_ref[j] = part_refs[j][...]


def permute_local(place, design, order, tap_count, cols_dev):
    epochs, rows = design.shape
    parts, per_part = rows // cols_dev, cols_dev // (2 * HALF)
    piece = jax.ShapeDtypeStruct((per_part, HALF, LANES), BF16)
    both = jax.ShapeDtypeStruct((parts,) + piece.shape, BF16)
    note = jax.ShapeDtypeStruct((1, HALF + NOTE, LANES), BF16)
    return pl.pallas_call(
        permute_kernel,
        out_shape=(piece,) * parts + (both, note),
        in_specs=[SMEM] + [ANY] * 3,
        out_specs=(VMEM,) * (parts + 2),
        scratch_shapes=[
            pltpu.VMEM((rows // PB, PB), jnp.int32),
            pltpu.VMEM((1, epochs), jnp.int32),
            pltpu.VMEM((epochs, rows), BF16),
            pltpu.SemaphoreType.DMA((3,)),
        ],
        compiler_params=WIDE,
        name="permute_local",
    )(place, order.reshape(rows // PB, PB), tap_count.reshape(1, epochs), design)


PLACE_ROW, PLACE_GROUP, PLACE_EP, PLACE_COL, PLACE_TAKES, PLACE_OWNS, PLACE_HOME, PLACE_BACK = range(8)


def assemble_kernel(count, gated, after, whole, place_ref, *refs):
    shards, kept = refs[:count], refs[count : count + gated]
    out_refs, sem = refs[count + gated + after : -1], refs[-1]
    copies = [(shard, out_refs[0].at[n]) for n, shard in enumerate(shards)]
    if whole:
        copies += [(shard, out_refs[-1].at[n]) for n, shard in enumerate([kept[0], *shards])]
    copies = [pltpu.make_async_copy(a, b, sem.at[n]) for n, (a, b) in enumerate(copies)]
    for copy in copies:
        copy.start()
    for copy in copies:
        copy.wait()


def assemble(place, shards, gated, after, whole):
    count = len(shards)
    out_shape = [jax.ShapeDtypeStruct((count,) + shards[0].shape, BF16)]
    out_shape += [jax.ShapeDtypeStruct(g.shape, g.dtype) for g in gated]
    if whole:
        out_shape.append(jax.ShapeDtypeStruct((count + 1,) + shards[0].shape, BF16))
    return pl.pallas_call(
        functools.partial(assemble_kernel, count, len(gated), len(after), whole),
        out_shape=out_shape,
        in_specs=[SMEM] + [ANY] * (count + len(gated) + len(after)),
        out_specs=[ANY] * len(out_shape),
        input_output_aliases={1 + count + n: 1 + n for n in range(len(gated))},
        scratch_shapes=[pltpu.SemaphoreType.DMA((2 * count + 1,))],
        compiler_params=LIMIT,
        cost_estimate=FREE,
        name="assemble",
    )(place, *shards, *gated, *after)


def sort_kernel(place_ref, native_ref, foreign_ref, keep_ref, send_ref, sem):
    def copy(kept, sent):
        copies = [
            pltpu.make_async_copy(kept, keep_ref, sem.at[0]),
            pltpu.make_async_copy(sent, send_ref, sem.at[1]),
        ]
        for c in copies:
            c.start()
        for c in copies:
            c.wait()

    choose(
        place_ref[PLACE_HOME] != 0,
        lambda: copy(native_ref, foreign_ref),
        lambda: copy(foreign_ref, native_ref),
    )


def sort(place, native, foreign):
    shape = jax.ShapeDtypeStruct(native.shape, BF16)
    return pl.pallas_call(
        sort_kernel,
        out_shape=(shape, shape),
        in_specs=[SMEM, ANY, ANY],
        out_specs=(ANY, ANY),
        scratch_shapes=[pltpu.SemaphoreType.DMA((2,))],
        compiler_params=LIMIT,
        cost_estimate=FREE,
        name="sort",
    )(place, native, foreign)


def gate(arrays, after):
    count = len(arrays)
    return pl.pallas_call(
        lambda *refs: None,
        out_shape=tuple(jax.ShapeDtypeStruct(x.shape, x.dtype) for x in arrays),
        in_specs=[ANY] * (count + 1),
        out_specs=(ANY,) * count,
        input_output_aliases={n: n for n in range(count)},
        compiler_params=LIMIT,
        cost_estimate=FREE,
        name="gate",
    )(*arrays, after)


def filter_rows(blocks, band_ref, store):
    for b in range(band_ref.shape[0]):
        first = max(2 * b - 1, 0)
        skip = 0 if b else LANES
        packed = jnp.concatenate([blocks(e) for e in range(first, 2 * b + 2)], axis=1)
        got = dot(packed, band_ref[b, skip:, :]).astype(BF16)
        for half in range(2):
            across = slice(half * LANES, (half + 1) * LANES)
            store(slice(half * HALF, (half + 1) * HALF), slice(b * LANES, (b + 1) * LANES), got[:, across])


def spread(tile, lane):
    return jnp.broadcast_to(tile[:, lane : lane + 1], (SUB, tile.shape[1]))


def row_of(tile, k):
    return jnp.broadcast_to(tile[k : k + 1, :], (SUB, tile.shape[1]))


def factor_block(work):
    groups = BLOCK // SUB
    sub, lane = iota((SUB, BLOCK), 0), iota((SUB, BLOCK), 1)
    tiles = [work[g * SUB : (g + 1) * SUB, :] for g in range(groups)]
    for g in range(groups):
        inside = (lane >= g * SUB) & (lane < (g + 1) * SUB)
        cols = [spread(tiles[g], g * SUB + j) for j in range(SUB)]
        a = {(i, j): row_of(cols[j], i) for j in range(SUB) for i in range(j, SUB)}
        own = jnp.where(inside, jnp.where(lane - g * SUB == sub, 1.0, 0.0), tiles[g])
        u = [row_of(own, k) for k in range(SUB)]
        inv = []
        low = {}
        for k in range(SUB):
            r = lax.rsqrt(a[k, k])
            inv.append(r)
            for i in range(k + 1, SUB):
                low[i, k] = a[i, k] * r
            for j in range(k + 1, SUB):
                for i in range(j, SUB):
                    a[i, j] = a[i, j] - low[i, k] * low[j, k]
            u[k] = u[k] * r
            for j in range(k + 1, SUB):
                u[j] = u[j] - low[j, k] * u[k]
        for t in range(g + 1, groups):
            left = [spread(tiles[t], g * SUB + j) for j in range(SUB)]
            tile = jnp.where(inside, 0.0, tiles[t])
            for k in range(SUB):
                left[k] = left[k] * inv[k]
                for j in range(k + 1, SUB):
                    left[j] = left[j] - low[j, k] * left[k]
                tile = tile - left[k] * u[k]
            tiles[t] = tile
        merged = u[0]
        for k in range(1, SUB):
            merged = jnp.where(sub == k, u[k], merged)
        work[g * SUB : (g + 1) * SUB, :] = jnp.where(lane < (g + 1) * SUB, merged, 0.0)


def start_kernel(
    chain, place_ref, taps_ref, own_ref, came_ref, reg_ref, after, band_ref, taper_ref, aug_ref, notes, a1,
    work,
):
    del after
    epochs = aug_ref.shape[1] - HEAD
    half = LANES // 2

    @pl.when(place_ref[0] % 2 == 0)
    def _():
        for rel in range(own_ref.shape[0]):
            notes[place_ref[chain + rel]] = own_ref[rel]

    @pl.when(place_ref[0] % 2 == 1)
    def _():
        for rel in range(own_ref.shape[0]):
            notes[place_ref[chain + rel]] = came_ref[rel]

    shape = (half, LANES)
    lag = iota(shape, 1) - iota(shape, 0)
    base = lax.fori_loop(
        0,
        taps_ref.shape[0],
        lambda k, kept: jnp.where(lag == k, taps_ref[k], kept),
        jnp.zeros(shape, F32),
    )
    lane = iota(shape, 1)
    swapped = jnp.concatenate([base[:, half:], base[:, :half]], axis=1)
    patterns = (jnp.where(lane < half, swapped, 0.0), base, jnp.where(lane >= half, swapped, 0.0))
    row = iota((1, LANES), 1)
    sources = epochs // half
    counts = [notes[e, HALF : HALF + NOTE, :].astype(F32)[:1] for e in range(sources)]
    counts.append(jnp.zeros_like(counts[0]))
    band_ref[...] = jnp.zeros_like(band_ref)
    for e in range(sources):
        limit = jnp.where(row < half, counts[e], counts[e + 1])
        taper_ref[e] = jnp.where(lag.astype(F32) < limit, base, 0.0).astype(BF16)
    for b in range(epochs // LANES):
        limit = jnp.where(row < half, counts[2 * b], counts[2 * b + 1])
        for j, pattern in enumerate(patterns):
            at = (lag + half - half * j).astype(F32)
            kept = jnp.where(at < limit, pattern, 0.0).astype(BF16)
            for h in range(2):
                rows = slice(j * LANES + h * half, j * LANES + (h + 1) * half)
                band_ref[b, rows, h * LANES : (h + 1) * LANES] = kept

    def store(rows, cols, got):
        a1[rows, cols] = got

    filter_rows(lambda e: notes[e, :HALF, :], band_ref, store)
    columns = a1[...]
    square = (HEAD, HEAD)
    on_diagonal = iota(square, 0) == iota(square, 1)
    aug_ref[:, :HEAD] = dot(columns, columns, NT) + jnp.where(on_diagonal, reg_ref[:, :HEAD], 0.0)
    aug_ref[:, HEAD:] = columns.astype(F32)
    eliminate(aug_ref, 0, work)


def eliminate(aug, kb, work):
    here = slice(kb * BLOCK, (kb + 1) * BLOCK)
    work[...] = aug[here, here]
    factor_block(work)
    rest = slice(kb * BLOCK, aug.shape[1])
    aug[here, rest] = dot(work[...], aug[here, rest], precision=EXACT)
    for rb in range(kb + 1, HEAD // BLOCK):
        below = slice(rb * BLOCK, (rb + 1) * BLOCK)
        rest = slice(rb * BLOCK, aug.shape[1])
        aug[below, rest] -= dot(aug[here, below], aug[here, rest], TN, precision=EXACT)


def next_kernel(kb, aug_in, after, aug_ref, work):
    del after
    aug_ref[...] = aug_in[...]
    eliminate(aug_ref, kb, work)


def last_kernel(kb, aug_in, after, taper_ref, factor_ref, w_ref, high_ref, low_ref, aug, work, high, low):
    del after
    aug[...] = aug_in[...]
    eliminate(aug, kb, work)
    square = (HEAD, HEAD)
    epochs = aug.shape[1] - HEAD
    factor_ref[...] = jnp.where(iota(square, 0) >= iota(square, 1), aug[:, :HEAD].T, 0.0)
    wt = aug[:, HEAD:]

    def keep(rows, cols, values):
        top = values.astype(BF16)
        high[rows, cols] = top
        low[rows, cols] = (values - top.astype(F32)).astype(BF16)

    keep(slice(None), slice(epochs, None), wt.T)
    for b in range(epochs // BLOCK):
        here = slice(b * BLOCK, (b + 1) * BLOCK)
        shape = (BLOCK, epochs)
        unit = jnp.where(iota(shape, 0) + b * BLOCK == iota(shape, 1), 1.0, 0.0)
        keep(here, slice(0, epochs), unit - dot(wt[:, here], wt, TN, precision=lax.Precision.HIGH))
    count, half = taper_ref.shape[:2]
    for e in range(count):
        reach = min(LANES, epochs - e * half)
        rows = slice(e * half, e * half + reach)
        taper = taper_ref[e, :, :reach]
        got = dot(taper, high[rows, :]) + dot(taper, low[rows, :])
        here = slice(e * half, (e + 1) * half)
        w_ref[here, :] = got[:, epochs:].astype(BF16)
        top = got[:, :epochs].astype(BF16)
        high_ref[here, :] = top
        low_ref[here, :] = (got[:, :epochs] - top.astype(F32)).astype(BF16)


def start_panel(place, chain, taps, own, came, regular, after):
    epochs = own.shape[0] * (LANES // 2)
    half = LANES // 2
    return pl.pallas_call(
        functools.partial(start_kernel, chain),
        out_shape=(
            jax.ShapeDtypeStruct((epochs // LANES, 3 * LANES, 2 * LANES), BF16),
            jax.ShapeDtypeStruct((epochs // half, half, LANES), BF16),
            jax.ShapeDtypeStruct((HEAD, HEAD + epochs), F32),
        ),
        in_specs=[SMEM, SMEM, VMEM, VMEM, VMEM, ANY],
        out_specs=(VMEM,) * 3,
        scratch_shapes=[
            pltpu.VMEM(own.shape, BF16),
            pltpu.VMEM((HEAD, epochs), BF16),
            pltpu.VMEM((BLOCK, BLOCK), F32),
        ],
        compiler_params=LIMIT,
        cost_estimate=FREE,
        name="start_panel",
    )(place, taps, own, came, regular.reshape(1, -1), after)


def next_panel(kb, aug, after):
    return pl.pallas_call(
        functools.partial(next_kernel, kb),
        out_shape=jax.ShapeDtypeStruct(aug.shape, F32),
        in_specs=[VMEM, ANY],
        out_specs=VMEM,
        scratch_shapes=[pltpu.VMEM((BLOCK, BLOCK), F32)],
        compiler_params=LIMIT,
        cost_estimate=FREE,
        name="next_panel",
    )(aug, after)


def last_panel(kb, aug, after, taper):
    epochs = aug.shape[1] - HEAD
    return pl.pallas_call(
        functools.partial(last_kernel, kb),
        out_shape=(
            jax.ShapeDtypeStruct((HEAD, HEAD), F32),
            jax.ShapeDtypeStruct((epochs, HEAD), BF16),
            jax.ShapeDtypeStruct((epochs, epochs), BF16),
            jax.ShapeDtypeStruct((epochs, epochs), BF16),
        ),
        in_specs=[VMEM, ANY, VMEM],
        out_specs=(VMEM,) * 4,
        scratch_shapes=[
            pltpu.VMEM(aug.shape, F32),
            pltpu.VMEM((BLOCK, BLOCK), F32),
            pltpu.VMEM((epochs, epochs + HEAD), BF16),
            pltpu.VMEM((epochs, epochs + HEAD), BF16),
        ],
        compiler_params=LIMIT,
        cost_estimate=FREE,
        name="last_panel",
    )(aug, after, taper)


def shards_of(ref, block):
    return [ref.at[n, block] for n in range(ref.shape[0])]


def unpack(place_ref, own, other, blocks):
    width = len(own)
    here = place_ref[PLACE_EP] * width
    there = width - here
    for n in range(width):
        back = place_ref[PLACE_BACK + n]
        blocks[here + back] = own[n][...]
        blocks[there + back] = other[n][...]


def choose(condition, yes, no):
    pl.when(condition)(yes)
    pl.when(jnp.logical_not(condition))(no)


def fixed(array):
    return pl.BlockSpec(
        array.shape, lambda i, place: (0,) * array.ndim, pipeline_mode=pl.Buffered(1)
    )


def project_kernel(
    place_ref, own, own_came, other, other_came, w_ref, high_ref, low_ref, band_ref, right_ref,
    both, blocks, columns, sem,
):
    def bring(sources):
        copies = [
            pltpu.make_async_copy(source, both.at[n], sem.at[n]) for n, source in enumerate(sources)
        ]
        for copy in copies:
            copy.start()
        for copy in copies:
            copy.wait()

    choose(
        place_ref[PLACE_TAKES] != 0,
        lambda: bring((own_came, other_came)),
        lambda: bring((own, other)),
    )

    def store(rows, cols, got):
        columns[rows, cols] = got

    rows = 2 * HALF
    for n in range(right_ref.shape[1] // rows):
        unpack(place_ref, shards_of(both.at[0], n), shards_of(both.at[1], n), blocks)
        filter_rows(lambda e: blocks[e], band_ref, store)
        wanted = columns[...]
        projected = dot(high_ref[...], wanted, NT) + dot(low_ref[...], wanted, NT)
        right_ref[:, n * rows : (n + 1) * rows] = projected.astype(BF16)

    @pl.when(place_ref[PLACE_GROUP] == 0)
    def _():
        right_ref[:, :HEAD] = w_ref[...]


def project(place, own, own_came, other, other_came, w, high, low, band):
    width, count = own.shape[:2]
    epochs = high.shape[0]
    return pl.pallas_call(
        project_kernel,
        out_shape=jax.ShapeDtypeStruct((epochs, count * 2 * HALF), BF16),
        in_specs=[SMEM] + [ANY] * 4 + [VMEM] * 4,
        out_specs=VMEM,
        scratch_shapes=[
            pltpu.VMEM((2,) + own.shape, BF16),
            pltpu.VMEM((2 * width, HALF, LANES), BF16),
            pltpu.VMEM((2 * HALF, epochs), BF16),
            pltpu.SemaphoreType.DMA((2,)),
        ],
        compiler_params=LIMIT,
        cost_estimate=FREE,
        name="project",
    )(place, own, own_came, other, other_came, w, high, low, band)


def tile_kernel(part, parts, place_ref, own_first, own_rest, other_first, other_rest, *refs):
    theirs_ref = refs[0]
    right_ref, factor_ref, reg_ref = refs[:3] if part else refs[1:4]
    out_ref, blocks, lhs = refs[-3:]
    i, steps = pl.program_id(0), pl.num_programs(0)
    rows, cols = out_ref.shape
    half = LANES // 2
    block = lax.rem(place_ref[PLACE_COL] + part, parts) * steps + i
    first_row = (place_ref[PLACE_ROW] * parts * steps + block) * rows
    first_col = place_ref[PLACE_GROUP] * cols

    @pl.when(first_row >= HEAD)
    def _():
        mine = [own_first.at[0], *shards_of(own_rest, 0)]
        others = [other_first.at[0, 0], *shards_of(other_rest, 0)]
        if part == 0:
            choose(
                place_ref[PLACE_OWNS] != 0,
                lambda: unpack(place_ref, mine, shards_of(theirs_ref, 0), blocks),
                lambda: unpack(place_ref, mine, others, blocks),
            )
        else:
            unpack(place_ref, mine, others, blocks)
        for pair in range(lhs.shape[1] // LANES):
            even, odd = blocks[2 * pair], blocks[2 * pair + 1]
            across = slice(pair * LANES, (pair + 1) * LANES)
            lhs[:HALF, across] = jnp.concatenate([even[:, :half], odd[:, :half]], axis=1)
            lhs[HALF:, across] = jnp.concatenate([even[:, half:], odd[:, half:]], axis=1)
        out_ref[...] = dot(lhs[...], right_ref[...])

        @pl.when((first_row >= first_col) & (first_row < first_col + cols))
        def _():
            at = pl.multiple_of(first_row - first_col, rows)
            on_diagonal = iota((rows, rows), 0) == iota((rows, rows), 1)
            out_ref[:, pl.ds(at, rows)] += jnp.where(on_diagonal, reg_ref[...], 0.0)

    @pl.when(first_row < HEAD)
    def _():
        out_ref[...] = jnp.zeros_like(out_ref)

        @pl.when(first_col == 0)
        def _():
            out_ref[:, :HEAD] = factor_ref[...]


def multiply_part(part, parts, place, own, other, theirs, right, factor, regular, out):
    steps = own[0].shape[0]
    rows = 2 * HALF
    epochs, cols = right.shape

    def reg_block(i, place):
        block = lax.rem(place[PLACE_COL] + part, parts) * steps + i
        return 0, place[PLACE_ROW] * parts * steps + block

    def out_block(i, place):
        return lax.rem(place[PLACE_COL] + part, parts) * steps + i, 0

    def shards_spec(array):
        return pl.BlockSpec((array.shape[0], 1, HALF, LANES), lambda i, place: (0, i, 0, 0))

    operands = [*own, *other]
    in_specs = [pl.BlockSpec((1, HALF, LANES), lambda i, place: (i, 0, 0)), shards_spec(own[1])]
    in_specs += [pl.BlockSpec((1, 1, HALF, LANES), lambda i, place: (part, i, 0, 0))]
    in_specs += [shards_spec(other[1])]
    if part == 0:
        operands.append(theirs)
        in_specs.append(shards_spec(theirs))
    operands += [right, factor, regular.reshape(1, -1)]
    in_specs += [fixed(right), fixed(factor), pl.BlockSpec((1, rows), reg_block)]
    if part:
        operands.append(out)
        in_specs.append(ANY)
    return pl.pallas_call(
        functools.partial(tile_kernel, part, parts),
        out_shape=jax.ShapeDtypeStruct((parts * steps * rows, cols), F32),
        grid_spec=pltpu.PrefetchScalarGridSpec(
            num_scalar_prefetch=1,
            grid=(steps,),
            in_specs=in_specs,
            out_specs=pl.BlockSpec((rows, cols), out_block),
            scratch_shapes=[
                pltpu.VMEM((epochs // (LANES // 2), HALF, LANES), BF16),
                pltpu.VMEM((rows, epochs), BF16),
            ],
        ),
        input_output_aliases={len(operands): 0} if part else {},
        compiler_params=MIDDLE,
        cost_estimate=FREE,
        name="multiply_part",
    )(place, *operands)


AXES = ("ep", "row", "col")


def sizes():
    return tuple(lax.axis_size(axis) for axis in AXES)


def flat(ep, row, col):
    _, rows, cols = sizes()
    return (ep * rows + row) * cols + col


def doubling(count, least):
    distances = []
    distance = count // 2
    while distance >= least:
        distances.append(distance)
        distance //= 2
    return distances


def spread_step(block, owner_of, distance):
    eps, rows, cols = sizes()
    route = []
    for e in range(eps):
        for c in range(cols):
            for other in range(0, rows, 2 * distance):
                source = owner_of(e, c) ^ other
                route.append((flat(e, source, c), flat(e, source ^ distance, c)))
    return lax.ppermute(block, AXES, route)


def panel_hops():
    eps, _, cols = sizes()
    return [(d, 0) for d in doubling(eps, 1)] + [(0, d) for d in reversed(doubling(cols, 1))]


def gather_panel(note):
    eps, rows, cols = sizes()
    row = lax.axis_index("row")
    for distance in doubling(rows, 2):
        came = spread_step(note, lambda e, c: 0, distance)
        note = jnp.where((row & (2 * distance - 1)) == distance, came, note)
    for de, dc in panel_hops():
        route = [
            (flat(e, r, c), flat(e ^ de, r, c ^ dc))
            for e in range(eps)
            for r in range(0, rows, 2)
            for c in range(cols)
        ]
        note = jnp.concatenate([note, lax.ppermute(note, AXES, route)])
    came = lax.ppermute(note, "row", [(r, r + 1) for r in range(0, rows, 2)])
    return note, came


def on_device(design, taps, tap_count, order, regular):
    rows_dev = design.shape[1]
    eps, rows, cols = sizes()
    cols_dev = regular.shape[0] // (eps * cols)
    parts = rows_dev // cols_dev
    row, ep, col = (lax.axis_index(axis) for axis in ("row", "ep", "col"))
    group = lax.axis_index(("ep", "col"))
    everywhere = [(e, r, c) for e in range(eps) for r in range(rows) for c in range(cols)]
    owner = lambda e, c: (e * cols + c) * cols_dev // rows_dev
    inside = lambda r, c: c // parts == (r * parts % cols) // parts
    owns = lambda e, r, c: inside(r, c) & (r * parts // cols == e)
    first_owner = group * cols_dev // rows_dev
    takes = ((row ^ first_owner) & 1) == 1
    home = row * parts // cols == ep
    back = [(col - n) % cols for n in range(cols)]
    place = [row, group, ep, col, takes, owns(ep, row, col), home, *back]
    chain = len(place)
    steps = [(0, 0)]
    for de, dc in panel_hops():
        steps += [(e ^ de, c ^ dc) for e, c in steps]
    place += [(ep ^ de) * cols + (col ^ dc) for de, dc in steps]
    place = jnp.stack([jnp.asarray(p, jnp.int32) for p in place])

    *local, both, note = permute_local(place, design, order, tap_count, cols_dev)

    def shift(block, n):
        route = [(flat(e, r, (c - n) % cols), flat(e, r, c)) for e, r, c in everywhere]
        return lax.ppermute(block, AXES, route)

    def across(block, wanted):
        route = [(flat(1 - e, r, c), flat(e, r, c)) for e, r, c in everywhere if wanted(e, r, c)]
        return lax.ppermute(block, AXES, route)

    distances = doubling(rows, 1)

    def trade(block):
        route = [
            (flat(e, r, c), flat(e, r ^ distances[0], c)) for e, r, c in everywhere if inside(r, c)
        ]
        return lax.ppermute(block, AXES, route)

    def spread_rest(block):
        for distance in distances[1:-1]:
            got = spread_step(block, owner, distance)
            hit = ((row ^ first_owner) & (2 * distance - 1)) == distance
            block = jnp.where(hit, got, block)
        return block, spread_step(block, owner, distances[-1])

    notes, came = gather_panel(note)
    early = [shift(local[n % parts], n) for n in range(1, cols)]
    swapped = across(both, lambda e, r, c: True)
    band, taper, aug = start_panel(place, chain, taps, notes, came, regular, notes)
    rest, *local, first = assemble(place, early, local, [aug, swapped], True)
    aug = next_panel(1, aug, first)
    foreign = trade(first)
    others = [across(rest, lambda e, r, c: not owns(e, r, c))]
    mine = [rest]
    order = [(j, n) for j in range(1, parts) for n in range(1, cols)]
    late = [shift(local[(n + j) % parts], n) for j, n in order]
    aug = next_panel(2, aug, first)
    foreign, others[0], *late[:2] = gate([foreign, others[0], *late[:2]], aug)
    own, sent = sort(place, first, foreign)
    theirs = across(sent, lambda e, r, c: inside(r, c))
    factor, w, high, low = last_panel(3, aug, own, taper)
    theirs, *late[2:] = gate([theirs, *late[2:]], factor)
    own, own_came = spread_rest(own)
    other, other_came = spread_rest(theirs)
    for j in range(1, parts):
        shards = late[(j - 1) * (cols - 1) : j * (cols - 1)]
        (whole,) = assemble(place, shards, [], [factor], False)
        mine.append(whole)
        others.append(across(whole, lambda e, r, c: True))
    right = project(place, own, own_came, other, other_came, w, high, low, band)
    out = None
    for j in range(parts):
        out = multiply_part(
            j, parts, place, (local[j], mine[j]), (swapped, others[j]), theirs, right, factor,
            regular, out,
        )
    return out


def solution(mesh):
    in_specs = (P(("ep", "col"), "row"), P(), P(("ep", "col")), P("row"), P())
    out_specs = P("row", ("ep", "col"))
    return jax.shard_map(
        on_device, mesh=mesh, in_specs=in_specs, out_specs=out_specs, check_vma=False
    )
```

```python
import functools

import jax
import jax.numpy as jnp
from jax import lax
from jax.experimental import pallas as pl
from jax.experimental.pallas import tpu as pltpu
from jax.sharding import PartitionSpec as P

PANEL = 256
SECTIONS = 2
HEAD = PANEL * SECTIONS
PB = 128
LANES = 128
BLOCK = 128
HALF = 256
SUB = 8
NOTE = 16
EXACT = lax.Precision.HIGHEST
F32 = jnp.float32
BF16 = jnp.bfloat16


def iota(shape, axis):
    return lax.broadcasted_iota(jnp.int32, shape, axis)


def dot(left, right, contract=((1,), (0,)), precision=None):
    return lax.dot_general(
        left, right, (contract, ((), ())), preferred_element_type=F32, precision=precision
    )


NT = ((1,), (1,))
TN = ((0,), (0,))
VMEM = pl.BlockSpec(memory_space=pltpu.VMEM)
SMEM = pl.BlockSpec(memory_space=pltpu.SMEM)
ANY = pl.BlockSpec(memory_space=pl.ANY)
FREE = pl.CostEstimate(flops=0, bytes_accessed=0, transcendentals=0)
LIMIT = pltpu.CompilerParams(vmem_limit_bytes=24 << 20)
MIDDLE = pltpu.CompilerParams(vmem_limit_bytes=32 << 20)
WIDE = pltpu.CompilerParams(vmem_limit_bytes=58 << 20)


def permute_kernel(*refs):
    sources, refs = refs[:3], refs[3:]
    *part_refs, both_ref, note_ref = refs[:-4]
    order_ref, counts_ref, design_ref = targets = refs[-4:-1]
    copies = [
        pltpu.make_async_copy(source, target, refs[-1].at[n])
        for n, (source, target) in enumerate(zip(sources, targets))
    ]
    for copy in copies:
        copy.start()
    for copy in copies:
        copy.wait()
    epochs = design_ref.shape[0]
    parts, per_part = len(part_refs), part_refs[0].shape[0]
    lane = iota((PB, PB), 1).astype(F32)
    none = jnp.zeros((epochs, PB), BF16)
    groups = 2 * HALF // PB

    def packed(local, columns, block, part):
        first = block * groups + part
        second = first + HALF // PB
        pick = [jnp.where(local[:, g : g + 1] == lane, 1.0, 0.0) for g in (first, second)]
        pick = jnp.concatenate(pick, axis=1).astype(BF16)
        top = jnp.concatenate([columns(first), none], axis=1)
        low = jnp.concatenate([none, columns(second)], axis=1)
        return dot(pick, jnp.concatenate([top, low], axis=0), NT).astype(BF16)

    def order_of(rows):
        return (order_ref[rows, :] & (PB - 1)).astype(F32).T

    local = order_of(slice(0, per_part * groups))
    for part in range(HALF // PB):
        columns = lambda g: design_ref[:, g * PB : (g + 1) * PB]
        note_ref[0, part * PB : (part + 1) * PB, :] = packed(local, columns, 0, part)
    counts = counts_ref[...].astype(F32)
    counts = jnp.concatenate([counts] * (LANES // epochs), axis=1)
    note_ref[0, HALF:, :] = jnp.broadcast_to(counts, (NOTE, LANES)).astype(BF16)
    for j in range(parts):
        piece = lax.rem(lax.axis_index("col") + j, parts)
        at = pl.multiple_of(piece * per_part * groups, per_part * groups)
        local = order_of(pl.ds(at, per_part * groups))
        columns = lambda g: design_ref[:, pl.ds(pl.multiple_of((at + g) * PB, PB), PB)]
        for block in range(per_part):
            for part in range(HALF // PB):
                rows = slice(part * PB, (part + 1) * PB)
                part_refs[j][block, rows, :] = packed(local, columns, block, part)
        both_ref[j] = part_refs[j][...]


def permute_local(design, order, tap_count, cols_dev):
    epochs, rows = design.shape
    parts, per_part = rows // cols_dev, cols_dev // (2 * HALF)
    piece = jax.ShapeDtypeStruct((per_part, HALF, LANES), BF16)
    both = jax.ShapeDtypeStruct((parts,) + piece.shape, BF16)
    note = jax.ShapeDtypeStruct((1, HALF + NOTE, LANES), BF16)
    return pl.pallas_call(
        permute_kernel,
        out_shape=(piece,) * parts + (both, note),
        in_specs=[ANY] * 3,
        out_specs=(VMEM,) * (parts + 2),
        scratch_shapes=[
            pltpu.VMEM((rows // PB, PB), jnp.int32),
            pltpu.VMEM((1, epochs), jnp.int32),
            pltpu.VMEM((epochs, rows), BF16),
            pltpu.SemaphoreType.DMA((3,)),
        ],
        compiler_params=WIDE,
        name="permute_local",
    )(order.reshape(rows // PB, PB), tap_count.reshape(1, epochs), design)


PLACE_ROW, PLACE_GROUP, PLACE_EP, PLACE_COL, PLACE_TAKES, PLACE_OWNS, PLACE_HOME, PLACE_BACK = range(8)


def assemble_kernel(count, gated, after, whole, place_ref, *refs):
    shards, kept = refs[:count], refs[count : count + gated]
    out_refs, sem = refs[count + gated + after : -1], refs[-1]
    copies = [(shard, out_refs[0].at[n]) for n, shard in enumerate(shards)]
    if whole:
        copies += [(shard, out_refs[-1].at[n]) for n, shard in enumerate([kept[0], *shards])]
    copies = [pltpu.make_async_copy(a, b, sem.at[n]) for n, (a, b) in enumerate(copies)]
    for copy in copies:
        copy.start()
    for copy in copies:
        copy.wait()


def assemble(place, shards, gated, after, whole):
    count = len(shards)
    out_shape = [jax.ShapeDtypeStruct((count,) + shards[0].shape, BF16)]
    out_shape += [jax.ShapeDtypeStruct(g.shape, g.dtype) for g in gated]
    if whole:
        out_shape.append(jax.ShapeDtypeStruct((count + 1,) + shards[0].shape, BF16))
    return pl.pallas_call(
        functools.partial(assemble_kernel, count, len(gated), len(after), whole),
        out_shape=out_shape,
        in_specs=[SMEM] + [ANY] * (count + len(gated) + len(after)),
        out_specs=[ANY] * len(out_shape),
        input_output_aliases={1 + count + n: 1 + n for n in range(len(gated))},
        scratch_shapes=[pltpu.SemaphoreType.DMA((2 * count + 1,))],
        compiler_params=LIMIT,
        cost_estimate=FREE,
        name="assemble",
    )(place, *shards, *gated, *after)


def sort_kernel(place_ref, native_ref, foreign_ref, keep_ref, send_ref, sem):
    def copy(kept, sent):
        copies = [
            pltpu.make_async_copy(kept, keep_ref, sem.at[0]),
            pltpu.make_async_copy(sent, send_ref, sem.at[1]),
        ]
        for c in copies:
            c.start()
        for c in copies:
            c.wait()

    choose(
        place_ref[PLACE_HOME] != 0,
        lambda: copy(native_ref, foreign_ref),
        lambda: copy(foreign_ref, native_ref),
    )


def sort(place, native, foreign):
    shape = jax.ShapeDtypeStruct(native.shape, BF16)
    return pl.pallas_call(
        sort_kernel,
        out_shape=(shape, shape),
        in_specs=[SMEM, ANY, ANY],
        out_specs=(ANY, ANY),
        scratch_shapes=[pltpu.SemaphoreType.DMA((2,))],
        compiler_params=LIMIT,
        cost_estimate=FREE,
        name="sort",
    )(place, native, foreign)


def gate(arrays, after):
    count = len(arrays)
    return pl.pallas_call(
        lambda *refs: None,
        out_shape=tuple(jax.ShapeDtypeStruct(x.shape, x.dtype) for x in arrays),
        in_specs=[ANY] * (count + 1),
        out_specs=(ANY,) * count,
        input_output_aliases={n: n for n in range(count)},
        compiler_params=LIMIT,
        cost_estimate=FREE,
        name="gate",
    )(*arrays, after)


def filter_rows(blocks, band_ref, store):
    for b in range(band_ref.shape[0]):
        first = max(2 * b - 1, 0)
        skip = 0 if b else LANES
        packed = jnp.concatenate([blocks(e) for e in range(first, 2 * b + 2)], axis=1)
        got = dot(packed, band_ref[b, skip:, :]).astype(BF16)
        for half in range(2):
            across = slice(half * LANES, (half + 1) * LANES)
            store(slice(half * HALF, (half + 1) * HALF), slice(b * LANES, (b + 1) * LANES), got[:, across])


def spread(tile, lane):
    return jnp.broadcast_to(tile[:, lane : lane + 1], (SUB, tile.shape[1]))


def row_of(tile, k):
    return jnp.broadcast_to(tile[k : k + 1, :], (SUB, tile.shape[1]))


def factor_block(work):
    groups = BLOCK // SUB
    sub, lane = iota((SUB, BLOCK), 0), iota((SUB, BLOCK), 1)
    tiles = [work[g * SUB : (g + 1) * SUB, :] for g in range(groups)]
    for g in range(groups):
        inside = (lane >= g * SUB) & (lane < (g + 1) * SUB)
        cols = [spread(tiles[g], g * SUB + j) for j in range(SUB)]
        a = {(i, j): row_of(cols[j], i) for j in range(SUB) for i in range(j, SUB)}
        own = jnp.where(inside, jnp.where(lane - g * SUB == sub, 1.0, 0.0), tiles[g])
        u = [row_of(own, k) for k in range(SUB)]
        inv = []
        low = {}
        for k in range(SUB):
            r = lax.rsqrt(a[k, k])
            inv.append(r)
            for i in range(k + 1, SUB):
                low[i, k] = a[i, k] * r
            for j in range(k + 1, SUB):
                for i in range(j, SUB):
                    a[i, j] = a[i, j] - low[i, k] * low[j, k]
            u[k] = u[k] * r
            for j in range(k + 1, SUB):
                u[j] = u[j] - low[j, k] * u[k]
        for t in range(g + 1, groups):
            left = [spread(tiles[t], g * SUB + j) for j in range(SUB)]
            tile = jnp.where(inside, 0.0, tiles[t])
            for k in range(SUB):
                left[k] = left[k] * inv[k]
                for j in range(k + 1, SUB):
                    left[j] = left[j] - low[j, k] * left[k]
                tile = tile - left[k] * u[k]
            tiles[t] = tile
        merged = u[0]
        for k in range(1, SUB):
            merged = jnp.where(sub == k, u[k], merged)
        work[g * SUB : (g + 1) * SUB, :] = jnp.where(lane < (g + 1) * SUB, merged, 0.0)


def start_kernel(
    chain, place_ref, taps_ref, own_ref, came_ref, reg_ref, after, band_ref, taper_ref, aug_ref, notes, a1,
    work,
):
    del after
    epochs = aug_ref.shape[1] - HEAD
    half = LANES // 2

    @pl.when(place_ref[0] % 2 == 0)
    def _():
        for rel in range(own_ref.shape[0]):
            notes[place_ref[chain + rel]] = own_ref[rel]

    @pl.when(place_ref[0] % 2 == 1)
    def _():
        for rel in range(own_ref.shape[0]):
            notes[place_ref[chain + rel]] = came_ref[rel]

    shape = (half, LANES)
    lag = iota(shape, 1) - iota(shape, 0)
    base = jnp.zeros(shape, F32)
    for k in range(taps_ref.shape[0]):
        base = jnp.where(lag == k, taps_ref[k], base)
    lane = iota(shape, 1)
    swapped = jnp.concatenate([base[:, half:], base[:, :half]], axis=1)
    patterns = (jnp.where(lane < half, swapped, 0.0), base, jnp.where(lane >= half, swapped, 0.0))
    row = iota((1, LANES), 1)
    sources = epochs // half
    counts = [notes[e, HALF : HALF + NOTE, :].astype(F32)[:1] for e in range(sources)]
    counts.append(jnp.zeros_like(counts[0]))
    band_ref[...] = jnp.zeros_like(band_ref)
    for e in range(sources):
        limit = jnp.where(row < half, counts[e], counts[e + 1])
        taper_ref[e] = jnp.where(lag.astype(F32) < limit, base, 0.0).astype(BF16)
    for b in range(epochs // LANES):
        limit = jnp.where(row < half, counts[2 * b], counts[2 * b + 1])
        for j, pattern in enumerate(patterns):
            at = (lag + half - half * j).astype(F32)
            kept = jnp.where(at < limit, pattern, 0.0).astype(BF16)
            for h in range(2):
                rows = slice(j * LANES + h * half, j * LANES + (h + 1) * half)
                band_ref[b, rows, h * LANES : (h + 1) * LANES] = kept

    def store(rows, cols, got):
        a1[rows, cols] = got

    filter_rows(lambda e: notes[e, :HALF, :], band_ref, store)
    columns = a1[...]
    square = (HEAD, HEAD)
    on_diagonal = iota(square, 0) == iota(square, 1)
    aug_ref[:, :HEAD] = dot(columns, columns, NT) + jnp.where(on_diagonal, reg_ref[:, :HEAD], 0.0)
    aug_ref[:, HEAD:] = columns.astype(F32)
    eliminate(aug_ref, 0, work)


def eliminate(aug, kb, work):
    here = slice(kb * BLOCK, (kb + 1) * BLOCK)
    work[...] = aug[here, here]
    factor_block(work)
    rest = slice(kb * BLOCK, aug.shape[1])
    aug[here, rest] = dot(work[...], aug[here, rest], precision=EXACT)
    for rb in range(kb + 1, HEAD // BLOCK):
        below = slice(rb * BLOCK, (rb + 1) * BLOCK)
        rest = slice(rb * BLOCK, aug.shape[1])
        aug[below, rest] -= dot(aug[here, below], aug[here, rest], TN, precision=EXACT)


def next_kernel(blocks, aug_in, after, aug_ref, work):
    del after
    aug_ref[...] = aug_in[...]
    for kb in blocks:
        eliminate(aug_ref, kb, work)


def last_kernel(kb, aug_in, after, taper_ref, factor_ref, w_ref, high_ref, low_ref, aug, work, high, low):
    del after
    aug[...] = aug_in[...]
    eliminate(aug, kb, work)
    square = (HEAD, HEAD)
    epochs = aug.shape[1] - HEAD
    factor_ref[...] = jnp.where(iota(square, 0) >= iota(square, 1), aug[:, :HEAD].T, 0.0)
    wt = aug[:, HEAD:]

    def keep(rows, cols, values):
        top = values.astype(BF16)
        high[rows, cols] = top
        low[rows, cols] = (values - top.astype(F32)).astype(BF16)

    keep(slice(None), slice(epochs, None), wt.T)
    for b in range(epochs // BLOCK):
        here = slice(b * BLOCK, (b + 1) * BLOCK)
        shape = (BLOCK, epochs)
        unit = jnp.where(iota(shape, 0) + b * BLOCK == iota(shape, 1), 1.0, 0.0)
        keep(here, slice(0, epochs), unit - dot(wt[:, here], wt, TN, precision=lax.Precision.HIGH))
    count, half = taper_ref.shape[:2]
    for e in range(count):
        reach = min(LANES, epochs - e * half)
        rows = slice(e * half, e * half + reach)
        taper = taper_ref[e, :, :reach]
        got = dot(taper, high[rows, :]) + dot(taper, low[rows, :])
        here = slice(e * half, (e + 1) * half)
        w_ref[here, :] = got[:, epochs:].astype(BF16)
        top = got[:, :epochs].astype(BF16)
        high_ref[here, :] = top
        low_ref[here, :] = (got[:, :epochs] - top.astype(F32)).astype(BF16)


def start_panel(place, chain, taps, own, came, regular, after):
    epochs = own.shape[0] * (LANES // 2)
    half = LANES // 2
    return pl.pallas_call(
        functools.partial(start_kernel, chain),
        out_shape=(
            jax.ShapeDtypeStruct((epochs // LANES, 3 * LANES, 2 * LANES), BF16),
            jax.ShapeDtypeStruct((epochs // half, half, LANES), BF16),
            jax.ShapeDtypeStruct((HEAD, HEAD + epochs), F32),
        ),
        in_specs=[SMEM, SMEM, VMEM, VMEM, VMEM, ANY],
        out_specs=(VMEM,) * 3,
        scratch_shapes=[
            pltpu.VMEM(own.shape, BF16),
            pltpu.VMEM((HEAD, epochs), BF16),
            pltpu.VMEM((BLOCK, BLOCK), F32),
        ],
        compiler_params=LIMIT,
        cost_estimate=FREE,
        name="start_panel",
    )(place, taps, own, came, regular.reshape(1, -1), after)


def next_panel(blocks, aug, after):
    return pl.pallas_call(
        functools.partial(next_kernel, blocks),
        out_shape=jax.ShapeDtypeStruct(aug.shape, F32),
        in_specs=[VMEM, ANY],
        out_specs=VMEM,
        scratch_shapes=[pltpu.VMEM((BLOCK, BLOCK), F32)],
        compiler_params=LIMIT,
        cost_estimate=FREE,
        name="next_panel",
    )(aug, after)


def last_panel(kb, aug, after, taper):
    epochs = aug.shape[1] - HEAD
    return pl.pallas_call(
        functools.partial(last_kernel, kb),
        out_shape=(
            jax.ShapeDtypeStruct((HEAD, HEAD), F32),
            jax.ShapeDtypeStruct((epochs, HEAD), BF16),
            jax.ShapeDtypeStruct((epochs, epochs), BF16),
            jax.ShapeDtypeStruct((epochs, epochs), BF16),
        ),
        in_specs=[VMEM, ANY, VMEM],
        out_specs=(VMEM,) * 4,
        scratch_shapes=[
            pltpu.VMEM(aug.shape, F32),
            pltpu.VMEM((BLOCK, BLOCK), F32),
            pltpu.VMEM((epochs, epochs + HEAD), BF16),
            pltpu.VMEM((epochs, epochs + HEAD), BF16),
        ],
        compiler_params=LIMIT,
        cost_estimate=FREE,
        name="last_panel",
    )(aug, after, taper)


def shards_of(ref, block):
    return [ref.at[n, block] for n in range(ref.shape[0])]


def unpack(place_ref, own, other, blocks):
    width = len(own)
    here = place_ref[PLACE_EP] * width
    there = width - here
    for n in range(width):
        back = place_ref[PLACE_BACK + n]
        blocks[here + back] = own[n][...]
        blocks[there + back] = other[n][...]


def choose(condition, yes, no):
    pl.when(condition)(yes)
    pl.when(jnp.logical_not(condition))(no)


def fixed(array):
    return pl.BlockSpec(
        array.shape, lambda i, place: (0,) * array.ndim, pipeline_mode=pl.Buffered(1)
    )


def project_kernel(
    place_ref, own, own_came, other, other_came, w_ref, high_ref, low_ref, band_ref, right_ref,
    both, blocks, columns, sem,
):
    def bring(sources):
        copies = [
            pltpu.make_async_copy(source, both.at[n], sem.at[n]) for n, source in enumerate(sources)
        ]
        for copy in copies:
            copy.start()
        for copy in copies:
            copy.wait()

    choose(
        place_ref[PLACE_TAKES] != 0,
        lambda: bring((own_came, other_came)),
        lambda: bring((own, other)),
    )

    def store(rows, cols, got):
        columns[rows, cols] = got

    rows = 2 * HALF
    for n in range(right_ref.shape[1] // rows):
        unpack(place_ref, shards_of(both.at[0], n), shards_of(both.at[1], n), blocks)
        filter_rows(lambda e: blocks[e], band_ref, store)
        wanted = columns[...]
        projected = dot(high_ref[...], wanted, NT) + dot(low_ref[...], wanted, NT)
        right_ref[:, n * rows : (n + 1) * rows] = projected.astype(BF16)

    @pl.when(place_ref[PLACE_GROUP] == 0)
    def _():
        right_ref[:, :HEAD] = w_ref[...]


def project(place, own, own_came, other, other_came, w, high, low, band):
    width, count = own.shape[:2]
    epochs = high.shape[0]
    return pl.pallas_call(
        project_kernel,
        out_shape=jax.ShapeDtypeStruct((epochs, count * 2 * HALF), BF16),
        in_specs=[SMEM] + [ANY] * 4 + [VMEM] * 4,
        out_specs=VMEM,
        scratch_shapes=[
            pltpu.VMEM((2,) + own.shape, BF16),
            pltpu.VMEM((2 * width, HALF, LANES), BF16),
            pltpu.VMEM((2 * HALF, epochs), BF16),
            pltpu.SemaphoreType.DMA((2,)),
        ],
        compiler_params=LIMIT,
        cost_estimate=FREE,
        name="project",
    )(place, own, own_came, other, other_came, w, high, low, band)


def tile_kernel(part, parts, place_ref, own_first, own_rest, other_first, other_rest, *refs):
    theirs_ref = refs[0]
    right_ref, factor_ref, reg_ref = refs[:3] if part else refs[1:4]
    out_ref, blocks, lhs = refs[-3:]
    i, steps = pl.program_id(0), pl.num_programs(0)
    rows, cols = out_ref.shape
    half = LANES // 2
    block = lax.rem(place_ref[PLACE_COL] + part, parts) * steps + i
    first_row = (place_ref[PLACE_ROW] * parts * steps + block) * rows
    first_col = place_ref[PLACE_GROUP] * cols

    @pl.when(first_row >= HEAD)
    def _():
        mine = [own_first.at[0], *shards_of(own_rest, 0)]
        others = [other_first.at[0, 0], *shards_of(other_rest, 0)]
        if part == 0:
            choose(
                place_ref[PLACE_OWNS] != 0,
                lambda: unpack(place_ref, mine, shards_of(theirs_ref, 0), blocks),
                lambda: unpack(place_ref, mine, others, blocks),
            )
        else:
            unpack(place_ref, mine, others, blocks)
        for pair in range(lhs.shape[1] // LANES):
            even, odd = blocks[2 * pair], blocks[2 * pair + 1]
            across = slice(pair * LANES, (pair + 1) * LANES)
            lhs[:HALF, across] = jnp.concatenate([even[:, :half], odd[:, :half]], axis=1)
            lhs[HALF:, across] = jnp.concatenate([even[:, half:], odd[:, half:]], axis=1)
        out_ref[...] = dot(lhs[...], right_ref[...])

        @pl.when((first_row >= first_col) & (first_row < first_col + cols))
        def _():
            at = pl.multiple_of(first_row - first_col, rows)
            on_diagonal = iota((rows, rows), 0) == iota((rows, rows), 1)
            out_ref[:, pl.ds(at, rows)] += jnp.where(on_diagonal, reg_ref[...], 0.0)

    @pl.when(first_row < HEAD)
    def _():
        out_ref[...] = jnp.zeros_like(out_ref)

        @pl.when(first_col == 0)
        def _():
            out_ref[:, :HEAD] = factor_ref[...]


def multiply_part(part, parts, place, own, other, theirs, right, factor, regular, out):
    steps = own[0].shape[0]
    rows = 2 * HALF
    epochs, cols = right.shape

    def reg_block(i, place):
        block = lax.rem(place[PLACE_COL] + part, parts) * steps + i
        return 0, place[PLACE_ROW] * parts * steps + block

    def out_block(i, place):
        return lax.rem(place[PLACE_COL] + part, parts) * steps + i, 0

    def shards_spec(array):
        return pl.BlockSpec((array.shape[0], 1, HALF, LANES), lambda i, place: (0, i, 0, 0))

    operands = [*own, *other]
    in_specs = [pl.BlockSpec((1, HALF, LANES), lambda i, place: (i, 0, 0)), shards_spec(own[1])]
    in_specs += [pl.BlockSpec((1, 1, HALF, LANES), lambda i, place: (part, i, 0, 0))]
    in_specs += [shards_spec(other[1])]
    if part == 0:
        operands.append(theirs)
        in_specs.append(shards_spec(theirs))
    operands += [right, factor, regular.reshape(1, -1)]
    in_specs += [fixed(right), fixed(factor), pl.BlockSpec((1, rows), reg_block)]
    if part:
        operands.append(out)
        in_specs.append(ANY)
    return pl.pallas_call(
        functools.partial(tile_kernel, part, parts),
        out_shape=jax.ShapeDtypeStruct((parts * steps * rows, cols), F32),
        grid_spec=pltpu.PrefetchScalarGridSpec(
            num_scalar_prefetch=1,
            grid=(steps,),
            in_specs=in_specs,
            out_specs=pl.BlockSpec((rows, cols), out_block),
            scratch_shapes=[
                pltpu.VMEM((epochs // (LANES // 2), HALF, LANES), BF16),
                pltpu.VMEM((rows, epochs), BF16),
            ],
        ),
        input_output_aliases={len(operands): 0} if part else {},
        compiler_params=MIDDLE,
        cost_estimate=FREE,
        name="multiply_part",
    )(place, *operands)


AXES = ("ep", "row", "col")


def sizes():
    return tuple(lax.axis_size(axis) for axis in AXES)


def flat(ep, row, col):
    _, rows, cols = sizes()
    return (ep * rows + row) * cols + col


def doubling(count, least):
    distances = []
    distance = count // 2
    while distance >= least:
        distances.append(distance)
        distance //= 2
    return distances


def spread_step(block, owner_of, distance):
    eps, rows, cols = sizes()
    route = []
    for e in range(eps):
        for c in range(cols):
            for other in range(0, rows, 2 * distance):
                source = owner_of(e, c) ^ other
                route.append((flat(e, source, c), flat(e, source ^ distance, c)))
    return lax.ppermute(block, AXES, route)


def panel_hops():
    eps, _, cols = sizes()
    across = [(0, d) for d in doubling(cols, 1)]
    return across[:-1] + [(d, 0) for d in doubling(eps, 1)] + across[-1:]


def gather_panel(note):
    eps, rows, cols = sizes()
    row = lax.axis_index("row")
    for distance in doubling(rows, 2):
        came = spread_step(note, lambda e, c: 0, distance)
        note = jnp.where((row & (2 * distance - 1)) == distance, came, note)
    for de, dc in panel_hops():
        route = [
            (flat(e, r, c), flat(e ^ de, r, c ^ dc))
            for e in range(eps)
            for r in range(0, rows, 2)
            for c in range(cols)
        ]
        note = jnp.concatenate([note, lax.ppermute(note, AXES, route)])
    came = lax.ppermute(note, "row", [(r, r + 1) for r in range(0, rows, 2)])
    return note, came


def on_device(design, taps, tap_count, order, regular):
    rows_dev = design.shape[1]
    eps, rows, cols = sizes()
    cols_dev = regular.shape[0] // (eps * cols)
    parts = rows_dev // cols_dev
    row, ep, col = (lax.axis_index(axis) for axis in ("row", "ep", "col"))
    group = lax.axis_index(("ep", "col"))
    everywhere = [(e, r, c) for e in range(eps) for r in range(rows) for c in range(cols)]
    owner = lambda e, c: (e * cols + c) * cols_dev // rows_dev
    inside = lambda r, c: c // parts == (r * parts % cols) // parts
    owns = lambda e, r, c: inside(r, c) & (r * parts // cols == e)
    first_owner = group * cols_dev // rows_dev
    takes = ((row ^ first_owner) & 1) == 1
    home = row * parts // cols == ep
    back = [(col - n) % cols for n in range(cols)]
    place = [row, group, ep, col, takes, owns(ep, row, col), home, *back]
    chain = len(place)
    steps = [(0, 0)]
    for de, dc in panel_hops():
        steps += [(e ^ de, c ^ dc) for e, c in steps]
    place += [(ep ^ de) * cols + (col ^ dc) for de, dc in steps]
    place = jnp.stack([jnp.asarray(p, jnp.int32) for p in place])

    *local, both, note = permute_local(design, order, tap_count, cols_dev)

    def shift(block, n):
        route = [(flat(e, r, (c - n) % cols), flat(e, r, c)) for e, r, c in everywhere]
        return lax.ppermute(block, AXES, route)

    def across(block, wanted):
        route = [(flat(1 - e, r, c), flat(e, r, c)) for e, r, c in everywhere if wanted(e, r, c)]
        return lax.ppermute(block, AXES, route)

    distances = doubling(rows, 1)

    def trade(block):
        route = [
            (flat(e, r, c), flat(e, r ^ distances[0], c)) for e, r, c in everywhere if inside(r, c)
        ]
        return lax.ppermute(block, AXES, route)

    def spread_rest(block):
        for distance in distances[1:-1]:
            got = spread_step(block, owner, distance)
            hit = ((row ^ first_owner) & (2 * distance - 1)) == distance
            block = jnp.where(hit, got, block)
        return block, spread_step(block, owner, distances[-1])

    notes, came = gather_panel(note)
    early = [shift(local[n % parts], n) for n in range(1, cols)]
    swapped = across(both, lambda e, r, c: True)
    band, taper, aug = start_panel(place, chain, taps, notes, came, regular, notes)
    rest, *local, first = assemble(place, early, local, [aug, swapped], True)
    foreign = trade(first)
    others = [across(rest, lambda e, r, c: not owns(e, r, c))]
    mine = [rest]
    order = [(j, n) for j in range(1, parts) for n in range(1, cols)]
    late = [shift(local[(n + j) % parts], n) for j, n in order]
    aug = next_panel(range(1, HEAD // BLOCK - 1), aug, first)
    foreign, others[0], *late[:2] = gate([foreign, others[0], *late[:2]], aug)
    own, sent = sort(place, first, foreign)
    theirs = across(sent, lambda e, r, c: inside(r, c))
    factor, w, high, low = last_panel(HEAD // BLOCK - 1, aug, own, taper)
    theirs, *late[2:] = gate([theirs, *late[2:]], factor)
    own, own_came = spread_rest(own)
    other, other_came = spread_rest(theirs)
    for j in range(1, parts):
        shards = late[(j - 1) * (cols - 1) : j * (cols - 1)]
        (whole,) = assemble(place, shards, [], [factor], False)
        mine.append(whole)
        others.append(across(whole, lambda e, r, c: True))
    right = project(place, own, own_came, other, other_came, w, high, low, band)
    out = None
    for j in range(parts):
        out = multiply_part(
            j, parts, place, (local[j], mine[j]), (swapped, others[j]), theirs, right, factor,
            regular, out,
        )
    return out


def solution(mesh):
    in_specs = (P(("ep", "col"), "row"), P(), P(("ep", "col")), P("row"), P())
    out_specs = P("row", ("ep", "col"))
    return jax.shard_map(
        on_device, mesh=mesh, in_specs=in_specs, out_specs=out_specs, check_vma=False
    )
```

```python
import functools

import jax
import jax.numpy as jnp
from jax import lax
from jax.experimental import pallas as pl
from jax.experimental.pallas import tpu as pltpu
from jax.sharding import PartitionSpec as P

PANEL = 256
SECTIONS = 2
HEAD = PANEL * SECTIONS
PB = 128
LANES = 128
BLOCK = 128
HALF = 256
SUB = 8
NOTE = 16
EXACT = lax.Precision.HIGHEST
F32 = jnp.float32
BF16 = jnp.bfloat16


def iota(shape, axis):
    return lax.broadcasted_iota(jnp.int32, shape, axis)


def dot(left, right, contract=((1,), (0,)), precision=None):
    return lax.dot_general(
        left, right, (contract, ((), ())), preferred_element_type=F32, precision=precision
    )


NT = ((1,), (1,))
TN = ((0,), (0,))
VMEM = pl.BlockSpec(memory_space=pltpu.VMEM)
SMEM = pl.BlockSpec(memory_space=pltpu.SMEM)
ANY = pl.BlockSpec(memory_space=pl.ANY)
FREE = pl.CostEstimate(flops=0, bytes_accessed=0, transcendentals=0)
LIMIT = pltpu.CompilerParams(vmem_limit_bytes=24 << 20)
MIDDLE = pltpu.CompilerParams(vmem_limit_bytes=32 << 20)
WIDE = pltpu.CompilerParams(vmem_limit_bytes=58 << 20)


def permute_kernel(*refs):
    sources, refs = refs[:3], refs[3:]
    *part_refs, both_ref, note_ref = refs[:-4]
    order_ref, counts_ref, design_ref = targets = refs[-4:-1]
    copies = [
        pltpu.make_async_copy(source, target, refs[-1].at[n])
        for n, (source, target) in enumerate(zip(sources, targets))
    ]
    for copy in copies:
        copy.start()
    for copy in copies:
        copy.wait()
    epochs = design_ref.shape[0]
    parts, per_part = len(part_refs), part_refs[0].shape[0]
    lane = iota((PB, PB), 1).astype(F32)
    none = jnp.zeros((epochs, PB), BF16)
    groups = 2 * HALF // PB

    def packed(local, columns, block, part):
        first = block * groups + part
        second = first + HALF // PB
        pick = [jnp.where(local[:, g : g + 1] == lane, 1.0, 0.0) for g in (first, second)]
        pick = jnp.concatenate(pick, axis=1).astype(BF16)
        top = jnp.concatenate([columns(first), none], axis=1)
        low = jnp.concatenate([none, columns(second)], axis=1)
        return dot(pick, jnp.concatenate([top, low], axis=0), NT).astype(BF16)

    def order_of(rows):
        return (order_ref[rows, :] & (PB - 1)).astype(F32).T

    local = order_of(slice(0, per_part * groups))
    for part in range(HALF // PB):
        columns = lambda g: design_ref[:, g * PB : (g + 1) * PB]
        note_ref[0, part * PB : (part + 1) * PB, :] = packed(local, columns, 0, part)
    counts = counts_ref[...].astype(F32)
    counts = jnp.concatenate([counts] * (LANES // epochs), axis=1)
    note_ref[0, HALF:, :] = jnp.broadcast_to(counts, (NOTE, LANES)).astype(BF16)
    for j in range(parts):
        piece = lax.rem(lax.axis_index("col") + j, parts)
        at = pl.multiple_of(piece * per_part * groups, per_part * groups)
        local = order_of(pl.ds(at, per_part * groups))
        columns = lambda g: design_ref[:, pl.ds(pl.multiple_of((at + g) * PB, PB), PB)]
        for block in range(per_part):
            for part in range(HALF // PB):
                rows = slice(part * PB, (part + 1) * PB)
                part_refs[j][block, rows, :] = packed(local, columns, block, part)
        both_ref[j] = part_refs[j][...]


def permute_local(design, order, tap_count, cols_dev):
    epochs, rows = design.shape
    parts, per_part = rows // cols_dev, cols_dev // (2 * HALF)
    piece = jax.ShapeDtypeStruct((per_part, HALF, LANES), BF16)
    both = jax.ShapeDtypeStruct((parts,) + piece.shape, BF16)
    note = jax.ShapeDtypeStruct((1, HALF + NOTE, LANES), BF16)
    return pl.pallas_call(
        permute_kernel,
        out_shape=(piece,) * parts + (both, note),
        in_specs=[ANY] * 3,
        out_specs=(VMEM,) * (parts + 2),
        scratch_shapes=[
            pltpu.VMEM((rows // PB, PB), jnp.int32),
            pltpu.VMEM((1, epochs), jnp.int32),
            pltpu.VMEM((epochs, rows), BF16),
            pltpu.SemaphoreType.DMA((3,)),
        ],
        compiler_params=WIDE,
        name="permute_local",
    )(order.reshape(rows // PB, PB), tap_count.reshape(1, epochs), design)


PLACE_ROW, PLACE_GROUP, PLACE_EP, PLACE_COL, PLACE_TAKES, PLACE_OWNS, PLACE_HOME, PLACE_BACK = range(8)


def assemble_kernel(count, gated, after, whole, place_ref, *refs):
    shards, kept = refs[:count], refs[count : count + gated]
    out_refs, sem = refs[count + gated + after : -1], refs[-1]
    copies = [(shard, out_refs[0].at[n]) for n, shard in enumerate(shards)]
    if whole:
        copies += [(shard, out_refs[-1].at[n]) for n, shard in enumerate([kept[0], *shards])]
    copies = [pltpu.make_async_copy(a, b, sem.at[n]) for n, (a, b) in enumerate(copies)]
    for copy in copies:
        copy.start()
    for copy in copies:
        copy.wait()


def assemble(place, shards, gated, after, whole):
    count = len(shards)
    out_shape = [jax.ShapeDtypeStruct((count,) + shards[0].shape, BF16)]
    out_shape += [jax.ShapeDtypeStruct(g.shape, g.dtype) for g in gated]
    if whole:
        out_shape.append(jax.ShapeDtypeStruct((count + 1,) + shards[0].shape, BF16))
    return pl.pallas_call(
        functools.partial(assemble_kernel, count, len(gated), len(after), whole),
        out_shape=out_shape,
        in_specs=[SMEM] + [ANY] * (count + len(gated) + len(after)),
        out_specs=[ANY] * len(out_shape),
        input_output_aliases={1 + count + n: 1 + n for n in range(len(gated))},
        scratch_shapes=[pltpu.SemaphoreType.DMA((2 * count + 1,))],
        compiler_params=LIMIT,
        cost_estimate=FREE,
        name="assemble",
    )(place, *shards, *gated, *after)


def sort_kernel(place_ref, native_ref, foreign_ref, keep_ref, send_ref, sem):
    def copy(kept, sent):
        copies = [
            pltpu.make_async_copy(kept, keep_ref, sem.at[0]),
            pltpu.make_async_copy(sent, send_ref, sem.at[1]),
        ]
        for c in copies:
            c.start()
        for c in copies:
            c.wait()

    choose(
        place_ref[PLACE_HOME] != 0,
        lambda: copy(native_ref, foreign_ref),
        lambda: copy(foreign_ref, native_ref),
    )


def sort(place, native, foreign):
    shape = jax.ShapeDtypeStruct(native.shape, BF16)
    return pl.pallas_call(
        sort_kernel,
        out_shape=(shape, shape),
        in_specs=[SMEM, ANY, ANY],
        out_specs=(ANY, ANY),
        scratch_shapes=[pltpu.SemaphoreType.DMA((2,))],
        compiler_params=LIMIT,
        cost_estimate=FREE,
        name="sort",
    )(place, native, foreign)


def gate(arrays, after):
    count = len(arrays)
    return pl.pallas_call(
        lambda *refs: None,
        out_shape=tuple(jax.ShapeDtypeStruct(x.shape, x.dtype) for x in arrays),
        in_specs=[ANY] * (count + 1),
        out_specs=(ANY,) * count,
        input_output_aliases={n: n for n in range(count)},
        compiler_params=LIMIT,
        cost_estimate=FREE,
        name="gate",
    )(*arrays, after)


def filter_rows(blocks, band_ref, store):
    for b in range(band_ref.shape[0]):
        first = max(2 * b - 1, 0)
        skip = 0 if b else LANES
        packed = jnp.concatenate([blocks(e) for e in range(first, 2 * b + 2)], axis=1)
        got = dot(packed, band_ref[b, skip:, :]).astype(BF16)
        for half in range(2):
            across = slice(half * LANES, (half + 1) * LANES)
            store(slice(half * HALF, (half + 1) * HALF), slice(b * LANES, (b + 1) * LANES), got[:, across])


def spread(tile, lane):
    return jnp.broadcast_to(tile[:, lane : lane + 1], (SUB, tile.shape[1]))


def row_of(tile, k):
    return jnp.broadcast_to(tile[k : k + 1, :], (SUB, tile.shape[1]))


def factor_block(work):
    groups = BLOCK // SUB
    sub, lane = iota((SUB, BLOCK), 0), iota((SUB, BLOCK), 1)
    tiles = [work[g * SUB : (g + 1) * SUB, :] for g in range(groups)]
    for g in range(groups):
        inside = (lane >= g * SUB) & (lane < (g + 1) * SUB)
        cols = [spread(tiles[g], g * SUB + j) for j in range(SUB)]
        a = {(i, j): row_of(cols[j], i) for j in range(SUB) for i in range(j, SUB)}
        own = jnp.where(inside, jnp.where(lane - g * SUB == sub, 1.0, 0.0), tiles[g])
        u = [row_of(own, k) for k in range(SUB)]
        inv = []
        low = {}
        for k in range(SUB):
            r = lax.rsqrt(a[k, k])
            inv.append(r)
            for i in range(k + 1, SUB):
                low[i, k] = a[i, k] * r
            for j in range(k + 1, SUB):
                for i in range(j, SUB):
                    a[i, j] = a[i, j] - low[i, k] * low[j, k]
            u[k] = u[k] * r
            for j in range(k + 1, SUB):
                u[j] = u[j] - low[j, k] * u[k]
        for t in range(g + 1, groups):
            left = [spread(tiles[t], g * SUB + j) for j in range(SUB)]
            tile = jnp.where(inside, 0.0, tiles[t])
            for k in range(SUB):
                left[k] = left[k] * inv[k]
                for j in range(k + 1, SUB):
                    left[j] = left[j] - low[j, k] * left[k]
                tile = tile - left[k] * u[k]
            tiles[t] = tile
        merged = u[0]
        for k in range(1, SUB):
            merged = jnp.where(sub == k, u[k], merged)
        work[g * SUB : (g + 1) * SUB, :] = jnp.where(lane < (g + 1) * SUB, merged, 0.0)


def start_kernel(
    chain, place_ref, taps_ref, own_ref, came_ref, reg_ref, after, band_ref, taper_ref, aug_ref, notes, a1,
    work,
):
    del after
    epochs = aug_ref.shape[1] - HEAD
    half = LANES // 2

    @pl.when(place_ref[0] % 2 == 0)
    def _():
        for rel in range(own_ref.shape[0]):
            notes[place_ref[chain + rel]] = own_ref[rel]

    @pl.when(place_ref[0] % 2 == 1)
    def _():
        for rel in range(own_ref.shape[0]):
            notes[place_ref[chain + rel]] = came_ref[rel]

    shape = (half, LANES)
    lag = iota(shape, 1) - iota(shape, 0)
    base = jnp.zeros(shape, F32)
    for k in range(taps_ref.shape[0]):
        base = jnp.where(lag == k, taps_ref[k], base)
    lane = iota(shape, 1)
    swapped = jnp.concatenate([base[:, half:], base[:, :half]], axis=1)
    patterns = (jnp.where(lane < half, swapped, 0.0), base, jnp.where(lane >= half, swapped, 0.0))
    row = iota((1, LANES), 1)
    sources = epochs // half
    counts = [notes[e, HALF : HALF + NOTE, :].astype(F32)[:1] for e in range(sources)]
    counts.append(jnp.zeros_like(counts[0]))
    band_ref[...] = jnp.zeros_like(band_ref)
    for e in range(sources):
        limit = jnp.where(row < half, counts[e], counts[e + 1])
        taper_ref[e] = jnp.where(lag.astype(F32) < limit, base, 0.0).astype(BF16)
    for b in range(epochs // LANES):
        limit = jnp.where(row < half, counts[2 * b], counts[2 * b + 1])
        for j, pattern in enumerate(patterns):
            at = (lag + half - half * j).astype(F32)
            kept = jnp.where(at < limit, pattern, 0.0).astype(BF16)
            for h in range(2):
                rows = slice(j * LANES + h * half, j * LANES + (h + 1) * half)
                band_ref[b, rows, h * LANES : (h + 1) * LANES] = kept

    def store(rows, cols, got):
        a1[rows, cols] = got

    filter_rows(lambda e: notes[e, :HALF, :], band_ref, store)
    columns = a1[...]
    square = (HEAD, HEAD)
    on_diagonal = iota(square, 0) == iota(square, 1)
    aug_ref[:, :HEAD] = dot(columns, columns, NT) + jnp.where(on_diagonal, reg_ref[:, :HEAD], 0.0)
    aug_ref[:, HEAD:] = columns.astype(F32)
    eliminate(aug_ref, 0, work)


def eliminate(aug, kb, work):
    here = slice(kb * BLOCK, (kb + 1) * BLOCK)
    work[...] = aug[here, here]
    factor_block(work)
    rest = slice(kb * BLOCK, aug.shape[1])
    aug[here, rest] = dot(work[...], aug[here, rest], precision=EXACT)
    for rb in range(kb + 1, HEAD // BLOCK):
        below = slice(rb * BLOCK, (rb + 1) * BLOCK)
        rest = slice(rb * BLOCK, aug.shape[1])
        aug[below, rest] -= dot(aug[here, below], aug[here, rest], TN, precision=EXACT)


def next_kernel(blocks, aug_in, after, aug_ref, work):
    del after
    aug_ref[...] = aug_in[...]
    for kb in blocks:
        eliminate(aug_ref, kb, work)


def last_kernel(kb, aug_in, after, taper_ref, factor_ref, w_ref, high_ref, low_ref, aug, work, high, low):
    del after
    aug[...] = aug_in[...]
    eliminate(aug, kb, work)
    square = (HEAD, HEAD)
    epochs = aug.shape[1] - HEAD
    factor_ref[...] = jnp.where(iota(square, 0) >= iota(square, 1), aug[:, :HEAD].T, 0.0)
    wt = aug[:, HEAD:]

    def keep(rows, cols, values):
        top = values.astype(BF16)
        high[rows, cols] = top
        low[rows, cols] = (values - top.astype(F32)).astype(BF16)

    keep(slice(None), slice(epochs, None), wt.T)
    for b in range(epochs // BLOCK):
        here = slice(b * BLOCK, (b + 1) * BLOCK)
        shape = (BLOCK, epochs)
        unit = jnp.where(iota(shape, 0) + b * BLOCK == iota(shape, 1), 1.0, 0.0)
        keep(here, slice(0, epochs), unit - dot(wt[:, here], wt, TN, precision=lax.Precision.HIGH))
    count, half = taper_ref.shape[:2]
    for e in range(count):
        reach = min(LANES, epochs - e * half)
        rows = slice(e * half, e * half + reach)
        taper = taper_ref[e, :, :reach]
        got = dot(taper, high[rows, :]) + dot(taper, low[rows, :])
        here = slice(e * half, (e + 1) * half)
        w_ref[here, :] = got[:, epochs:].astype(BF16)
        top = got[:, :epochs].astype(BF16)
        high_ref[here, :] = top
        low_ref[here, :] = (got[:, :epochs] - top.astype(F32)).astype(BF16)


def start_panel(place, chain, taps, own, came, regular, after):
    epochs = own.shape[0] * (LANES // 2)
    half = LANES // 2
    return pl.pallas_call(
        functools.partial(start_kernel, chain),
        out_shape=(
            jax.ShapeDtypeStruct((epochs // LANES, 3 * LANES, 2 * LANES), BF16),
            jax.ShapeDtypeStruct((epochs // half, half, LANES), BF16),
            jax.ShapeDtypeStruct((HEAD, HEAD + epochs), F32),
        ),
        in_specs=[SMEM, SMEM, VMEM, VMEM, VMEM, ANY],
        out_specs=(VMEM,) * 3,
        scratch_shapes=[
            pltpu.VMEM(own.shape, BF16),
            pltpu.VMEM((HEAD, epochs), BF16),
            pltpu.VMEM((BLOCK, BLOCK), F32),
        ],
        compiler_params=LIMIT,
        cost_estimate=FREE,
        name="start_panel",
    )(place, taps, own, came, regular.reshape(1, -1), after)


def next_panel(blocks, aug, after):
    return pl.pallas_call(
        functools.partial(next_kernel, blocks),
        out_shape=jax.ShapeDtypeStruct(aug.shape, F32),
        in_specs=[VMEM, ANY],
        out_specs=VMEM,
        scratch_shapes=[pltpu.VMEM((BLOCK, BLOCK), F32)],
        compiler_params=LIMIT,
        cost_estimate=FREE,
        name="next_panel",
    )(aug, after)


def last_panel(kb, aug, after, taper):
    epochs = aug.shape[1] - HEAD
    return pl.pallas_call(
        functools.partial(last_kernel, kb),
        out_shape=(
            jax.ShapeDtypeStruct((HEAD, HEAD), F32),
            jax.ShapeDtypeStruct((epochs, HEAD), BF16),
            jax.ShapeDtypeStruct((epochs, epochs), BF16),
            jax.ShapeDtypeStruct((epochs, epochs), BF16),
        ),
        in_specs=[VMEM, ANY, VMEM],
        out_specs=(VMEM,) * 4,
        scratch_shapes=[
            pltpu.VMEM(aug.shape, F32),
            pltpu.VMEM((BLOCK, BLOCK), F32),
            pltpu.VMEM((epochs, epochs + HEAD), BF16),
            pltpu.VMEM((epochs, epochs + HEAD), BF16),
        ],
        compiler_params=LIMIT,
        cost_estimate=FREE,
        name="last_panel",
    )(aug, after, taper)


def shards_of(ref, block):
    return [ref.at[n, block] for n in range(ref.shape[0])]


def unpack(place_ref, own, other, blocks):
    width = len(own)
    here = place_ref[PLACE_EP] * width
    there = width - here
    for n in range(width):
        back = place_ref[PLACE_BACK + n]
        blocks[here + back] = own[n][...]
        blocks[there + back] = other[n][...]


def choose(condition, yes, no):
    pl.when(condition)(yes)
    pl.when(jnp.logical_not(condition))(no)


def fixed(array):
    return pl.BlockSpec(
        array.shape, lambda i, place: (0,) * array.ndim, pipeline_mode=pl.Buffered(1)
    )


def project_kernel(
    place_ref, own, own_came, other, other_came, w_ref, high_ref, low_ref, band_ref, right_ref,
    both, blocks, columns, sem,
):
    def bring(sources):
        copies = [
            pltpu.make_async_copy(source, both.at[n], sem.at[n]) for n, source in enumerate(sources)
        ]
        for copy in copies:
            copy.start()
        for copy in copies:
            copy.wait()

    choose(
        place_ref[PLACE_TAKES] != 0,
        lambda: bring((own_came, other_came)),
        lambda: bring((own, other)),
    )

    def store(rows, cols, got):
        columns[rows, cols] = got

    rows = 2 * HALF
    for n in range(right_ref.shape[1] // rows):
        unpack(place_ref, shards_of(both.at[0], n), shards_of(both.at[1], n), blocks)
        filter_rows(lambda e: blocks[e], band_ref, store)
        wanted = columns[...]
        projected = dot(high_ref[...], wanted, NT)
        right_ref[:, n * rows : (n + 1) * rows] = projected.astype(BF16)

    @pl.when(place_ref[PLACE_GROUP] == 0)
    def _():
        right_ref[:, :HEAD] = w_ref[...]


def project(place, own, own_came, other, other_came, w, high, low, band):
    width, count = own.shape[:2]
    epochs = high.shape[0]
    return pl.pallas_call(
        project_kernel,
        out_shape=jax.ShapeDtypeStruct((epochs, count * 2 * HALF), BF16),
        in_specs=[SMEM] + [ANY] * 4 + [VMEM] * 4,
        out_specs=VMEM,
        scratch_shapes=[
            pltpu.VMEM((2,) + own.shape, BF16),
            pltpu.VMEM((2 * width, HALF, LANES), BF16),
            pltpu.VMEM((2 * HALF, epochs), BF16),
            pltpu.SemaphoreType.DMA((2,)),
        ],
        compiler_params=LIMIT,
        cost_estimate=FREE,
        name="project",
    )(place, own, own_came, other, other_came, w, high, low, band)


def tile_kernel(part, parts, place_ref, own_first, own_rest, other_first, other_rest, *refs):
    theirs_ref = refs[0]
    right_ref, factor_ref, reg_ref = refs[:3] if part else refs[1:4]
    out_ref, blocks, lhs = refs[-3:]
    i, steps = pl.program_id(0), pl.num_programs(0)
    rows, cols = out_ref.shape
    half = LANES // 2
    block = lax.rem(place_ref[PLACE_COL] + part, parts) * steps + i
    first_row = (place_ref[PLACE_ROW] * parts * steps + block) * rows
    first_col = place_ref[PLACE_GROUP] * cols

    @pl.when(first_row >= HEAD)
    def _():
        mine = [own_first.at[0], *shards_of(own_rest, 0)]
        others = [other_first.at[0, 0], *shards_of(other_rest, 0)]
        if part == 0:
            choose(
                place_ref[PLACE_OWNS] != 0,
                lambda: unpack(place_ref, mine, shards_of(theirs_ref, 0), blocks),
                lambda: unpack(place_ref, mine, others, blocks),
            )
        else:
            unpack(place_ref, mine, others, blocks)
        for pair in range(lhs.shape[1] // LANES):
            even, odd = blocks[2 * pair], blocks[2 * pair + 1]
            across = slice(pair * LANES, (pair + 1) * LANES)
            lhs[:HALF, across] = jnp.concatenate([even[:, :half], odd[:, :half]], axis=1)
            lhs[HALF:, across] = jnp.concatenate([even[:, half:], odd[:, half:]], axis=1)
        out_ref[...] = dot(lhs[...], right_ref[...])

        @pl.when((first_row >= first_col) & (first_row < first_col + cols))
        def _():
            at = pl.multiple_of(first_row - first_col, rows)
            on_diagonal = iota((rows, rows), 0) == iota((rows, rows), 1)
            out_ref[:, pl.ds(at, rows)] += jnp.where(on_diagonal, reg_ref[...], 0.0)

    @pl.when(first_row < HEAD)
    def _():
        out_ref[...] = jnp.zeros_like(out_ref)

        @pl.when(first_col == 0)
        def _():
            out_ref[:, :HEAD] = factor_ref[...]


def multiply_part(part, parts, place, own, other, theirs, right, factor, regular, out):
    steps = own[0].shape[0]
    rows = 2 * HALF
    epochs, cols = right.shape

    def reg_block(i, place):
        block = lax.rem(place[PLACE_COL] + part, parts) * steps + i
        return 0, place[PLACE_ROW] * parts * steps + block

    def out_block(i, place):
        return lax.rem(place[PLACE_COL] + part, parts) * steps + i, 0

    def shards_spec(array):
        return pl.BlockSpec((array.shape[0], 1, HALF, LANES), lambda i, place: (0, i, 0, 0))

    operands = [*own, *other]
    in_specs = [pl.BlockSpec((1, HALF, LANES), lambda i, place: (i, 0, 0)), shards_spec(own[1])]
    in_specs += [pl.BlockSpec((1, 1, HALF, LANES), lambda i, place: (part, i, 0, 0))]
    in_specs += [shards_spec(other[1])]
    if part == 0:
        operands.append(theirs)
        in_specs.append(shards_spec(theirs))
    operands += [right, factor, regular.reshape(1, -1)]
    in_specs += [fixed(right), fixed(factor), pl.BlockSpec((1, rows), reg_block)]
    if part:
        operands.append(out)
        in_specs.append(ANY)
    return pl.pallas_call(
        functools.partial(tile_kernel, part, parts),
        out_shape=jax.ShapeDtypeStruct((parts * steps * rows, cols), F32),
        grid_spec=pltpu.PrefetchScalarGridSpec(
            num_scalar_prefetch=1,
            grid=(steps,),
            in_specs=in_specs,
            out_specs=pl.BlockSpec((rows, cols), out_block),
            scratch_shapes=[
                pltpu.VMEM((epochs // (LANES // 2), HALF, LANES), BF16),
                pltpu.VMEM((rows, epochs), BF16),
            ],
        ),
        input_output_aliases={len(operands): 0} if part else {},
        compiler_params=MIDDLE,
        cost_estimate=FREE,
        name="multiply_part",
    )(place, *operands)


AXES = ("ep", "row", "col")


def sizes():
    return tuple(lax.axis_size(axis) for axis in AXES)


def flat(ep, row, col):
    _, rows, cols = sizes()
    return (ep * rows + row) * cols + col


def doubling(count, least):
    distances = []
    distance = count // 2
    while distance >= least:
        distances.append(distance)
        distance //= 2
    return distances


def spread_step(block, owner_of, distance):
    eps, rows, cols = sizes()
    route = []
    for e in range(eps):
        for c in range(cols):
            for other in range(0, rows, 2 * distance):
                source = owner_of(e, c) ^ other
                route.append((flat(e, source, c), flat(e, source ^ distance, c)))
    return lax.ppermute(block, AXES, route)


def panel_hops():
    eps, _, cols = sizes()
    across = [(0, d) for d in doubling(cols, 1)]
    return across[:-1] + [(d, 0) for d in doubling(eps, 1)] + across[-1:]


def gather_panel(note):
    eps, rows, cols = sizes()
    row = lax.axis_index("row")
    for distance in doubling(rows, 2):
        came = spread_step(note, lambda e, c: 0, distance)
        note = jnp.where((row & (2 * distance - 1)) == distance, came, note)
    for de, dc in panel_hops():
        route = [
            (flat(e, r, c), flat(e ^ de, r, c ^ dc))
            for e in range(eps)
            for r in range(0, rows, 2)
            for c in range(cols)
        ]
        note = jnp.concatenate([note, lax.ppermute(note, AXES, route)])
    came = lax.ppermute(note, "row", [(r, r + 1) for r in range(0, rows, 2)])
    return note, came


def on_device(design, taps, tap_count, order, regular):
    rows_dev = design.shape[1]
    eps, rows, cols = sizes()
    cols_dev = regular.shape[0] // (eps * cols)
    parts = rows_dev // cols_dev
    row, ep, col = (lax.axis_index(axis) for axis in ("row", "ep", "col"))
    group = lax.axis_index(("ep", "col"))
    everywhere = [(e, r, c) for e in range(eps) for r in range(rows) for c in range(cols)]
    owner = lambda e, c: (e * cols + c) * cols_dev // rows_dev
    inside = lambda r, c: c // parts == (r * parts % cols) // parts
    owns = lambda e, r, c: inside(r, c) & (r * parts // cols == e)
    first_owner = group * cols_dev // rows_dev
    takes = ((row ^ first_owner) & 1) == 1
    home = row * parts // cols == ep
    back = [(col - n) % cols for n in range(cols)]
    place = [row, group, ep, col, takes, owns(ep, row, col), home, *back]
    chain = len(place)
    steps = [(0, 0)]
    for de, dc in panel_hops():
        steps += [(e ^ de, c ^ dc) for e, c in steps]
    place += [(ep ^ de) * cols + (col ^ dc) for de, dc in steps]
    place = jnp.stack([jnp.asarray(p, jnp.int32) for p in place])

    *local, both, note = permute_local(design, order, tap_count, cols_dev)

    def shift(block, n):
        route = [(flat(e, r, (c - n) % cols), flat(e, r, c)) for e, r, c in everywhere]
        return lax.ppermute(block, AXES, route)

    def across(block, wanted):
        route = [(flat(1 - e, r, c), flat(e, r, c)) for e, r, c in everywhere if wanted(e, r, c)]
        return lax.ppermute(block, AXES, route)

    distances = doubling(rows, 1)

    def trade(block):
        route = [
            (flat(e, r, c), flat(e, r ^ distances[0], c)) for e, r, c in everywhere if inside(r, c)
        ]
        return lax.ppermute(block, AXES, route)

    def spread_rest(block):
        for distance in distances[1:-1]:
            got = spread_step(block, owner, distance)
            hit = ((row ^ first_owner) & (2 * distance - 1)) == distance
            block = jnp.where(hit, got, block)
        return block, spread_step(block, owner, distances[-1])

    notes, came = gather_panel(note)
    early = [shift(local[n % parts], n) for n in range(1, cols)]
    swapped = across(both, lambda e, r, c: True)
    band, taper, aug = start_panel(place, chain, taps, notes, came, regular, notes)
    rest, *local, first = assemble(place, early, local, [aug, swapped], True)
    foreign = trade(first)
    others = [across(rest, lambda e, r, c: not owns(e, r, c))]
    mine = [rest]
    order = [(j, n) for j in range(1, parts) for n in range(1, cols)]
    late = [shift(local[(n + j) % parts], n) for j, n in order]
    aug = next_panel(range(1, 2), aug, first)
    foreign, others[0], *late[:2] = gate([foreign, others[0], *late[:2]], aug)
    own, sent = sort(place, first, foreign)
    theirs = across(sent, lambda e, r, c: inside(r, c))
    aug = next_panel(range(2, HEAD // BLOCK - 1), aug, own)
    factor, w, high, low = last_panel(HEAD // BLOCK - 1, aug, own, taper)
    theirs, *late[2:] = gate([theirs, *late[2:]], factor)
    own, own_came = spread_rest(own)
    other, other_came = spread_rest(theirs)
    for j in range(1, parts):
        shards = late[(j - 1) * (cols - 1) : j * (cols - 1)]
        (whole,) = assemble(place, shards, [], [factor], False)
        mine.append(whole)
        others.append(across(whole, lambda e, r, c: True))
    right = project(place, own, own_came, other, other_came, w, high, low, band)
    out = None
    for j in range(parts):
        out = multiply_part(
            j, parts, place, (local[j], mine[j]), (swapped, others[j]), theirs, right, factor,
            regular, out,
        )
    return out


def solution(mesh):
    in_specs = (P(("ep", "col"), "row"), P(), P(("ep", "col")), P("row"), P())
    out_specs = P("row", ("ep", "col"))
    return jax.shard_map(
        on_device, mesh=mesh, in_specs=in_specs, out_specs=out_specs, check_vma=False
    )
```
